128 devices in a mesh: dp: 32 (over z, y, x_hi), tensor: 4 (over x_lo, core).
Axes of the slice: x: 4 (x_hi: 2, x_lo: 2; x = x_hi * 2 + x_lo), y: 4, z: 4, core: 2. Of those that a mesh axis runs over, the one named last changes fastest.
Arguments:
- inputs: bfloat16 [16384, 1024], P(('dp', 'tensor')), may hold values from -6 to 6
- positions: int32 [16384], P('dp'), may hold values from 0 to 1533, as said below
- cotangent: bfloat16 [16384, 1024], P(('dp', 'tensor')), may hold values from -6 to 6
- query_weight: bfloat16 [1024, 2048], P('dp', 'tensor'), may hold values from -0.1875 to 0.1875
- key_matrix: bfloat16 [1024, 1024], P('dp', 'tensor'), may hold values from -0.1875 to 0.1875
- value_matrix: bfloat16 [1024, 1024], P('dp', 'tensor'), may hold values from -0.1875 to 0.1875
- out_weight: bfloat16 [2048, 1024], P('tensor', 'dp'), may hold values from -0.5 to 0.5
- gate_weight: bfloat16 [1024, 3072], P('dp', 'tensor'), may hold values from -0.1875 to 0.1875
- up_weight: bfloat16 [1024, 3072], P('dp', 'tensor'), may hold values from -0.1875 to 0.1875
- down_weight: bfloat16 [3072, 1024], P('tensor', 'dp'), may hold values from -0.21875 to 0.21875
- query_moment: float32 [1024, 2048], P('dp', 'tensor'), may hold values from -224 to 224
- key_momentum: float32 [1024, 1024], P('dp', 'tensor'), may hold values from -448 to 448
- value_momentum: float32 [1024, 1024], P('dp', 'tensor'), may hold values from -640 to 640
- out_moment: float32 [2048, 1024], P('tensor', 'dp'), may hold values from -80 to 80
- gate_moment: float32 [1024, 3072], P('dp', 'tensor'), may hold values from -224 to 224
- up_moment: float32 [1024, 3072], P('dp', 'tensor'), may hold values from -224 to 224
- down_moment: float32 [3072, 1024], P('tensor', 'dp'), may hold values from -224 to 224
- norm_gains: float32 [2304], replicated, may hold values from 0.5 to 1.5
- gain_moment: float32 [2304], replicated, may hold values from -224 to 224
Outputs:
- outputs: float32 [16384, 1024], P(('dp', 'tensor'))
- layer_input_gradient: float32 [16384, 1024], P(('dp', 'tensor'))
- query_moment_new: float32 [1024, 2048], P('dp', 'tensor')
- key_moment_new: float32 [1024, 1024], P('dp', 'tensor')
- value_moment_new: float32 [1024, 1024], P('dp', 'tensor')
- out_moment_new: float32 [2048, 1024], P('tensor', 'dp')
- gate_moment_new: float32 [1024, 3072], P('dp', 'tensor')
- up_moment_new: float32 [1024, 3072], P('dp', 'tensor')
- down_moment_new: float32 [3072, 1024], P('tensor', 'dp')
- query_weight_new: float32 [1024, 2048], P('dp', 'tensor')
- key_weight_new: float32 [1024, 1024], P('dp', 'tensor')
- value_weight_new: float32 [1024, 1024], P('dp', 'tensor')
- out_weight_new: float32 [2048, 1024], P('tensor', 'dp')
- gate_weight_new: float32 [1024, 3072], P('dp', 'tensor')
- up_weight_new: float32 [1024, 3072], P('dp', 'tensor')
- down_weight_new: float32 [3072, 1024], P('tensor', 'dp')
- gain_moment_new: float32 [2304], replicated
- norm_gains_new: float32 [2304], replicated
The draws below stay inside these ranges and needn't reach their ends.
Inputs may be any that keep to these rules, and one draw needn't show every extreme that they name: Within each sequence the positions start at 0 and rise by 1, 2 or 3 from row to row.
All inputs are finite; a program needn't handle non-finite values.
Results may differ from the reference program's by a relative error of at most 0.033.
Values may be sent and summed in bfloat16 or wider, within the bound.
A program may use at most 192 MiB of HBM per device.

```python
import math
import jax
import jax.numpy as jnp
from jax import lax

MODEL_WIDTH = 1024
QUERY_HEADS = 16
KEY_VALUE_HEADS = 8
HEAD_SIZE = 128
FF = 3072
NS_ITERS = 5
SEQUENCE_TOKENS = 512
TOKEN_COUNT = 16384
N_TENSOR = 4


def draw_positions(key, part):
    key = jax.random.fold_in(key, 11)
    sequence_count = TOKEN_COUNT // SEQUENCE_TOKENS
    keys = jax.random.split(key, 2)
    increments = jax.random.randint(keys[0], (sequence_count, SEQUENCE_TOKENS), 1, 4)
    widest_seq = jax.random.randint(keys[1], (), 0, sequence_count)
    seq_ids = jnp.arange(sequence_count, dtype=jnp.int32)[:, None]
    increments = jnp.where(seq_ids == widest_seq, 3, increments)
    increments = increments.at[:, 0].set(0)
    grid = jnp.cumsum(increments, axis=1)
    return grid.reshape(TOKEN_COUNT).astype(jnp.int32)


def block_levels(rng, dims, shards, low, high):
    level, own = 1.0, jax.random.fold_in(rng, 6)
    for dim, parts in shards:
        steps = jnp.exp(jax.random.uniform(jax.random.fold_in(own, dim), (parts,), jnp.float32, low / len(shards), high / len(shards)))
        level = level * jnp.repeat(steps, dims[dim] // parts).reshape([-1 if axis == dim else 1 for axis in range(len(dims))])
    return level


def gaussian(rng, extent, width, most, cuts=(), kind=jnp.bfloat16):
    values = width * jax.random.normal(rng, extent, jnp.float32)
    if cuts:
        values = values * block_levels(rng, extent, cuts, -0.22, 0.18)
    return jnp.clip(values, -most, most).astype(kind)


def setup_inputs(seed: int = 0) -> dict:
    seeds = jax.random.split(jax.random.key(seed), 20)
    inputs = gaussian(seeds[0], (TOKEN_COUNT, MODEL_WIDTH), 1.0, 6.0, ((0, 128),))
    positions = draw_positions(jax.random.fold_in(seeds[19], 71), 0)
    cotangent = gaussian(seeds[2], (TOKEN_COUNT, MODEL_WIDTH), 1.0, 6.0, ((0, 128),))
    query_weight = gaussian(seeds[3], (MODEL_WIDTH, QUERY_HEADS * HEAD_SIZE), MODEL_WIDTH ** -0.5, 0.1875, ((0, 32), (1, 4)))
    key_matrix = gaussian(seeds[4], (MODEL_WIDTH, KEY_VALUE_HEADS * HEAD_SIZE), MODEL_WIDTH ** -0.5, 0.1875, ((0, 32), (1, 4)))
    value_matrix = gaussian(seeds[5], (MODEL_WIDTH, KEY_VALUE_HEADS * HEAD_SIZE), MODEL_WIDTH ** -0.5, 0.1875, ((0, 32), (1, 4)))
    out_weight = gaussian(seeds[6], (QUERY_HEADS * HEAD_SIZE, MODEL_WIDTH), (QUERY_HEADS * HEAD_SIZE // 16) ** -0.5, 0.5, ((0, 4), (1, 32)))
    gate_weight = gaussian(seeds[7], (MODEL_WIDTH, FF), MODEL_WIDTH ** -0.5, 0.1875, ((0, 32), (1, 4)))
    up_weight = gaussian(seeds[8], (MODEL_WIDTH, FF), MODEL_WIDTH ** -0.5, 0.1875, ((0, 32), (1, 4)))
    down_weight = gaussian(seeds[9], (FF, MODEL_WIDTH), (FF // 4) ** -0.5, 0.21875, ((0, 4), (1, 32)))
    query_moment = gaussian(seeds[10], (MODEL_WIDTH, QUERY_HEADS * HEAD_SIZE), (0.3 * TOKEN_COUNT ** 0.5), 224.0, ((0, 32), (1, 4)), jnp.float32)
    key_momentum = gaussian(seeds[11], (MODEL_WIDTH, KEY_VALUE_HEADS * HEAD_SIZE), (0.6 * TOKEN_COUNT ** 0.5), 448.0, ((0, 32), (1, 4)), jnp.float32)
    value_momentum = gaussian(seeds[12], (MODEL_WIDTH, KEY_VALUE_HEADS * HEAD_SIZE), (0.8 * TOKEN_COUNT ** 0.5), 640.0, ((0, 32), (1, 4)), jnp.float32)
    out_moment = gaussian(seeds[13], (QUERY_HEADS * HEAD_SIZE, MODEL_WIDTH), (0.1 * TOKEN_COUNT ** 0.5), 80.0, ((0, 4), (1, 32)), jnp.float32)
    gate_moment = gaussian(seeds[14], (MODEL_WIDTH, FF), (0.3 * TOKEN_COUNT ** 0.5), 224.0, ((0, 32), (1, 4)), jnp.float32)
    up_moment = gaussian(seeds[15], (MODEL_WIDTH, FF), (0.3 * TOKEN_COUNT ** 0.5), 224.0, ((0, 32), (1, 4)), jnp.float32)
    down_moment = gaussian(seeds[16], (FF, MODEL_WIDTH), (0.3 * TOKEN_COUNT ** 0.5), 224.0, ((0, 4), (1, 32)), jnp.float32)
    norm_gains = jnp.clip(1.0 + 0.1 * jax.random.normal(seeds[17], (2 * MODEL_WIDTH + 2 * HEAD_SIZE,), jnp.float32), 0.5, 1.5)
    gain_moment = gaussian(seeds[18], (2 * MODEL_WIDTH + 2 * HEAD_SIZE,), (0.3 * TOKEN_COUNT ** 0.5), 224.0, (), jnp.float32)
    return dict(inputs=inputs, positions=positions, cotangent=cotangent, query_weight=query_weight, key_matrix=key_matrix, value_matrix=value_matrix, out_weight=out_weight, gate_weight=gate_weight, up_weight=up_weight, down_weight=down_weight, query_moment=query_moment, key_momentum=key_momentum, value_momentum=value_momentum, out_moment=out_moment, gate_moment=gate_moment, up_moment=up_moment, down_moment=down_moment, norm_gains=norm_gains, gain_moment=gain_moment)


epsilon = 1e-06
highest_precision = lax.Precision.HIGHEST
moment_decay = 0.95
gain_decay = 0.9
gain_rate = 0.3
rope_base = 1000000.0
newton_one = 3.4445
newton_two = -4.775
newton_three = 2.0315

@jax.custom_vjp
def low(v):
    return lax.optimization_barrier(v.astype(jnp.bfloat16)).astype(jnp.float32)

@jax.custom_vjp
def low_back(v):
    return v

def low_keep(v):
    return (low(v), None)

def low_pass(kept, grad):
    return (grad,)

def back_keep(v):
    return (v, None)

def back_low(kept, grad):
    return (low(grad),)
low.defvjp(low_keep, low_pass)
low_back.defvjp(back_keep, back_low)

def rms_scale(values):
    return lax.rsqrt(lax.optimization_barrier(jnp.mean(values * values, axis=-1, keepdims=True)) + epsilon)

def rotate(values, rope_cos, rope_sin):
    half_width = values.shape[-1] // 2
    turned = jnp.concatenate([-values[..., half_width:], values[..., :half_width]], axis=-1)
    return values * rope_cos + turned * rope_sin

def rope_tables(positions):
    freq_steps = jnp.arange(HEAD_SIZE // 2, dtype=jnp.float32)
    inverse = jnp.exp(freq_steps * (-2.0 * math.log(rope_base) / HEAD_SIZE))
    angles = positions.astype(jnp.float32)[:, None] * inverse[None, :]
    rope_cos = jnp.concatenate([jnp.cos(angles), jnp.cos(angles)], axis=-1)
    rope_sin = jnp.concatenate([jnp.sin(angles), jnp.sin(angles)], axis=-1)
    return (rope_cos, rope_sin)

def attend_heads(operands):
    query_rows, keys_rot, values_low = operands
    group_width = QUERY_HEADS // KEY_VALUE_HEADS
    grouped_heads = query_rows.reshape(SEQUENCE_TOKENS, KEY_VALUE_HEADS, group_width, HEAD_SIZE)
    scores = jnp.einsum('qhgd,khd->hgqk', grouped_heads, keys_rot, precision=highest_precision) * HEAD_SIZE ** (-0.5)
    scores = low_back(scores)
    row_ids = jnp.arange(SEQUENCE_TOKENS)[:, None]
    col_ids = jnp.arange(SEQUENCE_TOKENS)[None, :]
    scores = jnp.where(col_ids <= row_ids, scores, -1e+30)
    shifted = jnp.exp(scores - lax.optimization_barrier(jnp.max(scores, axis=-1, keepdims=True)))
    probs = low(shifted / lax.optimization_barrier(jnp.sum(shifted, axis=-1, keepdims=True)))
    mixed_heads = jnp.einsum('hgqk,khd->qhgd', probs, values_low, precision=highest_precision)
    return mixed_heads.reshape(SEQUENCE_TOKENS, QUERY_HEADS * HEAD_SIZE)

def layer(widened_inputs, query_weight, key_matrix, value_matrix, out_weight, gate_weight, up_weight, down_weight, norm_gains, rope_cos, rope_sin):
    attention_gain = norm_gains[:MODEL_WIDTH]
    feedforward_gain = norm_gains[MODEL_WIDTH:2 * MODEL_WIDTH]
    gain_query = norm_gains[2 * MODEL_WIDTH:2 * MODEL_WIDTH + HEAD_SIZE]
    gain_key = norm_gains[2 * MODEL_WIDTH + HEAD_SIZE:]
    first_normalized = low(widened_inputs * rms_scale(widened_inputs) * attention_gain)
    query_raw = low_back(jnp.dot(first_normalized, query_weight, precision=highest_precision)).reshape(TOKEN_COUNT, QUERY_HEADS, HEAD_SIZE)
    unrotated_key = low_back(jnp.dot(first_normalized, key_matrix, precision=highest_precision)).reshape(TOKEN_COUNT, KEY_VALUE_HEADS, HEAD_SIZE)
    lower_value = low(low_back(jnp.dot(first_normalized, value_matrix, precision=highest_precision))).reshape(TOKEN_COUNT, KEY_VALUE_HEADS, HEAD_SIZE)
    cos_heads = rope_cos[:, None, :]
    sin_heads = rope_sin[:, None, :]
    rotated_query = low(rotate(query_raw * rms_scale(query_raw) * gain_query, cos_heads, sin_heads))
    rotated_key = low(rotate(unrotated_key * rms_scale(unrotated_key) * gain_key, cos_heads, sin_heads))
    sequence_count = TOKEN_COUNT // SEQUENCE_TOKENS
    mixed_heads = lax.map(jax.checkpoint(attend_heads), (rotated_query.reshape(sequence_count, SEQUENCE_TOKENS, QUERY_HEADS, HEAD_SIZE), rotated_key.reshape(sequence_count, SEQUENCE_TOKENS, KEY_VALUE_HEADS, HEAD_SIZE), lower_value.reshape(sequence_count, SEQUENCE_TOKENS, KEY_VALUE_HEADS, HEAD_SIZE)))
    attention = low(low_back(mixed_heads.reshape(TOKEN_COUNT, QUERY_HEADS * HEAD_SIZE)))
    first_hidden = widened_inputs + low_back(jnp.dot(attention, out_weight, precision=highest_precision))
    second_normalized = low(first_hidden * rms_scale(first_hidden) * feedforward_gain)
    gate_val = low_back(jnp.dot(second_normalized, gate_weight, precision=highest_precision))
    up_val = low_back(jnp.dot(second_normalized, up_weight, precision=highest_precision))
    hidden = low(gate_val * jax.nn.sigmoid(gate_val) * up_val)
    return first_hidden + low_back(jnp.dot(hidden, down_weight, precision=highest_precision))

def orthogonal(block):
    matrix = block
    flipped = matrix.shape[0] > matrix.shape[1]
    if flipped:
        matrix = matrix.T
    current = matrix / (jnp.sqrt(jnp.sum(matrix * matrix)) + 1e-07)
    for newton_step in range(NS_ITERS):
        square = jnp.dot(current, current.T, precision=highest_precision)
        mixer = newton_two * square + newton_three * jnp.dot(square, square, precision=highest_precision)
        current = newton_one * current + jnp.dot(mixer, current, precision=highest_precision)
    if flipped:
        current = current.T
    return current

def reference(inputs, positions, cotangent, query_weight, key_matrix, value_matrix, out_weight, gate_weight, up_weight, down_weight, query_moment, key_momentum, value_momentum, out_moment, gate_moment, up_moment, down_moment, norm_gains, gain_moment):
    rope_cos, rope_sin = rope_tables(positions)
    weights = (query_weight, key_matrix, value_matrix, out_weight, gate_weight, up_weight, down_weight)
    wide_weights = tuple((w.astype(jnp.float32) for w in weights))

    def forward(widened_inputs, *params):
        return layer(widened_inputs, *params, rope_cos, rope_sin)
    result, pullback = jax.vjp(forward, inputs.astype(jnp.float32), *wide_weights, norm_gains)
    grads = pullback(cotangent.astype(jnp.float32))
    layer_input_gradient = grads[0]
    weight_grads = grads[1:8]
    gain_grad = grads[8]
    moments = (query_moment, key_momentum, value_momentum, out_moment, gate_moment, up_moment, down_moment)
    split_axes = (1, 1, 1, 0, 1, 1, 0)
    fans = (MODEL_WIDTH, MODEL_WIDTH, MODEL_WIDTH, QUERY_HEADS * HEAD_SIZE // 16, MODEL_WIDTH, MODEL_WIDTH, FF // 4)
    new_moments = []
    new_weights = []
    for slot in range(7):
        moment_new = moment_decay * moments[slot] + weight_grads[slot]
        new_moments.append(moment_new)
        pieces = jnp.split(moment_new, N_TENSOR, axis=split_axes[slot])
        ortho = jnp.concatenate([orthogonal(piece) for piece in pieces], axis=split_axes[slot])
        block_rows, block_cols = pieces[0].shape
        step_rate = math.sqrt(max(block_rows, block_cols) / fans[slot])
        new_weights.append(wide_weights[slot] - step_rate * ortho)
    gain_moment_new = gain_decay * gain_moment + gain_grad
    norm_gains_new = norm_gains - gain_rate / math.sqrt(TOKEN_COUNT) * gain_moment_new
    return (result, layer_input_gradient, new_moments[0], new_moments[1], new_moments[2], new_moments[3], new_moments[4], new_moments[5], new_moments[6], new_weights[0], new_weights[1], new_weights[2], new_weights[3], new_weights[4], new_weights[5], new_weights[6], gain_moment_new, norm_gains_new)
```

```python
import functools
import math

import jax
import jax.numpy as jnp
from jax import lax
from jax.experimental import pallas as pl
from jax.experimental.pallas import tpu as pltpu
from jax.sharding import PartitionSpec as P

MODEL_WIDTH = 1024
QUERY_HEADS = 16
HEAD_SIZE = 128
FF = 3072
NS_ITERS = 5


epsilon = 1e-06
moment_decay = 0.95
gain_decay = 0.9
gain_rate = 0.3
rope_base = 1000000.0
newton_one = 3.4445
newton_two = -4.775
newton_three = 2.0315
contract_rows = (((0,), (0,)), ((), ()))
contract_cols = (((1,), (1,)), ((), ()))


def rms_scale(values):
    return lax.rsqrt(jnp.mean(values * values, axis=-1, keepdims=True) + epsilon)


def norm_backward(gradient_value, normalized_input, scale_value):
    return scale_value * (
        gradient_value
        - normalized_input * jnp.mean(gradient_value * normalized_input, axis=-1, keepdims=True)
    )


def rotate(values, rope_cos, rope_sin):
    half_width = values.shape[-1] // 2
    turned = jnp.concatenate([-values[..., half_width:], values[..., :half_width]], axis=-1)
    return values * rope_cos + turned * rope_sin


def rotate_back(values, rope_cos, rope_sin):
    half_width = values.shape[-1] // 2
    product = values * rope_sin
    return values * rope_cos + jnp.concatenate(
        [product[..., half_width:], -product[..., :half_width]], axis=-1
    )


def rope_tables(positions):
    freq_steps = jnp.arange(HEAD_SIZE // 2, dtype=jnp.float32)
    inverse = jnp.exp(freq_steps * (-2.0 * math.log(rope_base) / HEAD_SIZE))
    angles = positions.astype(jnp.float32)[:, None] * inverse[None, :]
    rope_cos = jnp.concatenate([jnp.cos(angles), jnp.cos(angles)], axis=-1)
    rope_sin = jnp.concatenate([jnp.sin(angles), jnp.sin(angles)], axis=-1)
    return (rope_cos, rope_sin)


def masked_scores(query_block, key_block, block_start, scale_factor):
    scores = (
        jnp.einsum("qhgd,khd->hgqk", query_block, key_block, preferred_element_type=jnp.float32)
        * scale_factor
    )
    row_ids = block_start + jnp.arange(query_block.shape[0])[:, None]
    col_ids = jnp.arange(key_block.shape[0])[None, :]
    return jnp.where(col_ids <= row_ids, scores, -1e30)


COLUMNS = 3840
widths = (512, 256, 256, 512, 768, 768, 768)
starts = (0, 512, 768, 1024, 1536, 2304, 3072)
owners = (0, 4, 9, 13, 18, 22, 27)
rates = (1.0, 1.0, 1.0, math.sqrt(8.0), 1.0, 1.0, math.sqrt(4.0 / 3.0))
column_groups = ((0, 1536), (1536, 2304))
DP = 32
TENSOR = 4
SHARD_ROWS = 32
WIDEST = 768
MESH = pl.DeviceIdType.MESH
ANY = pl.BlockSpec(memory_space=pl.ANY)
VMEM = pl.BlockSpec(memory_space=pltpu.VMEM)


class Place:
    def __init__(self, send_sems, recv_sems):
        self.send_sems, self.recv_sems, self.used = send_sems, recv_sems, 0
        self.dp = lax.axis_index("dp")
        self.tensor = lax.axis_index("tensor")
        self.at = {"z": self.dp // 8, "y": (self.dp // 2) % 4, "x": self.dp % 2}

    def step(self, axis, delta):
        size = 2 if axis == "x" else 4
        return lax.rem(self.at[axis] + size + delta, size)

    def neighbour(self, axis, delta):
        at = dict(self.at)
        at[axis] = self.step(axis, delta)
        return {"dp": at["z"] * 8 + at["y"] * 2 + at["x"]}

    def block(self, axis, delta, other, other_delta):
        first, second = self.step(axis, delta), self.step(other, other_delta)
        return (first, second) if axis == "z" else (second, first)

    def copy(self, source, target, device):
        slot = self.used
        self.used += 1
        return pltpu.make_async_remote_copy(
            src_ref=source,
            dst_ref=target,
            send_sem=self.send_sems.at[slot],
            recv_sem=self.recv_sems.at[slot],
            device_id=device,
            device_id_type=MESH,
        )

    def send(self, source, target, device):
        started = self.copy(source, target, device)
        started.start()
        return started


def greet(devices):
    barrier = pltpu.get_barrier_semaphore()
    for device in devices:
        pl.semaphore_signal(barrier, inc=1, device_id=device, device_id_type=MESH)
    pl.semaphore_wait(barrier, len(devices))


class GatherStream:
    def __init__(self, place, full, first, second, x_at, columns):
        self.place, self.full, self.first, self.second = place, full, first, second
        self.x_at, self.columns = x_at, columns
        self.copies, self.onward, self.along = [], [], {}

    def block(self, first_delta, second_delta, low=0, rows=SHARD_ROWS):
        z_at, y_at = self.place.block(self.first, first_delta, self.second, second_delta)
        return self.full.at[z_at, y_at, self.x_at, pl.ds(low, rows), pl.ds(*self.columns)]

    def send(self, ref, axis, delta):
        started = self.place.send(ref, ref, self.place.neighbour(axis, delta))
        self.copies.append(started)
        return started

    def spread(self, first_delta):
        ref = self.block(first_delta, 0)
        self.along[first_delta] = (self.send(ref, self.second, 1), self.send(ref, self.second, -1))

    def begin(self):
        own = self.block(0, 0)
        self.ahead = self.send(own, self.first, 1)
        self.behind = self.send(own, self.first, -1)
        self.spread(0)

    def forward_first(self):
        half = SHARD_ROWS // 2
        self.ahead.wait_recv()
        self.ahead = self.send(self.block(-1, 0, 0, half), self.first, 1)
        self.spread(-1)
        self.behind.wait_recv()
        self.behind = self.send(self.block(1, 0, half, half), self.first, -1)
        self.spread(1)

    def finish_first(self):
        self.ahead.wait_recv()
        self.behind.wait_recv()
        self.spread(2)

    def forward_second(self):
        half = SHARD_ROWS // 2
        for first_delta in (0, -1, 1, 2):
            ahead, behind = self.along[first_delta]
            ahead.wait_recv()
            self.onward.append(self.send(self.block(first_delta, -1, 0, half), self.second, 1))
            behind.wait_recv()
            self.onward.append(self.send(self.block(first_delta, 1, half, half), self.second, -1))

    def finish_second(self):
        for started in self.onward:
            started.wait_recv()

    def drain(self):
        for started in self.copies:
            started.wait_send()


def both_orders(build, start, width):
    half = width // 2
    return [build("z", "y", (start, half)), build("y", "z", (start + half, half))]


def gather_kernel(shard_ref, out_ref, full, send_sems, recv_sems, local_sem):
    place = Place(send_sems, recv_sems)
    x_at = place.at["x"]
    load = pltpu.make_async_copy(
        shard_ref, full.at[place.at["z"], place.at["y"], x_at], local_sem.at[0]
    )
    load.start()
    greet([place.neighbour(axis, delta) for axis, delta in (("z", 1), ("z", -1), ("y", 1), ("y", -1), ("x", 1))])
    load.wait()
    swaps, own, other = [], [], []
    for start, width in column_groups:
        mine = full.at[place.at["z"], place.at["y"], x_at, :, pl.ds(start, width)]
        swaps.append(place.send(mine, mine, place.neighbour("x", 1)))
        for streams, x_side in ((own, x_at), (other, 1 - x_at)):
            build = lambda first, second, columns, x_side=x_side: GatherStream(
                place, full, first, second, x_side, columns
            )
            streams.append(both_orders(build, start, width))

    def each(streams, name):
        for stream in streams:
            getattr(stream, name)()

    each(own[0], "begin")
    swaps[0].wait_recv()
    each(other[0], "begin")
    each(own[0] + other[0], "forward_first")
    each(own[0], "finish_first")
    swaps[1].wait_recv()
    each(own[1], "begin")
    each(other[0], "finish_first")
    each(other[1], "begin")
    each(own[0] + other[0], "forward_second")
    each(own[1] + other[1], "forward_first")
    each(own[0] + other[0], "finish_second")
    each(own[1] + other[1], "finish_first")
    each(own[1] + other[1], "forward_second")
    each(own[1] + other[1], "finish_second")
    store = pltpu.make_async_copy(full, out_ref, local_sem.at[0])
    store.start()
    for swap in swaps:
        swap.wait_send()
    for streams in own + other:
        each(streams, "drain")
    store.wait()


def gather_weights(shard):
    shape = (4, 4, 2, SHARD_ROWS, COLUMNS)
    return pl.pallas_call(
        gather_kernel,
        out_shape=jax.ShapeDtypeStruct(shape, jnp.bfloat16),
        in_specs=[ANY],
        out_specs=ANY,
        scratch_shapes=[
            pltpu.VMEM(shape, jnp.bfloat16),
            pltpu.SemaphoreType.DMA((162,)),
            pltpu.SemaphoreType.DMA((162,)),
            pltpu.SemaphoreType.DMA((1,)),
        ],
        compiler_params=pltpu.CompilerParams(
            collective_id=0, has_side_effects=True, vmem_limit_bytes=56 << 20
        ),
        name="gather_weights",
    )(shard)


def add_into(target, *terms):
    total = target[...].astype(jnp.float32)
    for term in terms:
        total = total + term[...].astype(jnp.float32)
    target[...] = total.astype(target.dtype)


class ReduceStream:
    def __init__(self, place, sums, far, near, last_far, last_near, first, second, side, columns):
        self.place, self.sums, self.first, self.second = place, sums, first, second
        self.columns = columns
        self.x_at = place.at["x"] if side == 0 else 1 - place.at["x"]
        cut = pl.ds(*columns)
        self.far = lambda second_delta, low: far.at[side, second_delta % 4, pl.ds(low, 16), cut]
        self.near = lambda way, second_delta: near.at[way, side, second_delta % 4, :, cut]
        self.last_far = lambda low: last_far.at[side, pl.ds(low, 16), cut]
        self.last_near = lambda way: last_near.at[way, side, :, cut]
        self.copies = []
        self.far_in, self.near_in = {}, {}

    def block(self, first_delta, second_delta, low=0, rows=SHARD_ROWS):
        z_at, y_at = self.place.block(self.first, first_delta, self.second, second_delta)
        return self.sums.at[z_at, y_at, self.x_at, pl.ds(low, rows), pl.ds(*self.columns)]

    def send(self, source, target, axis, delta):
        started = self.place.send(source, target, self.place.neighbour(axis, delta))
        self.copies.append(started)
        return started

    def begin(self):
        for k in (2, 1, -1, 0):
            self.far_in[k] = (
                self.send(self.block(2, k, 0, 16), self.far(k, 0), self.first, 1),
                self.send(self.block(2, k, 16, 16), self.far(k, 16), self.first, -1),
            )

    def pass_first(self):
        for k in (2, 1, -1, 0):
            ahead, behind = self.far_in[k]
            ahead.wait_recv()
            add_into(self.block(1, k, 0, 16), self.far(k, 0))
            near_ahead = self.send(self.block(1, k), self.near(0, k), self.first, 1)
            behind.wait_recv()
            add_into(self.block(-1, k, 16, 16), self.far(k, 16))
            near_behind = self.send(self.block(-1, k), self.near(1, k), self.first, -1)
            self.near_in[k] = (near_ahead, near_behind)

    def sum_first(self, k):
        for started in self.near_in[k]:
            started.wait_recv()
        add_into(self.block(0, k), self.near(0, k), self.near(1, k))

    def begin_second(self):
        self.sum_first(2)
        self.last_ahead = self.send(self.block(0, 2, 0, 16), self.last_far(0), self.second, 1)
        self.last_behind = self.send(self.block(0, 2, 16, 16), self.last_far(16), self.second, -1)
        for k in (1, -1, 0):
            self.sum_first(k)

    def pass_second(self):
        self.last_ahead.wait_recv()
        add_into(self.block(0, 1, 0, 16), self.last_far(0))
        self.last_ahead = self.send(self.block(0, 1), self.last_near(0), self.second, 1)
        self.last_behind.wait_recv()
        add_into(self.block(0, -1, 16, 16), self.last_far(16))
        self.last_behind = self.send(self.block(0, -1), self.last_near(1), self.second, -1)

    def finish(self):
        self.last_ahead.wait_recv()
        self.last_behind.wait_recv()
        add_into(self.block(0, 0), self.last_near(0), self.last_near(1))

    def drain(self):
        for started in self.copies:
            started.wait_send()


def tail_kernel(
    grads_ref,
    moment_ref,
    shard_ref,
    gain_ref,
    moment_out,
    weight_out,
    gain_out,
    sums,
    far,
    near,
    last_far,
    last_near,
    swapped,
    posted,
    inbox,
    current,
    narrow,
    square,
    low_square,
    mixer,
    outbox,
    settled,
    gain_tensor,
    gain_dp,
    send_sems,
    recv_sems,
    post_send,
    post_recv,
    back_send,
    back_recv,
    gain_send,
    gain_recv,
    local_sem,
):
    place = Place(send_sems, recv_sems)
    dp, tensor = place.dp, place.tensor
    load = pltpu.make_async_copy(grads_ref, sums, local_sem.at[0])
    load.start()

    barrier = pltpu.get_barrier_semaphore()

    def greet_peer(k, carry):
        pl.semaphore_signal(
            barrier, inc=1, device_id={"dp": lax.rem(dp + k, DP)}, device_id_type=MESH
        )
        return carry

    lax.fori_loop(1, DP, greet_peer, 0)
    for k in range(1, TENSOR):
        pl.semaphore_signal(
            barrier, inc=1, device_id={"tensor": lax.rem(tensor + k, TENSOR)}, device_id_type=MESH
        )
    pl.semaphore_wait(barrier, DP - 1 + TENSOR - 1)

    gain_tensor[tensor] = gain_ref[...]
    gain_copies = []
    for k in range(1, TENSOR):
        started = pltpu.make_async_remote_copy(
            src_ref=gain_ref,
            dst_ref=gain_tensor.at[tensor],
            send_sem=gain_send.at[k],
            recv_sem=gain_recv.at[k],
            device_id={"tensor": lax.rem(tensor + k, TENSOR)},
            device_id_type=MESH,
        )
        started.start()
        gain_copies.append(started)
    load.wait()

    own, other = [], []
    for start, width in column_groups:
        for streams, side in ((own, 0), (other, 1)):
            build = lambda first, second, columns, side=side: ReduceStream(
                place, sums, far, near, last_far, last_near, first, second, side, columns
            )
            streams.append(both_orders(build, start, width))

    def each(streams, name):
        for stream in streams:
            getattr(stream, name)()

    order = [other[1], own[1], other[0], own[0]]
    for streams in order:
        each(streams, "begin")

    for started in gain_copies:
        started.wait_recv()
    gain_dp[dp] = gain_tensor[0] + gain_tensor[1] + gain_tensor[2] + gain_tensor[3]

    def gain_copy(k):
        return pltpu.make_async_remote_copy(
            src_ref=gain_dp.at[dp],
            dst_ref=gain_dp.at[dp],
            send_sem=gain_send.at[TENSOR + k],
            recv_sem=gain_recv.at[TENSOR + k],
            device_id={"dp": lax.rem(dp + k, DP)},
            device_id_type=MESH,
        )

    def gain_start(k, carry):
        gain_copy(k).start()
        return carry

    lax.fori_loop(1, DP, gain_start, 0)

    swaps = {}

    def swap(group):
        start, width = column_groups[group]
        partial = sums.at[place.at["z"], place.at["y"], 1 - place.at["x"], :, pl.ds(start, width)]
        swaps[group] = place.send(
            partial, swapped.at[:, pl.ds(start, width)], place.neighbour("x", 1)
        )

    each(order[0], "pass_first")
    each(order[1], "pass_first")
    each(order[0], "begin_second")
    each(order[1], "begin_second")
    each(order[2], "pass_first")
    each(order[0], "pass_second")
    each(order[1], "pass_second")
    each(order[3], "pass_first")
    each(order[0], "finish")
    swap(1)
    each(order[1], "finish")
    each(order[2], "begin_second")
    each(order[3], "begin_second")
    each(order[2], "pass_second")
    each(order[3], "pass_second")
    each(order[2], "finish")
    swap(0)
    each(order[3], "finish")

    def post(slot):
        cut = pl.ds(starts[slot], widths[slot])
        target = inbox.at[dp, :, pl.ds(0, widths[slot])]

        @pl.when(dp != owners[slot])
        def _():
            pltpu.make_async_remote_copy(
                src_ref=posted.at[:, cut],
                dst_ref=target,
                send_sem=post_send.at[slot],
                recv_sem=post_recv.at[dp],
                device_id={"dp": jnp.int32(owners[slot])},
                device_id_type=MESH,
            ).start()

        @pl.when(dp == owners[slot])
        def _():
            target[...] = posted[:, cut]
            if widths[slot] < WIDEST:
                inbox[:, :, widths[slot] :] = jnp.zeros(
                    (DP, SHARD_ROWS, WIDEST - widths[slot]), jnp.bfloat16
                )

    for group, slots in ((1, (4, 5, 6)), (0, (0, 1, 2, 3))):
        start, width = column_groups[group]
        cut = pl.ds(start, width)
        swaps[group].wait_recv()
        total = sums[place.at["z"], place.at["y"], place.at["x"], :, cut].astype(jnp.float32)
        total = total + swapped[:, cut].astype(jnp.float32)
        fresh = moment_decay * moment_ref[:, cut] + total
        moment_out[:, cut] = fresh
        posted[:, cut] = fresh.astype(jnp.bfloat16)
        for slot in slots:
            post(slot)

    for slot in range(7):

        @pl.when(dp == owners[slot])
        def _():
            def arrive(k, carry):
                source = lax.rem(dp + k, DP)
                piece = inbox.at[source, :, pl.ds(0, widths[slot])]
                pltpu.make_async_remote_copy(
                    src_ref=piece,
                    dst_ref=piece,
                    send_sem=post_send.at[slot],
                    recv_sem=post_recv.at[source],
                    device_id={"dp": source},
                    device_id_type=MESH,
                ).wait_recv()
                return carry

            lax.fori_loop(1, DP, arrive, 0)
            orthogonalize(inbox, current, narrow, square, low_square, mixer, outbox)

            cut = pl.ds(starts[slot], widths[slot])

            def back(k):
                target = lax.rem(dp + k, DP)
                return pltpu.make_async_remote_copy(
                    src_ref=outbox.at[target, :, pl.ds(0, widths[slot])],
                    dst_ref=settled.at[:, cut],
                    send_sem=back_send.at[k],
                    recv_sem=back_recv.at[slot],
                    device_id={"dp": target},
                    device_id_type=MESH,
                )

            def back_start(k, carry):
                back(k).start()
                return carry

            lax.fori_loop(1, DP, back_start, 0)
            settled[:, cut] = outbox[dp, :, : widths[slot]]

            def back_wait(k, carry):
                back(k).wait_send()
                return carry

            lax.fori_loop(1, DP, back_wait, 0)

    def gain_arrive(k, carry):
        gain_copy(k).wait_recv()
        return carry

    lax.fori_loop(1, DP, gain_arrive, 0)

    def gain_add(k, carry):
        return carry + gain_dp[k]

    gain_out[...] = lax.fori_loop(1, DP, gain_add, gain_dp[0])

    for slot in range(7):
        cut = pl.ds(starts[slot], widths[slot])

        @pl.when(dp != owners[slot])
        def _():
            pltpu.make_async_remote_copy(
                src_ref=outbox.at[0, :, pl.ds(0, widths[slot])],
                dst_ref=settled.at[:, cut],
                send_sem=post_send.at[slot],
                recv_sem=back_recv.at[slot],
                device_id={"dp": jnp.int32(owners[slot])},
                device_id_type=MESH,
            ).wait_recv()

        weight_out[:, cut] = shard_ref[:, cut].astype(jnp.float32) - rates[slot] * settled[
            :, cut
        ].astype(jnp.float32)

    for started in gain_copies:
        started.wait_send()

    def gain_sent(k, carry):
        gain_copy(k).wait_send()
        return carry

    lax.fori_loop(1, DP, gain_sent, 0)
    for slot in range(7):

        @pl.when(dp != owners[slot])
        def _():
            pltpu.make_async_remote_copy(
                src_ref=posted.at[:, pl.ds(starts[slot], widths[slot])],
                dst_ref=inbox.at[dp, :, pl.ds(0, widths[slot])],
                send_sem=post_send.at[slot],
                recv_sem=post_recv.at[dp],
                device_id={"dp": jnp.int32(owners[slot])},
                device_id_type=MESH,
            ).wait_send()

    for group in (0, 1):
        swaps[group].wait_send()
    for streams in order:
        each(streams, "drain")


TILE = 256


def orthogonalize(inbox, current, narrow, square, low_square, mixer, outbox):
    def turn(k, total):
        piece = inbox[pl.ds(4 * k, 4)].reshape(4 * SHARD_ROWS, WIDEST).astype(jnp.float32)
        current[:, pl.ds(pl.multiple_of(k * 128, 128), 128)] = piece.T
        return total + jnp.sum(piece * piece)

    scale = 1.0 / (jnp.sqrt(lax.fori_loop(0, 8, turn, jnp.float32(0.0))) + 1e-07)

    def rows_of(k):
        return pl.ds(pl.multiple_of(k * TILE, TILE), TILE)

    def normalize(k, total):
        piece = current[rows_of(k), :] * scale
        current[rows_of(k), :] = piece
        narrow[rows_of(k), :] = piece.astype(jnp.bfloat16)
        return total + jnp.sum(piece * piece)

    tiles = WIDEST // TILE
    energy = lax.fori_loop(0, tiles, normalize, jnp.float32(0.0))

    def newton(step, energy):
        shift = energy * (1.0 / WIDEST)

        def make_square(k, carry):
            part = lax.dot_general(
                narrow[rows_of(k), :], narrow[...], contract_cols, preferred_element_type=jnp.float32
            )
            row = lax.broadcasted_iota(jnp.int32, (TILE, WIDEST), 0) + k * TILE
            column = lax.broadcasted_iota(jnp.int32, (TILE, WIDEST), 1)
            part = jnp.where(row == column, part - shift, part)
            square[rows_of(k), :] = part
            low_square[rows_of(k), :] = part.astype(jnp.bfloat16)
            return carry

        lax.fori_loop(0, tiles, make_square, 0)
        linear = newton_two + 2.0 * newton_three * shift
        constant = newton_one + newton_two * shift + newton_three * shift * shift

        def make_mixer(k, carry):
            part = jnp.dot(
                low_square[rows_of(k), :], low_square[...], preferred_element_type=jnp.float32
            )
            mixer[rows_of(k), :] = (linear * square[rows_of(k), :] + newton_three * part).astype(
                jnp.bfloat16
            )
            return carry

        lax.fori_loop(0, tiles, make_mixer, 0)

        def make_next(k, total):
            part = jnp.dot(mixer[rows_of(k), :], narrow[...], preferred_element_type=jnp.float32)
            part = part + constant * current[rows_of(k), :]
            current[rows_of(k), :] = part
            return total + jnp.sum(part * part)

        energy = lax.fori_loop(0, tiles, make_next, jnp.float32(0.0))

        def make_narrow(k, carry):
            narrow[rows_of(k), :] = current[rows_of(k), :].astype(jnp.bfloat16)
            return carry

        lax.fori_loop(0, tiles, make_narrow, 0)
        return energy

    lax.fori_loop(0, NS_ITERS, newton, energy)

    def turn_back(k, carry):
        piece = current[:, pl.ds(pl.multiple_of(k * 128, 128), 128)].T
        outbox[pl.ds(4 * k, 4)] = piece.astype(jnp.bfloat16).reshape(4, SHARD_ROWS, WIDEST)
        return carry

    lax.fori_loop(0, 8, turn_back, 0)


def tail(grads, moments, shard, gain):
    shard_shape = (SHARD_ROWS, COLUMNS)
    bf16, f32 = jnp.bfloat16, jnp.float32
    dma = pltpu.SemaphoreType.DMA
    return pl.pallas_call(
        tail_kernel,
        out_shape=(
            jax.ShapeDtypeStruct(shard_shape, f32),
            jax.ShapeDtypeStruct(shard_shape, f32),
            jax.ShapeDtypeStruct(gain.shape, f32),
        ),
        in_specs=[ANY, VMEM, VMEM, VMEM],
        out_specs=(VMEM, VMEM, VMEM),
        scratch_shapes=[
            pltpu.VMEM((4, 4, 2, SHARD_ROWS, COLUMNS), bf16),
            pltpu.VMEM((2, 4, SHARD_ROWS, COLUMNS), bf16),
            pltpu.VMEM((2, 2, 4, SHARD_ROWS, COLUMNS), bf16),
            pltpu.VMEM((2, SHARD_ROWS, COLUMNS), bf16),
            pltpu.VMEM((2, 2, SHARD_ROWS, COLUMNS), bf16),
            pltpu.VMEM(shard_shape, bf16),
            pltpu.VMEM(shard_shape, bf16),
            pltpu.VMEM((DP, SHARD_ROWS, WIDEST), bf16),
            pltpu.VMEM((WIDEST, MODEL_WIDTH), f32),
            pltpu.VMEM((WIDEST, MODEL_WIDTH), bf16),
            pltpu.VMEM((WIDEST, WIDEST), f32),
            pltpu.VMEM((WIDEST, WIDEST), bf16),
            pltpu.VMEM((WIDEST, WIDEST), bf16),
            pltpu.VMEM((DP, SHARD_ROWS, WIDEST), bf16),
            pltpu.VMEM(shard_shape, bf16),
            pltpu.VMEM((TENSOR,) + gain.shape, f32),
            pltpu.VMEM((DP,) + gain.shape, f32),
            dma((162,)),
            dma((162,)),
            dma((7,)),
            dma((DP,)),
            dma((DP,)),
            dma((7,)),
            dma((TENSOR + DP,)),
            dma((TENSOR + DP,)),
            dma((1,)),
        ],
        compiler_params=pltpu.CompilerParams(
            collective_id=1, has_side_effects=True, vmem_limit_bytes=56 << 20
        ),
        name="reduce_and_update",
    )(grads, moments, shard, gain)


def pack_columns(query, key, value, out, gate, up, down):
    return jnp.concatenate([query, key, value, out.T, gate, up, down.T], axis=1)


def cut_columns(packed):
    return tuple(packed[:, start : start + width] for start, width in zip(starts, widths))


def unpack_columns(packed):
    query, key, value, out, gate, up, down = cut_columns(packed)
    return (query, key, value, out.T, gate, up, down.T)


def body(
    inputs,
    positions,
    cotangent,
    query_weight,
    key_matrix,
    value_matrix,
    out_weight,
    gate_weight,
    up_weight,
    down_weight,
    query_moment,
    key_momentum,
    value_momentum,
    out_moment,
    gate_moment,
    up_moment,
    down_moment,
    norm_gains,
    gain_moment,
):
    local_rows = inputs.shape[0]
    seq_rows = positions.shape[0]
    attention_gain = norm_gains[:MODEL_WIDTH]
    feedforward_gain = norm_gains[MODEL_WIDTH : 2 * MODEL_WIDTH]
    gain_query = norm_gains[2 * MODEL_WIDTH : 2 * MODEL_WIDTH + HEAD_SIZE]
    gain_key = norm_gains[2 * MODEL_WIDTH + HEAD_SIZE :]
    weight_shards = pack_columns(
        query_weight, key_matrix, value_matrix, out_weight, gate_weight, up_weight, down_weight
    )
    weights_full = gather_weights(weight_shards).reshape(MODEL_WIDTH, COLUMNS)
    query_full, key_full, value_full, out_turned, gate_full, up_full, down_turned = cut_columns(
        weights_full
    )
    widened_inputs = inputs.astype(jnp.float32)
    first_scale = rms_scale(widened_inputs)
    first_normalized_input = widened_inputs * first_scale
    first_normalized = (first_normalized_input * attention_gain).astype(jnp.bfloat16)
    normed_all = lax.all_gather(first_normalized, "tensor", axis=0, tiled=True)
    query_heads = query_full.shape[1] // HEAD_SIZE
    value_heads = key_full.shape[1] // HEAD_SIZE
    group_width = query_heads // value_heads
    query_raw = jnp.dot(normed_all, query_full, preferred_element_type=jnp.float32).reshape(
        seq_rows, query_heads, HEAD_SIZE
    )
    unrotated_key = jnp.dot(normed_all, key_full, preferred_element_type=jnp.float32).reshape(
        seq_rows, value_heads, HEAD_SIZE
    )
    lower_value = (
        jnp.dot(normed_all, value_full, preferred_element_type=jnp.float32)
        .astype(jnp.bfloat16)
        .reshape(seq_rows, value_heads, HEAD_SIZE)
    )
    rope_cos, rope_sin = rope_tables(positions)
    cos_heads = rope_cos[:, None, :]
    sin_heads = rope_sin[:, None, :]
    query_scale = rms_scale(query_raw)
    query_hat = query_raw * query_scale
    rotated_query = (
        rotate(query_hat * gain_query, cos_heads, sin_heads)
        .astype(jnp.bfloat16)
        .reshape(seq_rows, value_heads, group_width, HEAD_SIZE)
    )
    key_scale = rms_scale(unrotated_key)
    key_hat = unrotated_key * key_scale
    rotated_key = rotate(key_hat * gain_key, cos_heads, sin_heads).astype(jnp.bfloat16)
    block_rows = min(512, seq_rows)
    scale_factor = HEAD_SIZE ** (-0.5)
    block_index = 0
    block_start = block_index * block_rows
    scores = masked_scores(rotated_query, rotated_key, block_start, scale_factor)
    top_score = jnp.max(scores, axis=-1, keepdims=True)
    shifted = jnp.exp(scores - top_score)
    total = jnp.sum(shifted, axis=-1, keepdims=True)
    probs_low = (shifted / total).astype(jnp.bfloat16)
    mixed_heads = jnp.einsum(
        "hgqk,khd->qhgd", probs_low, lower_value, preferred_element_type=jnp.float32
    )
    mixed_parts = mixed_heads.reshape(block_rows, query_heads * HEAD_SIZE)
    log_totals = [top_score + jnp.log(total)]
    attention = mixed_parts.astype(jnp.bfloat16)
    attn_out = lax.psum_scatter(
        lax.dot_general(
            attention, out_turned, contract_cols, preferred_element_type=jnp.float32
        ).astype(jnp.bfloat16),
        "tensor",
        scatter_dimension=0,
        tiled=True,
    ).astype(jnp.float32)
    first_hidden = widened_inputs + attn_out
    second_scale = rms_scale(first_hidden)
    second_normalized_input = first_hidden * second_scale
    second_normalized = (second_normalized_input * feedforward_gain).astype(jnp.bfloat16)
    normed_two_all = lax.all_gather(second_normalized, "tensor", axis=0, tiled=True)
    gate_val = jnp.dot(normed_two_all, gate_full, preferred_element_type=jnp.float32)
    up_val = jnp.dot(normed_two_all, up_full, preferred_element_type=jnp.float32)
    sigmoid_gate = jax.nn.sigmoid(gate_val)
    activated = gate_val * sigmoid_gate
    hidden = (activated * up_val).astype(jnp.bfloat16)
    ffn_out = lax.psum_scatter(
        lax.dot_general(
            hidden, down_turned, contract_cols, preferred_element_type=jnp.float32
        ).astype(jnp.bfloat16),
        "tensor",
        scatter_dimension=0,
        tiled=True,
    ).astype(jnp.float32)
    outputs = first_hidden + ffn_out
    cotangent_all = lax.all_gather(cotangent, "tensor", axis=0, tiled=True)
    hidden_grad = jnp.dot(cotangent_all, down_turned, preferred_element_type=jnp.float32)
    down_grad = lax.dot_general(
        cotangent_all, hidden, contract_rows, preferred_element_type=jnp.float32
    )
    gate_grad = (
        hidden_grad * up_val * (sigmoid_gate * (1.0 + gate_val * (1.0 - sigmoid_gate)))
    ).astype(jnp.bfloat16)
    up_grad = (hidden_grad * activated).astype(jnp.bfloat16)
    gate_weight_grad = lax.dot_general(
        normed_two_all, gate_grad, contract_rows, preferred_element_type=jnp.float32
    )
    up_weight_grad = lax.dot_general(
        normed_two_all, up_grad, contract_rows, preferred_element_type=jnp.float32
    )
    part_gate = lax.dot_general(
        gate_grad, gate_full, contract_cols, preferred_element_type=jnp.float32
    )
    part_up = lax.dot_general(up_grad, up_full, contract_cols, preferred_element_type=jnp.float32)
    second_normalized_gradient = lax.psum_scatter(
        (part_gate + part_up).astype(jnp.bfloat16), "tensor", scatter_dimension=0, tiled=True
    ).astype(jnp.float32)
    feedforward_gain_gradient = jnp.sum(
        second_normalized_gradient * second_normalized_input, axis=0
    )
    first_hidden_gradient = cotangent.astype(jnp.float32) + norm_backward(
        second_normalized_gradient * feedforward_gain, second_normalized_input, second_scale
    )
    attn_out_grad = first_hidden_gradient.astype(jnp.bfloat16)
    attn_out_all = lax.all_gather(attn_out_grad, "tensor", axis=0, tiled=True)
    attention_grad = jnp.dot(
        attn_out_all, out_turned, preferred_element_type=jnp.float32
    ).astype(jnp.bfloat16)
    out_weight_grad = lax.dot_general(
        attn_out_all, attention, contract_rows, preferred_element_type=jnp.float32
    )
    attention_grad = attention_grad.reshape(seq_rows, value_heads, group_width, HEAD_SIZE)
    key_rot_grad = jnp.zeros((seq_rows, value_heads, HEAD_SIZE), jnp.float32)
    value_sum_grad = jnp.zeros((seq_rows, value_heads, HEAD_SIZE), jnp.float32)
    block_index = 0
    block_start = block_index * block_rows
    block_end = block_start + block_rows
    scores = masked_scores(rotated_query, rotated_key, block_start, scale_factor)
    probs = jnp.exp(scores - log_totals[block_index])
    probs_grad = jnp.einsum(
        "qhgd,khd->hgqk", attention_grad, lower_value, preferred_element_type=jnp.float32
    )
    score_grad = (
        probs * (probs_grad - jnp.sum(probs_grad * probs, axis=-1, keepdims=True))
    ).astype(jnp.bfloat16)
    query_parts = (
        jnp.einsum("hgqk,khd->qhgd", score_grad, rotated_key, preferred_element_type=jnp.float32)
        * scale_factor
    )
    key_rot_grad = key_rot_grad.at[:block_end].add(
        jnp.einsum("hgqk,qhgd->khd", score_grad, rotated_query, preferred_element_type=jnp.float32)
        * scale_factor
    )
    value_sum_grad = value_sum_grad.at[:block_end].add(
        jnp.einsum(
            "hgqk,qhgd->khd",
            probs.astype(jnp.bfloat16),
            attention_grad,
            preferred_element_type=jnp.float32,
        )
    )
    query_rot_grad = query_parts.reshape(seq_rows, query_heads, HEAD_SIZE)
    query_norm_grad = rotate_back(query_rot_grad, cos_heads, sin_heads)
    query_gain_grad = jnp.sum(query_norm_grad * query_hat, axis=(0, 1))
    query_grad = (
        norm_backward(query_norm_grad * gain_query, query_hat, query_scale)
        .astype(jnp.bfloat16)
        .reshape(seq_rows, query_heads * HEAD_SIZE)
    )
    key_norm_grad = rotate_back(key_rot_grad, cos_heads, sin_heads)
    key_gain_grad = jnp.sum(key_norm_grad * key_hat, axis=(0, 1))
    key_grad = (
        norm_backward(key_norm_grad * gain_key, key_hat, key_scale)
        .astype(jnp.bfloat16)
        .reshape(seq_rows, value_heads * HEAD_SIZE)
    )
    value_grad = value_sum_grad.astype(jnp.bfloat16).reshape(seq_rows, value_heads * HEAD_SIZE)
    query_weight_grad = lax.dot_general(
        normed_all, query_grad, contract_rows, preferred_element_type=jnp.float32
    )
    key_weight_grad = lax.dot_general(
        normed_all, key_grad, contract_rows, preferred_element_type=jnp.float32
    )
    value_weight_grad = lax.dot_general(
        normed_all, value_grad, contract_rows, preferred_element_type=jnp.float32
    )
    part_query = lax.dot_general(
        query_grad, query_full, contract_cols, preferred_element_type=jnp.float32
    )
    part_key = lax.dot_general(
        key_grad, key_full, contract_cols, preferred_element_type=jnp.float32
    )
    part_value = lax.dot_general(
        value_grad, value_full, contract_cols, preferred_element_type=jnp.float32
    )
    first_normalized_gradient = lax.psum_scatter(
        (part_query + part_key + part_value).astype(jnp.bfloat16),
        "tensor",
        scatter_dimension=0,
        tiled=True,
    ).astype(jnp.float32)
    attention_gain_gradient = jnp.sum(first_normalized_gradient * first_normalized_input, axis=0)
    layer_input_gradient = first_hidden_gradient + norm_backward(
        first_normalized_gradient * attention_gain, first_normalized_input, first_scale
    )
    grads = jnp.concatenate(
        [
            grad.astype(jnp.bfloat16)
            for grad in (
                query_weight_grad,
                key_weight_grad,
                value_weight_grad,
                out_weight_grad,
                gate_weight_grad,
                up_weight_grad,
                down_grad,
            )
        ],
        axis=1,
    ).reshape(4, 4, 2, SHARD_ROWS, COLUMNS)
    packed_moments = pack_columns(
        query_moment, key_momentum, value_momentum, out_moment, gate_moment, up_moment, down_moment
    )
    gain_parts = jnp.concatenate(
        [attention_gain_gradient, feedforward_gain_gradient, query_gain_grad, key_gain_grad]
    )
    gain_parts = jnp.pad(gain_parts.reshape(18, HEAD_SIZE), ((0, 6), (0, 0)))
    fresh_moments, fresh_weights, gain_total = tail(
        grads, packed_moments, weight_shards, gain_parts
    )
    gain_grad = gain_total[:18].reshape(-1)
    new_moments = unpack_columns(fresh_moments)
    new_weights = unpack_columns(fresh_weights)
    token_total = local_rows * lax.axis_size("dp") * lax.axis_size("tensor")
    gain_moment_new = gain_decay * gain_moment + gain_grad
    norm_gains_new = norm_gains - gain_rate / math.sqrt(token_total) * gain_moment_new
    return (
        outputs,
        layer_input_gradient,
        new_moments[0],
        new_moments[1],
        new_moments[2],
        new_moments[3],
        new_moments[4],
        new_moments[5],
        new_moments[6],
        new_weights[0],
        new_weights[1],
        new_weights[2],
        new_weights[3],
        new_weights[4],
        new_weights[5],
        new_weights[6],
        gain_moment_new,
        norm_gains_new,
    )


def solution(mesh):
    placed = (
        P(("dp", "tensor"), None),
        P("dp"),
        P(("dp", "tensor"), None),
        P("dp", "tensor"),
        P("dp", "tensor"),
        P("dp", "tensor"),
        P("tensor", "dp"),
        P("dp", "tensor"),
        P("dp", "tensor"),
        P("tensor", "dp"),
        P("dp", "tensor"),
        P("dp", "tensor"),
        P("dp", "tensor"),
        P("tensor", "dp"),
        P("dp", "tensor"),
        P("dp", "tensor"),
        P("tensor", "dp"),
        P(),
        P(),
    )
    return jax.shard_map(
        body,
        mesh=mesh,
        in_specs=placed,
        out_specs=(
            P(("dp", "tensor"), None),
            P(("dp", "tensor"), None),
            P("dp", "tensor"),
            P("dp", "tensor"),
            P("dp", "tensor"),
            P("tensor", "dp"),
            P("dp", "tensor"),
            P("dp", "tensor"),
            P("tensor", "dp"),
            P("dp", "tensor"),
            P("dp", "tensor"),
            P("dp", "tensor"),
            P("tensor", "dp"),
            P("dp", "tensor"),
            P("dp", "tensor"),
            P("tensor", "dp"),
            P(),
            P(),
        ),
        check_vma=False,
    )
```

```python
import functools
import math

import jax
import jax.numpy as jnp
from jax import lax
from jax.experimental import pallas as pl
from jax.experimental.pallas import tpu as pltpu
from jax.sharding import PartitionSpec as P

MODEL_WIDTH = 1024
QUERY_HEADS = 16
HEAD_SIZE = 128
FF = 3072
NS_ITERS = 5


epsilon = 1e-06
moment_decay = 0.95
gain_decay = 0.9
gain_rate = 0.3
rope_base = 1000000.0
newton_one = 3.4445
newton_two = -4.775
newton_three = 2.0315
contract_rows = (((0,), (0,)), ((), ()))
contract_cols = (((1,), (1,)), ((), ()))


def rms_scale(values):
    return lax.rsqrt(jnp.mean(values * values, axis=-1, keepdims=True) + epsilon)


def norm_backward(gradient_value, normalized_input, scale_value):
    return scale_value * (
        gradient_value
        - normalized_input * jnp.mean(gradient_value * normalized_input, axis=-1, keepdims=True)
    )


def rope_tables(positions):
    freq_steps = jnp.arange(HEAD_SIZE // 2, dtype=jnp.float32)
    inverse = jnp.exp(freq_steps * (-2.0 * math.log(rope_base) / HEAD_SIZE))
    angles = positions.astype(jnp.float32)[:, None] * inverse[None, :]
    rope_cos = jnp.concatenate([jnp.cos(angles), jnp.cos(angles)], axis=-1)
    rope_sin = jnp.concatenate([-jnp.sin(angles), jnp.sin(angles)], axis=-1)
    return (rope_cos, rope_sin)


COLUMNS = 3840
widths = (512, 256, 256, 512, 768, 768, 768)
starts = (0, 512, 768, 1024, 1536, 2304, 3072)
owners = (0, 4, 9, 13, 18, 22, 27)
rates = (1.0, 1.0, 1.0, math.sqrt(8.0), 1.0, 1.0, math.sqrt(4.0 / 3.0))
column_groups = ((0, 1536), (1536, 2304))
DP = 32
TENSOR = 4
SHARD_ROWS = 32
WIDEST = 768
MESH = pl.DeviceIdType.MESH
ANY = pl.BlockSpec(memory_space=pl.ANY)
VMEM = pl.BlockSpec(memory_space=pltpu.VMEM)


class Place:
    def __init__(self, send_sems, recv_sems):
        self.send_sems, self.recv_sems, self.used = send_sems, recv_sems, 0
        self.dp = lax.axis_index("dp")
        self.tensor = lax.axis_index("tensor")
        self.at = {"z": self.dp // 8, "y": (self.dp // 2) % 4, "x": self.dp % 2}

    def step(self, axis, delta):
        size = 2 if axis == "x" else 4
        return lax.rem(self.at[axis] + size + delta, size)

    def neighbour(self, axis, delta):
        at = dict(self.at)
        at[axis] = self.step(axis, delta)
        return {"dp": at["z"] * 8 + at["y"] * 2 + at["x"]}

    def block(self, axis, delta, other, other_delta):
        first, second = self.step(axis, delta), self.step(other, other_delta)
        return (first, second) if axis == "z" else (second, first)

    def rows(self, z_at, y_at, x_at, low=0, rows=SHARD_ROWS):
        begin = (z_at * 8 + y_at * 2 + x_at) * SHARD_ROWS + low
        return pl.ds(pl.multiple_of(begin, 16), rows)

    def copy(self, source, target, device):
        slot = self.used
        self.used += 1
        return pltpu.make_async_remote_copy(
            src_ref=source,
            dst_ref=target,
            send_sem=self.send_sems.at[slot],
            recv_sem=self.recv_sems.at[slot],
            device_id=device,
            device_id_type=MESH,
        )

    def send(self, source, target, device):
        started = self.copy(source, target, device)
        started.start()
        return started


def greet(devices):
    barrier = pltpu.get_barrier_semaphore()
    for device in devices:
        pl.semaphore_signal(barrier, inc=1, device_id=device, device_id_type=MESH)
    pl.semaphore_wait(barrier, len(devices))


class GatherStream:
    def __init__(self, place, full, first, second, x_at, columns):
        self.place, self.full, self.first, self.second = place, full, first, second
        self.x_at, self.columns = x_at, columns
        self.copies, self.onward, self.along = [], [], {}

    def block(self, first_delta, second_delta, low=0, rows=SHARD_ROWS):
        z_at, y_at = self.place.block(self.first, first_delta, self.second, second_delta)
        return self.full.at[self.place.rows(z_at, y_at, self.x_at, low, rows), pl.ds(*self.columns)]

    def send(self, ref, axis, delta):
        started = self.place.send(ref, ref, self.place.neighbour(axis, delta))
        self.copies.append(started)
        return started

    def spread(self, first_delta):
        ref = self.block(first_delta, 0)
        self.along[first_delta] = (self.send(ref, self.second, 1), self.send(ref, self.second, -1))

    def begin(self):
        own = self.block(0, 0)
        self.ahead = self.send(own, self.first, 1)
        self.behind = self.send(own, self.first, -1)
        self.spread(0)

    def forward_first(self):
        half = SHARD_ROWS // 2
        self.ahead.wait_recv()
        self.ahead = self.send(self.block(-1, 0, 0, half), self.first, 1)
        self.spread(-1)
        self.behind.wait_recv()
        self.behind = self.send(self.block(1, 0, half, half), self.first, -1)
        self.spread(1)

    def finish_first(self):
        self.ahead.wait_recv()
        self.behind.wait_recv()
        self.spread(2)

    def forward_second(self):
        half = SHARD_ROWS // 2
        for first_delta in (0, -1, 1, 2):
            ahead, behind = self.along[first_delta]
            ahead.wait_recv()
            self.onward.append(self.send(self.block(first_delta, -1, 0, half), self.second, 1))
            behind.wait_recv()
            self.onward.append(self.send(self.block(first_delta, 1, half, half), self.second, -1))

    def finish_second(self):
        for started in self.onward:
            started.wait_recv()

    def drain(self):
        for started in self.copies:
            started.wait_send()


def both_orders(build, start, width):
    half = width // 2
    return [build("z", "y", (start, half)), build("y", "z", (start + half, half))]


def add_into(target, *terms):
    total = target[...].astype(jnp.float32)
    for term in terms:
        total = total + term[...].astype(jnp.float32)
    target[...] = total.astype(target.dtype)


class ReduceStream:
    def __init__(self, place, sums, far, near, last_far, last_near, first, second, side, columns):
        self.place, self.sums, self.first, self.second = place, sums, first, second
        self.columns = columns
        self.x_at = place.at["x"] if side == 0 else 1 - place.at["x"]
        cut = pl.ds(*columns)
        self.far = lambda second_delta, low: far.at[side, second_delta % 4, pl.ds(low, 16), cut]
        self.near = lambda way, second_delta: near.at[way, side, second_delta % 4, :, cut]
        self.last_far = lambda low: last_far.at[side, pl.ds(low, 16), cut]
        self.last_near = lambda way: last_near.at[way, side, :, cut]
        self.copies = []
        self.far_in, self.near_in = {}, {}

    def block(self, first_delta, second_delta, low=0, rows=SHARD_ROWS):
        z_at, y_at = self.place.block(self.first, first_delta, self.second, second_delta)
        return self.sums.at[self.place.rows(z_at, y_at, self.x_at, low, rows), pl.ds(*self.columns)]

    def send(self, source, target, axis, delta):
        started = self.place.send(source, target, self.place.neighbour(axis, delta))
        self.copies.append(started)
        return started

    def begin(self):
        for k in (2, 1, -1, 0):
            self.far_in[k] = (
                self.send(self.block(2, k, 0, 16), self.far(k, 0), self.first, 1),
                self.send(self.block(2, k, 16, 16), self.far(k, 16), self.first, -1),
            )

    def pass_first(self):
        for k in (2, 1, -1, 0):
            ahead, behind = self.far_in[k]
            ahead.wait_recv()
            add_into(self.block(1, k, 0, 16), self.far(k, 0))
            near_ahead = self.send(self.block(1, k), self.near(0, k), self.first, 1)
            behind.wait_recv()
            add_into(self.block(-1, k, 16, 16), self.far(k, 16))
            near_behind = self.send(self.block(-1, k), self.near(1, k), self.first, -1)
            self.near_in[k] = (near_ahead, near_behind)

    def sum_first(self, k):
        for started in self.near_in[k]:
            started.wait_recv()
        add_into(self.block(0, k), self.near(0, k), self.near(1, k))

    def begin_second(self):
        self.sum_first(2)
        self.last_ahead = self.send(self.block(0, 2, 0, 16), self.last_far(0), self.second, 1)
        self.last_behind = self.send(self.block(0, 2, 16, 16), self.last_far(16), self.second, -1)
        for k in (1, -1, 0):
            self.sum_first(k)

    def pass_second(self):
        self.last_ahead.wait_recv()
        add_into(self.block(0, 1, 0, 16), self.last_far(0))
        self.last_ahead = self.send(self.block(0, 1), self.last_near(0), self.second, 1)
        self.last_behind.wait_recv()
        add_into(self.block(0, -1, 16, 16), self.last_far(16))
        self.last_behind = self.send(self.block(0, -1), self.last_near(1), self.second, -1)

    def finish(self):
        self.last_ahead.wait_recv()
        self.last_behind.wait_recv()
        add_into(self.block(0, 0), self.last_near(0), self.last_near(1))

    def drain(self):
        for started in self.copies:
            started.wait_send()


SEQ = 512
ROWS = 128
CHIP_ROWS = 256
SCALE = HEAD_SIZE ** (-0.5)


def rows_at(index, size):
    if isinstance(index, int):
        return pl.ds(index * size, size)
    return pl.ds(pl.multiple_of(index * size, size), size)


class Quad:
    def __init__(self, place):
        self.place = place
        self.tensor = place.tensor
        self.core, self.chip = place.tensor % 2, place.tensor // 2
        self.partner = {"tensor": self.chip * 2 + 1 - self.core}
        self.across = {"tensor": (1 - self.chip) * 2 + self.core}
        self.own_rows = rows_at(self.tensor, ROWS)
        self.near_rows = rows_at(self.chip, CHIP_ROWS)
        self.far_rows = rows_at(1 - self.chip, CHIP_ROWS)


class QuadGather:
    def __init__(self, quad, full):
        self.quad, self.full = quad, full

    def start(self):
        quad, place = self.quad, self.quad.place
        own = self.full.at[quad.own_rows]
        self.over = []
        for part in range(2):
            piece = self.full.at[pl.ds(pl.multiple_of(quad.tensor * ROWS + part * 64, 64), 64)]
            self.over.append(place.send(piece, piece, quad.across))
        self.side = place.send(own, own, quad.partner)

    def near(self):
        self.side.wait_recv()

    def forward(self):
        quad, place = self.quad, self.quad.place
        far = (1 - quad.chip) * 2 + quad.core
        self.on = []
        for part in range(2):
            self.over[part].wait_recv()
            piece = self.full.at[pl.ds(pl.multiple_of(far * ROWS + part * 64, 64), 64)]
            self.on.append(place.send(piece, piece, quad.partner))

    def finish(self):
        for started in self.on:
            started.wait_recv()

    def drain(self):
        for started in [self.side] + self.over + self.on:
            started.wait_send()


class QuadReduce:
    def __init__(self, quad, parts, chip_in, link_in):
        self.quad, self.parts, self.chip_in, self.link_in = quad, parts, chip_in, link_in
        far, near = 2 * (1 - quad.chip), 2 * quad.chip
        self.far_own, self.far_other = far + quad.core, far + 1 - quad.core
        self.near_other = near + 1 - quad.core

    def piece(self, block, part):
        return self.parts.at[rows_at(block, ROWS), pl.ds(512 * part, 512)]

    def far_ready(self):
        place, quad = self.quad.place, self.quad
        self.chip_far = [
            place.send(
                self.piece(self.far_other, part),
                self.chip_in.at[0, :, pl.ds(512 * part, 512)],
                quad.partner,
            )
            for part in range(2)
        ]

    def near_ready(self):
        self.chip_near = self.quad.place.send(
            self.parts.at[rows_at(self.near_other, ROWS)], self.chip_in.at[1], self.quad.partner
        )

    def link(self):
        place, quad = self.quad.place, self.quad
        self.over = []
        for part in range(2):
            self.chip_far[part].wait_recv()
            piece = self.piece(self.far_own, part)
            add_into(piece, self.chip_in.at[0, :, pl.ds(512 * part, 512)])
            self.over.append(
                place.send(piece, self.link_in.at[:, pl.ds(512 * part, 512)], quad.across)
            )

    def total(self):
        self.chip_near.wait_recv()
        for started in self.over:
            started.wait_recv()
        total = self.parts[self.quad.own_rows, :].astype(jnp.float32)
        total = total + self.chip_in[1].astype(jnp.float32)
        return total + self.link_in[...].astype(jnp.float32)

    def drain(self):
        for started in self.chip_far + [self.chip_near] + self.over:
            started.wait_send()


def turn_rows(source, target):
    def turn(k, carry):
        cut = rows_at(k, 128)
        target[cut, :] = source[:, cut].T
        return carry

    lax.fori_loop(0, source.shape[1] // 128, turn, 0)


def rope(values, cos, sin):
    return values * cos + pltpu.roll(values, HEAD_SIZE // 2, 1) * sin


def rope_back(values, cos, sin):
    return values * cos + pltpu.roll(values * sin, HEAD_SIZE // 2, 1)


def layer_kernel(
    x_ref,
    cotangent_ref,
    cos_ref,
    sin_ref,
    shard_ref,
    moment_ref,
    gains_ref,
    out_ref,
    grad_ref,
    moment_out,
    posted_out,
    gain_out,
    full,
    sums,
    far,
    near,
    last_far,
    last_near,
    swapped,
    normed,
    normed_two,
    cotangents,
    branch_grads,
    turned,
    query_raw,
    key_raw,
    query_rot,
    key_rot,
    value_low,
    key_turned,
    value_turned,
    probs,
    attention,
    attention_grad,
    hidden,
    ffn_grads,
    head_grads,
    key_sum,
    value_sum,
    hidden_one,
    parts,
    chip_in,
    link_in,
    send_sems,
    recv_sems,
):
    bf16, f32 = jnp.bfloat16, jnp.float32
    place = Place(send_sems, recv_sems)
    quad = Quad(place)
    x_at = place.at["x"]
    gain_attn = gains_ref[:, pl.ds(0, MODEL_WIDTH)]
    gain_ffn = gains_ref[:, pl.ds(MODEL_WIDTH, MODEL_WIDTH)]
    gain_query = gains_ref[:, pl.ds(2 * MODEL_WIDTH, HEAD_SIZE)]
    gain_key = gains_ref[:, pl.ds(2 * MODEL_WIDTH + HEAD_SIZE, HEAD_SIZE)]

    def each(streams, name):
        for stream in streams:
            getattr(stream, name)()

    mine = place.rows(place.at["z"], place.at["y"], x_at)
    full[mine, :] = shard_ref[...]
    greet(
        [
            place.neighbour(axis, delta)
            for axis, delta in (("z", 1), ("z", -1), ("y", 1), ("y", -1), ("x", 1))
        ]
        + [quad.partner, quad.across]
    )

    swaps, own, other = [], [], []
    for start, width in column_groups:
        cut = full.at[mine, pl.ds(start, width)]
        swaps.append(place.send(cut, cut, place.neighbour("x", 1)))
        for streams, x_side in ((own, x_at), (other, 1 - x_at)):
            build = lambda first, second, columns, x_side=x_side: GatherStream(
                place, full, first, second, x_side, columns
            )
            streams.append(both_orders(build, start, width))
    each(own[0], "begin")

    x = x_ref[...].astype(f32)
    first_scale = rms_scale(x)
    normed[quad.own_rows, :] = (x * first_scale * gain_attn).astype(bf16)
    gather_normed = QuadGather(quad, normed)
    gather_normed.start()
    cotangents[quad.own_rows, :] = cotangent_ref[...]
    gather_cotangent = QuadGather(quad, cotangents)
    gather_cotangent.start()

    swaps[0].wait_recv()
    each(other[0], "begin")
    each(own[0] + other[0], "forward_first")
    gather_normed.forward()
    each(own[0], "finish_first")
    swaps[1].wait_recv()
    each(own[1], "begin")
    each(other[0], "finish_first")
    each(other[1], "begin")
    gather_cotangent.forward()
    each(own[0] + other[0], "forward_second")
    gather_normed.near()
    gather_normed.finish()
    each(own[1] + other[1], "forward_first")
    each(own[0] + other[0], "finish_second")

    cos, sin = cos_ref[...], sin_ref[...]

    def project_query(k, carry):
        pair = jnp.dot(
            normed[...], full[:, rows_at(k, 256)], preferred_element_type=f32
        )
        query_raw[:, rows_at(k, 256)] = pair
        for head in range(2):
            raw = pair[:, HEAD_SIZE * head : HEAD_SIZE * (head + 1)]
            rotated = rope(raw * rms_scale(raw) * gain_query, cos, sin)
            query_rot[:, rows_at(2 * k + head, HEAD_SIZE)] = rotated.astype(bf16)
        return carry

    lax.fori_loop(0, 2, project_query, 0)
    pair = jnp.dot(normed[...], full[:, 512:768], preferred_element_type=f32)
    key_raw[...] = pair
    for head in range(2):
        raw = pair[:, HEAD_SIZE * head : HEAD_SIZE * (head + 1)]
        rotated = rope(raw * rms_scale(raw) * gain_key, cos, sin).astype(bf16)
        key_rot[:, HEAD_SIZE * head : HEAD_SIZE * (head + 1)] = rotated
        key_turned[HEAD_SIZE * head : HEAD_SIZE * (head + 1), :] = rotated.T
    pair = jnp.dot(normed[...], full[:, 768:1024], preferred_element_type=f32).astype(bf16)
    value_low[...] = pair
    for head in range(2):
        value_turned[HEAD_SIZE * head : HEAD_SIZE * (head + 1), :] = pair[
            :, HEAD_SIZE * head : HEAD_SIZE * (head + 1)
        ].T

    each(own[1] + other[1], "finish_first")

    def attend(head, carry):
        lanes, shared = rows_at(head, HEAD_SIZE), rows_at(head // 2, HEAD_SIZE)
        for block in range(2):
            keys, begin = 256 * (block + 1), 256 * block
            scores = lax.dot_general(
                key_rot[pl.ds(0, keys), shared],
                query_rot[pl.ds(begin, 256), lanes],
                contract_cols,
                preferred_element_type=f32,
            )
            row = lax.broadcasted_iota(jnp.int32, (keys, 256), 0)
            column = lax.broadcasted_iota(jnp.int32, (keys, 256), 1) + begin
            scores = jnp.where(row <= column, scores * SCALE, -1e30)
            shifted = jnp.exp(scores - jnp.max(scores, axis=0, keepdims=True))
            total = jnp.sum(shifted, axis=0, keepdims=True)
            low = (shifted * (1.0 / total)).astype(bf16)
            probs[head, pl.ds(0, keys), pl.ds(begin, 256)] = low
            mixed = jnp.dot(
                value_turned[shared, pl.ds(0, keys)], low, preferred_element_type=f32
            )
            attention[pl.ds(begin, 256), lanes] = mixed.T.astype(bf16)
        return carry

    lax.fori_loop(0, 4, attend, 0)
    each(own[1] + other[1], "forward_second")

    def project_back(source, start, width, target):
        def run(rows):
            def tile(k, carry):
                part = lax.dot_general(
                    source[rows, :],
                    full[rows_at(k, 256), pl.ds(start, width)],
                    contract_cols,
                    preferred_element_type=f32,
                )
                target[rows, rows_at(k, 256)] = part.astype(bf16)
                return carry

            lax.fori_loop(0, 4, tile, 0)

        return run

    def reducer(k):
        return QuadReduce(quad, parts.at[k], chip_in.at[k], link_in.at[k])

    reduce_attn = reducer(0)
    out_rows = project_back(attention, 1024, 512, parts.at[0])
    out_rows(quad.far_rows)
    reduce_attn.far_ready()
    out_rows(quad.near_rows)
    reduce_attn.near_ready()
    reduce_attn.link()
    each(own[1] + other[1], "finish_second")
    gather_cotangent.near()
    gather_cotangent.finish()
    turn_rows(cotangents, turned.at[0])

    x = x_ref[...].astype(f32)
    first_hidden = x + reduce_attn.total()
    hidden_one[...] = first_hidden
    normed_two[quad.own_rows, :] = (
        first_hidden * rms_scale(first_hidden) * gain_ffn
    ).astype(bf16)
    gather_two = QuadGather(quad, normed_two)
    gather_two.start()

    def feed(rows):
        def tile(k, carry):
            low = normed_two[rows, :]
            gate = jnp.dot(
                low, full[:, pl.ds(pl.multiple_of(1536 + k * 256, 256), 256)],
                preferred_element_type=f32,
            )
            up = jnp.dot(
                low, full[:, pl.ds(pl.multiple_of(2304 + k * 256, 256), 256)],
                preferred_element_type=f32,
            )
            grad = jnp.dot(
                cotangents[rows, :], full[:, pl.ds(pl.multiple_of(3072 + k * 256, 256), 256)],
                preferred_element_type=f32,
            )
            sigmoid = 1.0 / (1.0 + jnp.exp(-gate))
            activated = gate * sigmoid
            hidden[rows, rows_at(k, 256)] = (activated * up).astype(bf16)
            ffn_grads[rows, rows_at(k, 256)] = (
                grad * up * (sigmoid * (1.0 + gate * (1.0 - sigmoid)))
            ).astype(bf16)
            ffn_grads[rows, rows_at(k + 3, 256)] = (grad * activated).astype(bf16)
            return carry

        lax.fori_loop(0, 3, tile, 0)

    reduce_two = reducer(1)
    two_rows = project_back(ffn_grads, 1536, 1536, parts.at[1])
    gather_two.near()
    feed(quad.near_rows)
    gather_two.forward()
    two_rows(quad.near_rows)
    reduce_two.near_ready()
    gather_two.finish()
    feed(quad.far_rows)
    two_rows(quad.far_rows)
    reduce_two.far_ready()

    def weight_grads(left, right, start, tiles):
        def tile(k, carry):
            part = jnp.dot(
                left[...], right[:, rows_at(k, 256)], preferred_element_type=f32
            )
            sums[:, pl.ds(pl.multiple_of(start + k * 256, 256), 256)] = part.astype(bf16)
            return carry

        lax.fori_loop(0, tiles, tile, 0)

    weight_grads(turned.at[0], hidden, 3072, 3)
    reduce_two.link()
    turn_rows(normed_two, turned.at[1])
    weight_grads(turned.at[1], ffn_grads, 1536, 6)

    own_sums, other_sums = [], []
    for start, width in column_groups:
        for streams, side in ((own_sums, 0), (other_sums, 1)):
            build = lambda first, second, columns, side=side: ReduceStream(
                place, sums, far, near, last_far, last_near, first, second, side, columns
            )
            streams.append(both_orders(build, start, width))
    ffn_order = [other_sums[1], own_sums[1]]
    attn_order = [other_sums[0], own_sums[0]]
    for streams in ffn_order:
        each(streams, "begin")

    normed_two_grad = reduce_two.total()
    first_hidden = hidden_one[...]
    second_scale = rms_scale(first_hidden)
    second_hat = first_hidden * second_scale
    gain_out[:, pl.ds(MODEL_WIDTH, MODEL_WIDTH)] = jnp.sum(
        normed_two_grad * second_hat, axis=0, keepdims=True
    )
    hidden_one_grad = cotangent_ref[...].astype(f32) + norm_backward(
        normed_two_grad * gain_ffn, second_hat, second_scale
    )
    grad_ref[...] = hidden_one_grad
    branch_grads[quad.own_rows, :] = hidden_one_grad.astype(bf16)
    gather_branch = QuadGather(quad, branch_grads)
    gather_branch.start()

    reduce_ffn = reducer(2)
    down_rows = project_back(hidden, 3072, 768, parts.at[2])
    down_rows(quad.far_rows)
    gather_branch.forward()
    reduce_ffn.far_ready()
    down_rows(quad.near_rows)
    reduce_ffn.near_ready()
    each(ffn_order[0], "pass_first")

    def attend_grad(rows):
        part = jnp.dot(branch_grads[rows, :], full[:, 1024:1536], preferred_element_type=f32)
        attention_grad[rows, :] = part.astype(bf16)

    gather_branch.near()
    attend_grad(quad.near_rows)
    gather_branch.finish()
    attend_grad(quad.far_rows)
    reduce_ffn.link()
    each(ffn_order[1], "pass_first")

    gain_query_sum = jnp.zeros((1, HEAD_SIZE), f32)
    gain_key_sum = jnp.zeros((1, HEAD_SIZE), f32)

    def head_norm_back(rotated_grad, raw, gain, rows):
        scale = rms_scale(raw)
        hat = raw * scale
        norm_grad = rope_back(rotated_grad, cos_ref[rows, :], sin_ref[rows, :])
        gain_grad = jnp.sum(norm_grad * hat, axis=0, keepdims=True)
        return norm_backward(norm_grad * gain, hat, scale).astype(bf16), gain_grad

    def attend_back(shared_head, gain_sums):
        gain_query_sum, gain_key_sum = gain_sums
        shared = rows_at(shared_head, HEAD_SIZE)
        for inner in range(2):
            head = 2 * shared_head + inner
            lanes = rows_at(head, HEAD_SIZE)
            for block in (1, 0):
                keys, begin = 256 * (block + 1), 256 * block
                key_cut, query_cut = pl.ds(0, keys), pl.ds(begin, 256)
                mixed_grad = attention_grad[query_cut, lanes]
                low = probs[head, key_cut, query_cut]
                wide = low.astype(f32)
                probs_grad = lax.dot_general(
                    value_low[key_cut, shared],
                    mixed_grad,
                    contract_cols,
                    preferred_element_type=f32,
                )
                inner_sum = jnp.sum(wide * probs_grad, axis=0, keepdims=True)
                score_grad = (wide * (probs_grad - inner_sum)).astype(bf16)
                value_part = jnp.dot(low, mixed_grad, preferred_element_type=f32)
                key_part = jnp.dot(
                    score_grad, query_rot[query_cut, lanes], preferred_element_type=f32
                )
                if inner == 0 and block == 1:
                    value_sum[:, shared] = value_part
                    key_sum[:, shared] = key_part
                else:
                    value_sum[key_cut, shared] += value_part
                    key_sum[key_cut, shared] += key_part
                query_part = jnp.dot(
                    key_turned[shared, key_cut], score_grad, preferred_element_type=f32
                )
                grad, gain_part = head_norm_back(
                    query_part.T * SCALE, query_raw[query_cut, lanes], gain_query, query_cut
                )
                head_grads[query_cut, lanes] = grad
                gain_query_sum = gain_query_sum + gain_part
        grad, gain_part = head_norm_back(
            key_sum[:, shared] * SCALE, key_raw[:, shared], gain_key, pl.ds(0, SEQ)
        )
        head_grads[:, rows_at(4 + shared_head, HEAD_SIZE)] = grad
        head_grads[:, rows_at(6 + shared_head, HEAD_SIZE)] = value_sum[:, shared].astype(bf16)
        return gain_query_sum, gain_key_sum + gain_part

    gain_sums = attend_back(0, (gain_query_sum, gain_key_sum))
    for streams in ffn_order:
        each(streams, "begin_second")
    gain_sums = attend_back(1, gain_sums)
    gain_out[:, pl.ds(2 * MODEL_WIDTH, HEAD_SIZE)] = gain_sums[0]
    gain_out[:, pl.ds(2 * MODEL_WIDTH + HEAD_SIZE, HEAD_SIZE)] = gain_sums[1]

    reduce_one = reducer(3)
    one_rows = project_back(head_grads, 0, 1024, parts.at[3])
    one_rows(quad.far_rows)
    reduce_one.far_ready()
    one_rows(quad.near_rows)
    reduce_one.near_ready()
    for streams in ffn_order:
        each(streams, "pass_second")
    reduce_one.link()

    turn_rows(branch_grads, turned.at[0])
    weight_grads(turned.at[0], attention, 1024, 2)
    turn_rows(normed, turned.at[1])
    weight_grads(turned.at[1], head_grads, 0, 4)
    for streams in attn_order:
        each(streams, "begin")

    sum_swaps = {}

    def swap_sums(group):
        start, width = column_groups[group]
        partial = sums.at[
            place.rows(place.at["z"], place.at["y"], 1 - x_at), pl.ds(start, width)
        ]
        sum_swaps[group] = place.send(
            partial, swapped.at[:, pl.ds(start, width)], place.neighbour("x", 1)
        )

    each(ffn_order[0], "finish")
    swap_sums(1)
    each(ffn_order[1], "finish")

    def update(group):
        start, width = column_groups[group]
        cut = pl.ds(start, width)
        sum_swaps[group].wait_recv()
        total = sums[mine, cut].astype(f32) + swapped[:, cut].astype(f32)
        fresh = moment_decay * moment_ref[:, cut] + total
        moment_out[:, cut] = fresh
        posted_out[:, cut] = fresh.astype(bf16)

    out_ref[...] = hidden_one[...] + reduce_ffn.total()
    for streams in attn_order:
        each(streams, "pass_first")
    normed_grad = reduce_one.total()
    x = x_ref[...].astype(f32)
    first_scale = rms_scale(x)
    first_hat = x * first_scale
    gain_out[:, pl.ds(0, MODEL_WIDTH)] = jnp.sum(normed_grad * first_hat, axis=0, keepdims=True)
    grad_ref[...] = grad_ref[...] + norm_backward(normed_grad * gain_attn, first_hat, first_scale)
    for streams in attn_order:
        each(streams, "begin_second")
    update(1)
    for streams in attn_order:
        each(streams, "pass_second")
    each(attn_order[0], "finish")
    swap_sums(0)
    each(attn_order[1], "finish")
    update(0)

    for group in range(2):
        swaps[group].wait_send()
        sum_swaps[group].wait_send()
        for streams in (own, other, own_sums, other_sums):
            each(streams[group], "drain")
    for exchange in (gather_normed, gather_cotangent, gather_two, gather_branch):
        exchange.drain()
    for exchange in (reduce_attn, reduce_two, reduce_ffn, reduce_one):
        exchange.drain()


def run_layer(x, cotangent, cos, sin, shard, moments, gains):
    bf16, f32 = jnp.bfloat16, jnp.float32
    shard_shape = (SHARD_ROWS, COLUMNS)
    copies = 380
    return pl.pallas_call(
        layer_kernel,
        out_shape=(
            jax.ShapeDtypeStruct((ROWS, MODEL_WIDTH), f32),
            jax.ShapeDtypeStruct((ROWS, MODEL_WIDTH), f32),
            jax.ShapeDtypeStruct(shard_shape, f32),
            jax.ShapeDtypeStruct(shard_shape, bf16),
            jax.ShapeDtypeStruct((1, 2 * MODEL_WIDTH + 2 * HEAD_SIZE), f32),
        ),
        in_specs=[VMEM] * 7,
        out_specs=(VMEM,) * 5,
        scratch_shapes=[
            pltpu.VMEM((MODEL_WIDTH, COLUMNS), bf16),
            pltpu.VMEM((MODEL_WIDTH, COLUMNS), bf16),
            pltpu.VMEM((2, 4, SHARD_ROWS, COLUMNS), bf16),
            pltpu.VMEM((2, 2, 4, SHARD_ROWS, COLUMNS), bf16),
            pltpu.VMEM((2, SHARD_ROWS, COLUMNS), bf16),
            pltpu.VMEM((2, 2, SHARD_ROWS, COLUMNS), bf16),
            pltpu.VMEM(shard_shape, bf16),
            pltpu.VMEM((SEQ, MODEL_WIDTH), bf16),
            pltpu.VMEM((SEQ, MODEL_WIDTH), bf16),
            pltpu.VMEM((SEQ, MODEL_WIDTH), bf16),
            pltpu.VMEM((SEQ, MODEL_WIDTH), bf16),
            pltpu.VMEM((2, MODEL_WIDTH, SEQ), bf16),
            pltpu.VMEM((SEQ, 512), f32),
            pltpu.VMEM((SEQ, 256), f32),
            pltpu.VMEM((SEQ, 512), bf16),
            pltpu.VMEM((SEQ, 256), bf16),
            pltpu.VMEM((SEQ, 256), bf16),
            pltpu.VMEM((256, SEQ), bf16),
            pltpu.VMEM((256, SEQ), bf16),
            pltpu.VMEM((4, SEQ, SEQ), bf16),
            pltpu.VMEM((SEQ, 512), bf16),
            pltpu.VMEM((SEQ, 512), bf16),
            pltpu.VMEM((SEQ, 768), bf16),
            pltpu.VMEM((SEQ, 1536), bf16),
            pltpu.VMEM((SEQ, 1024), bf16),
            pltpu.VMEM((SEQ, 256), f32),
            pltpu.VMEM((SEQ, 256), f32),
            pltpu.VMEM((ROWS, MODEL_WIDTH), f32),
            pltpu.VMEM((4, SEQ, MODEL_WIDTH), bf16),
            pltpu.VMEM((4, 2, ROWS, MODEL_WIDTH), bf16),
            pltpu.VMEM((4, ROWS, MODEL_WIDTH), bf16),
            pltpu.SemaphoreType.DMA((copies,)),
            pltpu.SemaphoreType.DMA((copies,)),
        ],
        compiler_params=pltpu.CompilerParams(
            collective_id=0, has_side_effects=True, vmem_limit_bytes=60 << 20
        ),
        name="layer",
    )(x, cotangent, cos, sin, shard, moments, gains)
def update_kernel(
    posted,
    shard_ref,
    gain_ref,
    weight_out,
    gain_out,
    inbox,
    current,
    narrow,
    square,
    low_square,
    mixer,
    outbox,
    settled,
    gain_tensor,
    gain_dp,
    post_send,
    post_recv,
    back_send,
    back_recv,
    gain_send,
    gain_recv,
):
    dp, tensor = lax.axis_index("dp"), lax.axis_index("tensor")

    barrier = pltpu.get_barrier_semaphore()

    def greet_peer(k, carry):
        pl.semaphore_signal(
            barrier, inc=1, device_id={"dp": lax.rem(dp + k, DP)}, device_id_type=MESH
        )
        return carry

    lax.fori_loop(1, DP, greet_peer, 0)
    for k in range(1, TENSOR):
        pl.semaphore_signal(
            barrier, inc=1, device_id={"tensor": lax.rem(tensor + k, TENSOR)}, device_id_type=MESH
        )
    pl.semaphore_wait(barrier, DP - 1 + TENSOR - 1)

    def post(slot):
        cut = pl.ds(starts[slot], widths[slot])
        target = inbox.at[dp, :, pl.ds(0, widths[slot])]

        @pl.when(dp != owners[slot])
        def _():
            pltpu.make_async_remote_copy(
                src_ref=posted.at[:, cut],
                dst_ref=target,
                send_sem=post_send.at[slot],
                recv_sem=post_recv.at[dp],
                device_id={"dp": jnp.int32(owners[slot])},
                device_id_type=MESH,
            ).start()

        @pl.when(dp == owners[slot])
        def _():
            target[...] = posted[:, cut]
            if widths[slot] < WIDEST:
                inbox[:, :, widths[slot] :] = jnp.zeros(
                    (DP, SHARD_ROWS, WIDEST - widths[slot]), jnp.bfloat16
                )

    for slot in range(7):
        post(slot)

    gain_tensor[tensor] = gain_ref[...]
    gain_copies = []
    for k in range(1, TENSOR):
        started = pltpu.make_async_remote_copy(
            src_ref=gain_ref,
            dst_ref=gain_tensor.at[tensor],
            send_sem=gain_send.at[k],
            recv_sem=gain_recv.at[k],
            device_id={"tensor": lax.rem(tensor + k, TENSOR)},
            device_id_type=MESH,
        )
        started.start()
        gain_copies.append(started)

    for started in gain_copies:
        started.wait_recv()
    gain_dp[dp] = gain_tensor[0] + gain_tensor[1] + gain_tensor[2] + gain_tensor[3]

    def gain_copy(k):
        return pltpu.make_async_remote_copy(
            src_ref=gain_dp.at[dp],
            dst_ref=gain_dp.at[dp],
            send_sem=gain_send.at[TENSOR + k],
            recv_sem=gain_recv.at[TENSOR + k],
            device_id={"dp": lax.rem(dp + k, DP)},
            device_id_type=MESH,
        )

    def gain_start(k, carry):
        gain_copy(k).start()
        return carry

    lax.fori_loop(1, DP, gain_start, 0)

    for slot in range(7):

        @pl.when(dp == owners[slot])
        def _():
            def arrive(k, carry):
                source = lax.rem(dp + k, DP)
                piece = inbox.at[source, :, pl.ds(0, widths[slot])]
                pltpu.make_async_remote_copy(
                    src_ref=piece,
                    dst_ref=piece,
                    send_sem=post_send.at[slot],
                    recv_sem=post_recv.at[source],
                    device_id={"dp": source},
                    device_id_type=MESH,
                ).wait_recv()
                return carry

            lax.fori_loop(1, DP, arrive, 0)
            orthogonalize(inbox, current, narrow, square, low_square, mixer, outbox)

            cut = pl.ds(starts[slot], widths[slot])

            def back(k):
                target = lax.rem(dp + k, DP)
                return pltpu.make_async_remote_copy(
                    src_ref=outbox.at[target, :, pl.ds(0, widths[slot])],
                    dst_ref=settled.at[:, cut],
                    send_sem=back_send.at[k],
                    recv_sem=back_recv.at[slot],
                    device_id={"dp": target},
                    device_id_type=MESH,
                )

            def back_start(k, carry):
                back(k).start()
                return carry

            lax.fori_loop(1, DP, back_start, 0)
            settled[:, cut] = outbox[dp, :, : widths[slot]]

            def back_wait(k, carry):
                back(k).wait_send()
                return carry

            lax.fori_loop(1, DP, back_wait, 0)

    def gain_arrive(k, carry):
        gain_copy(k).wait_recv()
        return carry

    lax.fori_loop(1, DP, gain_arrive, 0)

    def gain_add(k, carry):
        return carry + gain_dp[k]

    gain_out[...] = lax.fori_loop(1, DP, gain_add, gain_dp[0])

    for slot in range(7):
        cut = pl.ds(starts[slot], widths[slot])

        @pl.when(dp != owners[slot])
        def _():
            pltpu.make_async_remote_copy(
                src_ref=outbox.at[0, :, pl.ds(0, widths[slot])],
                dst_ref=settled.at[:, cut],
                send_sem=post_send.at[slot],
                recv_sem=back_recv.at[slot],
                device_id={"dp": jnp.int32(owners[slot])},
                device_id_type=MESH,
            ).wait_recv()

        weight_out[:, cut] = shard_ref[:, cut].astype(jnp.float32) - rates[slot] * settled[
            :, cut
        ].astype(jnp.float32)

    for started in gain_copies:
        started.wait_send()

    def gain_sent(k, carry):
        gain_copy(k).wait_send()
        return carry

    lax.fori_loop(1, DP, gain_sent, 0)
    for slot in range(7):

        @pl.when(dp != owners[slot])
        def _():
            pltpu.make_async_remote_copy(
                src_ref=posted.at[:, pl.ds(starts[slot], widths[slot])],
                dst_ref=inbox.at[dp, :, pl.ds(0, widths[slot])],
                send_sem=post_send.at[slot],
                recv_sem=post_recv.at[dp],
                device_id={"dp": jnp.int32(owners[slot])},
                device_id_type=MESH,
            ).wait_send()


def run_update(posted, shard, gain):
    bf16, f32 = jnp.bfloat16, jnp.float32
    dma = pltpu.SemaphoreType.DMA
    shard_shape = (SHARD_ROWS, COLUMNS)
    return pl.pallas_call(
        update_kernel,
        out_shape=(
            jax.ShapeDtypeStruct(shard_shape, f32),
            jax.ShapeDtypeStruct(gain.shape, f32),
        ),
        in_specs=[VMEM] * 3,
        out_specs=(VMEM,) * 2,
        scratch_shapes=[
            pltpu.VMEM((DP, SHARD_ROWS, WIDEST), bf16),
            pltpu.VMEM((WIDEST, MODEL_WIDTH), f32),
            pltpu.VMEM((WIDEST, MODEL_WIDTH), bf16),
            pltpu.VMEM((WIDEST, WIDEST), f32),
            pltpu.VMEM((WIDEST, WIDEST), bf16),
            pltpu.VMEM((WIDEST, WIDEST), bf16),
            pltpu.VMEM((DP, SHARD_ROWS, WIDEST), bf16),
            pltpu.VMEM(shard_shape, bf16),
            pltpu.VMEM((TENSOR,) + gain.shape, f32),
            pltpu.VMEM((DP,) + gain.shape, f32),
            dma((7,)),
            dma((DP,)),
            dma((DP,)),
            dma((7,)),
            dma((TENSOR + DP,)),
            dma((TENSOR + DP,)),
        ],
        compiler_params=pltpu.CompilerParams(
            collective_id=1, has_side_effects=True, vmem_limit_bytes=56 << 20
        ),
        name="update",
    )(posted, shard, gain)


TILE = 256


def orthogonalize(inbox, current, narrow, square, low_square, mixer, outbox):
    def turn(k, total):
        piece = inbox[pl.ds(4 * k, 4)].reshape(4 * SHARD_ROWS, WIDEST).astype(jnp.float32)
        current[:, pl.ds(pl.multiple_of(k * 128, 128), 128)] = piece.T
        return total + jnp.sum(piece * piece)

    scale = 1.0 / (jnp.sqrt(lax.fori_loop(0, 8, turn, jnp.float32(0.0))) + 1e-07)

    def rows_of(k):
        return pl.ds(pl.multiple_of(k * TILE, TILE), TILE)

    def normalize(k, total):
        piece = current[rows_of(k), :] * scale
        current[rows_of(k), :] = piece
        narrow[rows_of(k), :] = piece.astype(jnp.bfloat16)
        return total + jnp.sum(piece * piece)

    tiles = WIDEST // TILE
    energy = lax.fori_loop(0, tiles, normalize, jnp.float32(0.0))

    def newton(step, energy):
        shift = energy * (1.0 / WIDEST)

        def make_square(k, carry):
            part = lax.dot_general(
                narrow[rows_of(k), :], narrow[...], contract_cols, preferred_element_type=jnp.float32
            )
            row = lax.broadcasted_iota(jnp.int32, (TILE, WIDEST), 0) + k * TILE
            column = lax.broadcasted_iota(jnp.int32, (TILE, WIDEST), 1)
            part = jnp.where(row == column, part - shift, part)
            square[rows_of(k), :] = part
            low_square[rows_of(k), :] = part.astype(jnp.bfloat16)
            return carry

        lax.fori_loop(0, tiles, make_square, 0)
        linear = newton_two + 2.0 * newton_three * shift
        constant = newton_one + newton_two * shift + newton_three * shift * shift

        def make_mixer(k, carry):
            part = jnp.dot(
                low_square[rows_of(k), :], low_square[...], preferred_element_type=jnp.float32
            )
            mixer[rows_of(k), :] = (linear * square[rows_of(k), :] + newton_three * part).astype(
                jnp.bfloat16
            )
            return carry

        lax.fori_loop(0, tiles, make_mixer, 0)

        def make_next(k, total):
            part = jnp.dot(mixer[rows_of(k), :], narrow[...], preferred_element_type=jnp.float32)
            part = part + constant * current[rows_of(k), :]
            current[rows_of(k), :] = part
            return total + jnp.sum(part * part)

        energy = lax.fori_loop(0, tiles, make_next, jnp.float32(0.0))

        def make_narrow(k, carry):
            narrow[rows_of(k), :] = current[rows_of(k), :].astype(jnp.bfloat16)
            return carry

        lax.fori_loop(0, tiles, make_narrow, 0)
        return energy

    lax.fori_loop(0, NS_ITERS, newton, energy)

    def turn_back(k, carry):
        piece = current[:, pl.ds(pl.multiple_of(k * 128, 128), 128)].T
        outbox[pl.ds(4 * k, 4)] = piece.astype(jnp.bfloat16).reshape(4, SHARD_ROWS, WIDEST)
        return carry

    lax.fori_loop(0, 8, turn_back, 0)


def pack_columns(query, key, value, out, gate, up, down):
    return jnp.concatenate([query, key, value, out.T, gate, up, down.T], axis=1)


def cut_columns(packed):
    return tuple(packed[:, start : start + width] for start, width in zip(starts, widths))


def unpack_columns(packed):
    query, key, value, out, gate, up, down = cut_columns(packed)
    return (query, key, value, out.T, gate, up, down.T)


def body(
    inputs,
    positions,
    cotangent,
    query_weight,
    key_matrix,
    value_matrix,
    out_weight,
    gate_weight,
    up_weight,
    down_weight,
    query_moment,
    key_momentum,
    value_momentum,
    out_moment,
    gate_moment,
    up_moment,
    down_moment,
    norm_gains,
    gain_moment,
):
    shard = pack_columns(
        query_weight, key_matrix, value_matrix, out_weight, gate_weight, up_weight, down_weight
    )
    moments = pack_columns(
        query_moment, key_momentum, value_momentum, out_moment, gate_moment, up_moment, down_moment
    )
    rope_cos, rope_sin = rope_tables(positions)
    outputs, layer_input_gradient, fresh_moments, posted, gain_parts = run_layer(
        inputs, cotangent, rope_cos, rope_sin, shard, moments, norm_gains.reshape(1, -1)
    )
    fresh_weights, gain_total = run_update(posted, shard, gain_parts)
    gain_moment_new = gain_decay * gain_moment + gain_total.reshape(-1)
    token_total = inputs.shape[0] * lax.axis_size("dp") * lax.axis_size("tensor")
    norm_gains_new = norm_gains - gain_rate / math.sqrt(token_total) * gain_moment_new
    return (
        outputs,
        layer_input_gradient,
        *unpack_columns(fresh_moments),
        *unpack_columns(fresh_weights),
        gain_moment_new,
        norm_gains_new,
    )


def solution(mesh):
    placed = (
        P(("dp", "tensor"), None),
        P("dp"),
        P(("dp", "tensor"), None),
        P("dp", "tensor"),
        P("dp", "tensor"),
        P("dp", "tensor"),
        P("tensor", "dp"),
        P("dp", "tensor"),
        P("dp", "tensor"),
        P("tensor", "dp"),
        P("dp", "tensor"),
        P("dp", "tensor"),
        P("dp", "tensor"),
        P("tensor", "dp"),
        P("dp", "tensor"),
        P("dp", "tensor"),
        P("tensor", "dp"),
        P(),
        P(),
    )
    return jax.shard_map(
        body,
        mesh=mesh,
        in_specs=placed,
        out_specs=(
            P(("dp", "tensor"), None),
            P(("dp", "tensor"), None),
            P("dp", "tensor"),
            P("dp", "tensor"),
            P("dp", "tensor"),
            P("tensor", "dp"),
            P("dp", "tensor"),
            P("dp", "tensor"),
            P("tensor", "dp"),
            P("dp", "tensor"),
            P("dp", "tensor"),
            P("dp", "tensor"),
            P("tensor", "dp"),
            P("dp", "tensor"),
            P("dp", "tensor"),
            P("tensor", "dp"),
            P(),
            P(),
        ),
        check_vma=False,
    )
```

```python
import functools
import math

import jax
import jax.numpy as jnp
from jax import lax
from jax.experimental import pallas as pl
from jax.experimental.pallas import tpu as pltpu
from jax.sharding import PartitionSpec as P

MODEL_WIDTH = 1024
HEAD_SIZE = 128
NS_ITERS = 5


epsilon = 1e-06
moment_decay = 0.95
gain_decay = 0.9
gain_rate = 0.3
rope_base = 1000000.0
newton_one = 3.4445
newton_two = -4.775
newton_three = 2.0315
contract_rows = (((0,), (0,)), ((), ()))
contract_cols = (((1,), (1,)), ((), ()))


def rms_scale(values):
    return lax.rsqrt(jnp.mean(values * values, axis=-1, keepdims=True) + epsilon)


def norm_backward(gradient_value, normalized_input, scale_value):
    return scale_value * (
        gradient_value
        - normalized_input * jnp.mean(gradient_value * normalized_input, axis=-1, keepdims=True)
    )


COLUMNS = 3840
widths = (512, 256, 256, 512, 768, 768, 768)
starts = (0, 512, 768, 1024, 1536, 2304, 3072)
owners = ((8, 26), (6, 17), (28, 3), (25, 14), (0, 31), (13, 5), (18, 23))
rates = (1.0, 1.0, 1.0, math.sqrt(8.0), 1.0, 1.0, math.sqrt(4.0 / 3.0))
gather_groups = ((0, 1024), (1024, 512), (1536, 1536), (3072, 768))
reduce_groups = ((0, 1024), (1024, 512), (1536, 2304))
group_slots = ((0, 1, 2), (3,), (4, 5, 6))
DP = 32
TENSOR = 4
SHARD_ROWS = 32
WIDEST = 768
MESH = pl.DeviceIdType.MESH
ANY = pl.BlockSpec(memory_space=pl.ANY)
VMEM = pl.BlockSpec(memory_space=pltpu.VMEM)


class Place:
    def __init__(self, send_sems, recv_sems):
        self.send_sems, self.recv_sems, self.used = send_sems, recv_sems, 0
        self.dp = lax.axis_index("dp")
        self.tensor = lax.axis_index("tensor")
        self.at = {"z": self.dp // 8, "y": (self.dp // 2) % 4, "x": self.dp % 2}

    def step(self, axis, delta):
        size = 2 if axis == "x" else 4
        return lax.rem(self.at[axis] + size + delta, size)

    def neighbour(self, axis, delta):
        at = dict(self.at)
        at[axis] = self.step(axis, delta)
        return {"dp": at["z"] * 8 + at["y"] * 2 + at["x"]}

    def block(self, axis, delta, other, other_delta):
        first, second = self.step(axis, delta), self.step(other, other_delta)
        return (first, second) if axis == "z" else (second, first)

    def rows(self, z_at, y_at, x_at, low=0, rows=SHARD_ROWS):
        begin = (z_at * 8 + y_at * 2 + x_at) * SHARD_ROWS + low
        return pl.ds(pl.multiple_of(begin, 16), rows)

    def copy(self, source, target, device):
        slot = self.used
        self.used += 1
        return pltpu.make_async_remote_copy(
            src_ref=source,
            dst_ref=target,
            send_sem=self.send_sems.at[slot],
            recv_sem=self.recv_sems.at[slot],
            device_id=device,
            device_id_type=MESH,
        )

    def send(self, source, target, device):
        started = self.copy(source, target, device)
        started.start()
        return started


class GatherStream:
    def __init__(self, place, full, first, second, x_at, columns):
        self.place, self.full, self.first, self.second = place, full, first, second
        self.x_at, self.columns = x_at, columns
        self.copies, self.onward, self.along = [], [], {}

    def block(self, first_delta, second_delta, low=0, rows=SHARD_ROWS):
        z_at, y_at = self.place.block(self.first, first_delta, self.second, second_delta)
        return self.full.at[self.place.rows(z_at, y_at, self.x_at, low, rows), pl.ds(*self.columns)]

    def send(self, ref, axis, delta):
        started = self.place.send(ref, ref, self.place.neighbour(axis, delta))
        self.copies.append(started)
        return started

    def spread(self, first_delta):
        ref = self.block(first_delta, 0)
        self.along[first_delta] = (self.send(ref, self.second, 1), self.send(ref, self.second, -1))

    def begin(self):
        own = self.block(0, 0)
        self.ahead = self.send(own, self.first, 1)
        self.behind = self.send(own, self.first, -1)
        self.spread(0)

    def forward_first(self):
        half = SHARD_ROWS // 2
        self.ahead.wait_recv()
        self.ahead = self.send(self.block(-1, 0, 0, half), self.first, 1)
        self.spread(-1)
        self.behind.wait_recv()
        self.behind = self.send(self.block(1, 0, half, half), self.first, -1)
        self.spread(1)

    def finish_first(self):
        self.ahead.wait_recv()
        self.behind.wait_recv()
        self.spread(2)

    def forward_second(self):
        half = SHARD_ROWS // 2
        for first_delta in (0, -1, 1, 2):
            ahead, behind = self.along[first_delta]
            ahead.wait_recv()
            self.onward.append(self.send(self.block(first_delta, -1, 0, half), self.second, 1))
            behind.wait_recv()
            self.onward.append(self.send(self.block(first_delta, 1, half, half), self.second, -1))

    def finish_second(self):
        for started in self.onward:
            started.wait_recv()

    def drain(self):
        for started in self.copies:
            started.wait_send()


def both_orders(build, start, width):
    half = width // 2
    return [build("z", "y", (start, half)), build("y", "z", (start + half, half))]


def add_into(target, *terms):
    total = target[...].astype(jnp.float32)
    for term in terms:
        total = total + term[...].astype(jnp.float32)
    target[...] = total.astype(target.dtype)


class ReduceStream:
    def __init__(self, place, sums, far, near, last_far, last_near, first, second, side, columns):
        self.place, self.sums, self.first, self.second = place, sums, first, second
        self.columns = columns
        self.x_at = place.at["x"] if side == 0 else 1 - place.at["x"]
        cut = pl.ds(*columns)
        self.far = lambda second_delta, low: far.at[side, second_delta % 4, pl.ds(low, 16), cut]
        self.near = lambda way, second_delta: near.at[way, side, second_delta % 4, :, cut]
        self.last_far = lambda low: last_far.at[side, pl.ds(low, 16), cut]
        self.last_near = lambda way: last_near.at[way, side, :, cut]
        self.copies = []
        self.far_in, self.near_in = {}, {}

    def block(self, first_delta, second_delta, low=0, rows=SHARD_ROWS):
        z_at, y_at = self.place.block(self.first, first_delta, self.second, second_delta)
        return self.sums.at[self.place.rows(z_at, y_at, self.x_at, low, rows), pl.ds(*self.columns)]

    def send(self, source, target, axis, delta):
        started = self.place.send(source, target, self.place.neighbour(axis, delta))
        self.copies.append(started)
        return started

    def begin(self):
        for k in (2, 1, -1, 0):
            self.far_in[k] = (
                self.send(self.block(2, k, 0, 16), self.far(k, 0), self.first, 1),
                self.send(self.block(2, k, 16, 16), self.far(k, 16), self.first, -1),
            )

    def pass_first(self):
        for k in (2, 1, -1, 0):
            ahead, behind = self.far_in[k]
            ahead.wait_recv()
            add_into(self.block(1, k, 0, 16), self.far(k, 0))
            near_ahead = self.send(self.block(1, k), self.near(0, k), self.first, 1)
            behind.wait_recv()
            add_into(self.block(-1, k, 16, 16), self.far(k, 16))
            near_behind = self.send(self.block(-1, k), self.near(1, k), self.first, -1)
            self.near_in[k] = (near_ahead, near_behind)

    def sum_first(self, k):
        for started in self.near_in[k]:
            started.wait_recv()
        add_into(self.block(0, k), self.near(0, k), self.near(1, k))

    def begin_second(self):
        self.sum_first(2)
        self.last_ahead = self.send(self.block(0, 2, 0, 16), self.last_far(0), self.second, 1)
        self.last_behind = self.send(self.block(0, 2, 16, 16), self.last_far(16), self.second, -1)
        for k in (1, -1, 0):
            self.sum_first(k)

    def pass_second(self):
        self.last_ahead.wait_recv()
        add_into(self.block(0, 1, 0, 16), self.last_far(0))
        self.last_ahead = self.send(self.block(0, 1), self.last_near(0), self.second, 1)
        self.last_behind.wait_recv()
        add_into(self.block(0, -1, 16, 16), self.last_far(16))
        self.last_behind = self.send(self.block(0, -1), self.last_near(1), self.second, -1)

    def finish(self):
        self.last_ahead.wait_recv()
        self.last_behind.wait_recv()
        add_into(self.block(0, 0), self.last_near(0), self.last_near(1))

    def drain(self):
        for started in self.copies:
            started.wait_send()


SEQ = 512
ROWS = 128
CHIP_ROWS = 256
SCALE = HEAD_SIZE ** (-0.5)
GAINS = 2 * MODEL_WIDTH + 2 * HEAD_SIZE


def rows_at(index, size):
    if isinstance(index, int):
        return pl.ds(index * size, size)
    return pl.ds(pl.multiple_of(index * size, size), size)


class Quad:
    def __init__(self, place):
        self.place = place
        self.tensor = place.tensor
        self.core, self.chip = place.tensor % 2, place.tensor // 2
        self.partner = {"tensor": self.chip * 2 + 1 - self.core}
        self.across = {"tensor": (1 - self.chip) * 2 + self.core}
        self.own_rows = rows_at(self.tensor, ROWS)
        self.near_rows = rows_at(self.chip, CHIP_ROWS)
        self.far_rows = rows_at(1 - self.chip, CHIP_ROWS)


class QuadGather:
    def __init__(self, quad, full):
        self.quad, self.full = quad, full

    def start(self):
        quad, place = self.quad, self.quad.place
        own = self.full.at[quad.own_rows]
        self.over = []
        for part in range(2):
            piece = self.full.at[pl.ds(pl.multiple_of(quad.tensor * ROWS + part * 64, 64), 64)]
            self.over.append(place.send(piece, piece, quad.across))
        self.side = place.send(own, own, quad.partner)

    def near(self):
        self.side.wait_recv()

    def forward(self):
        quad, place = self.quad, self.quad.place
        far = (1 - quad.chip) * 2 + quad.core
        self.on = []
        for part in range(2):
            self.over[part].wait_recv()
            piece = self.full.at[pl.ds(pl.multiple_of(far * ROWS + part * 64, 64), 64)]
            self.on.append(place.send(piece, piece, quad.partner))

    def finish(self):
        for started in self.on:
            started.wait_recv()

    def drain(self):
        for started in [self.side] + self.over + self.on:
            started.wait_send()


class QuadReduce:
    def __init__(self, quad, parts, chip_in, link_in):
        self.quad, self.parts, self.chip_in, self.link_in = quad, parts, chip_in, link_in
        far, near = 2 * (1 - quad.chip), 2 * quad.chip
        self.far_own, self.far_other = far + quad.core, far + 1 - quad.core
        self.near_other = near + 1 - quad.core

    def piece(self, block, part):
        return self.parts.at[rows_at(block, ROWS), pl.ds(512 * part, 512)]

    def far_ready(self):
        place, quad = self.quad.place, self.quad
        self.chip_far = [
            place.send(
                self.piece(self.far_other, part),
                self.chip_in.at[0, :, pl.ds(512 * part, 512)],
                quad.partner,
            )
            for part in range(2)
        ]

    def near_ready(self):
        self.chip_near = self.quad.place.send(
            self.parts.at[rows_at(self.near_other, ROWS)], self.chip_in.at[1], self.quad.partner
        )

    def link(self):
        place, quad = self.quad.place, self.quad
        self.over = []
        for part in range(2):
            self.chip_far[part].wait_recv()
            piece = self.piece(self.far_own, part)
            add_into(piece, self.chip_in.at[0, :, pl.ds(512 * part, 512)])
            self.over.append(
                place.send(piece, self.link_in.at[:, pl.ds(512 * part, 512)], quad.across)
            )

    def total(self):
        self.chip_near.wait_recv()
        for started in self.over:
            started.wait_recv()
        total = self.parts[self.quad.own_rows, :].astype(jnp.float32)
        total = total + self.chip_in[1].astype(jnp.float32)
        return total + self.link_in[...].astype(jnp.float32)

    def drain(self):
        for started in self.chip_far + [self.chip_near] + self.over:
            started.wait_send()


def turn_rows(source, target):
    for k in range(source.shape[1] // 128):
        target[128 * k : 128 * (k + 1), :] = source[:, 128 * k : 128 * (k + 1)].T


def rope(values, cos, sin):
    return values * cos + pltpu.roll(values, HEAD_SIZE // 2, 1) * sin


def rope_back(values, cos, sin):
    return values * cos + pltpu.roll(values * sin, HEAD_SIZE // 2, 1)


def orthogonalize(inbox, current, work, low_square, mixer, side):
    f32, bf16 = jnp.float32, jnp.bfloat16
    tiles = side // 256

    total = jnp.float32(0.0)
    for k in range(8):
        piece = inbox[4 * k : 4 * (k + 1), :, :side].reshape(4 * SHARD_ROWS, side).astype(f32)
        current[:side, 128 * k : 128 * (k + 1)] = piece.T
        total = total + jnp.sum(piece * piece)
    scale = 1.0 / (jnp.sqrt(total) + 1e-07)

    def narrow(slot):
        return work.at[pl.ds(0, side), pl.ds(pl.multiple_of(slot * MODEL_WIDTH, MODEL_WIDTH), MODEL_WIDTH)]

    energy = jnp.float32(0.0)
    for k in range(tiles):
        cut = slice(256 * k, 256 * (k + 1))
        piece = current[cut, :] * scale
        current[cut, :] = piece
        narrow(0)[cut, :] = piece.astype(bf16)
        energy = energy + jnp.sum(piece * piece)

    def newton(step, energy):
        now, later = narrow(step % 2), narrow((step + 1) % 2)
        shift = energy * (1.0 / side)
        linear = newton_two + 2.0 * newton_three * shift
        constant = newton_one + newton_two * shift + newton_three * shift * shift
        row = lax.broadcasted_iota(jnp.int32, (256, 256), 0)
        column = lax.broadcasted_iota(jnp.int32, (256, 256), 1)

        def put(target, k, part):
            cut = slice(256 * k, 256 * (k + 1))
            target[cut, 256 * k : side] = part
            for other in range(k + 1, tiles):
                block = part[:, 256 * (other - k) : 256 * (other - k + 1)]
                target[256 * other : 256 * (other + 1), cut] = block.T

        for k in range(tiles):
            part = lax.dot_general(
                now[256 * k : 256 * (k + 1), :],
                now[256 * k : side, :],
                contract_cols,
                preferred_element_type=f32,
            )
            first = jnp.where(row == column, part[:, :256] - shift, part[:, :256])
            if k < tiles - 1:
                part = jnp.concatenate([first, part[:, 256:]], axis=1)
            else:
                part = first
            put(low_square, k, part.astype(bf16))
        for k in range(tiles):
            cut = slice(256 * k, 256 * (k + 1))
            part = jnp.dot(
                low_square[cut, :side],
                low_square[:side, 256 * k : side],
                preferred_element_type=f32,
            )
            part = linear * low_square[cut, 256 * k : side].astype(f32) + newton_three * part
            put(mixer, k, part.astype(bf16))
        energy = jnp.float32(0.0)
        for k in range(tiles):
            cut = slice(256 * k, 256 * (k + 1))
            part = jnp.dot(mixer[cut, :side], now[...], preferred_element_type=f32)
            part = part + constant * current[cut, :]
            current[cut, :] = part
            later[cut, :] = part.astype(bf16)
            energy = energy + jnp.sum(part * part)
        return energy

    lax.fori_loop(0, NS_ITERS, newton, energy)
    for k in range(8):
        piece = current[:side, 128 * k : 128 * (k + 1)].T
        inbox[4 * k : 4 * (k + 1), :, :side] = piece.astype(bf16).reshape(4, SHARD_ROWS, side)


def layer_kernel(*refs):
    (
        x_in,
        positions_ref,
        cotangent_in,
        query_in,
        key_in,
        value_in,
        out_in,
        gate_in,
        up_in,
        down_in,
        query_moment_in,
        key_moment_in,
        value_moment_in,
        out_moment_in,
        gate_moment_in,
        up_moment_in,
        down_moment_in,
        gains_ref,
        gain_moment_ref,
        out_ref,
        grad_ref,
        moments_ref,
        weights_ref,
        gain_moment_out,
        gains_out,
        x_ref,
        cotangent_ref,
        shard,
        moments,
        weights,
        cos_ref,
        sin_ref,
        full,
        sums,
        far,
        near,
        last_far,
        last_near,
        swapped,
        normed,
        normed_two,
        cotangents,
        branch_grads,
        turned,
        query_raw,
        key_raw,
        query_rot,
        key_rot,
        value_low,
        key_turned,
        value_turned,
        probs,
        attention,
        attention_grad,
        hidden,
        ffn_grads,
        head_grads,
        key_sum,
        value_sum,
        hidden_one,
        input_grad,
        parts,
        chip_in,
        link_in,
        posted,
        inbox,
        current,
        settled,
        gain_parts,
        gain_tensor,
        gain_dp,
        send_sems,
        recv_sems,
        post_send,
        post_recv,
        back_send,
        back_recv,
        gain_send,
        gain_recv,
        load_sems,
        store_sems,
    ) = refs
    bf16, f32 = jnp.bfloat16, jnp.float32
    place = Place(send_sems, recv_sems)
    quad = Quad(place)
    dp, tensor = place.dp, place.tensor
    x_at = place.at["x"]

    loads = []

    def load(source, target):
        started = pltpu.make_async_copy(source, target, load_sems.at[len(loads)])
        started.start()
        loads.append(started)
        return started

    shard_ins = (query_in, key_in, value_in, out_in, gate_in, up_in, down_in)
    moment_ins = (
        query_moment_in,
        key_moment_in,
        value_moment_in,
        out_moment_in,
        gate_moment_in,
        up_moment_in,
        down_moment_in,
    )
    cuts = [pl.ds(start, width) for start, width in zip(starts, widths)]
    shard_loads = [load(source, shard.at[:, cut]) for source, cut in zip(shard_ins, cuts)]
    x_load = load(x_in, x_ref)
    cotangent_load = load(cotangent_in, cotangent_ref)
    moment_loads = [load(source, moments.at[:, cut]) for source, cut in zip(moment_ins, cuts)]

    barrier = pltpu.get_barrier_semaphore()

    def greet(k, carry):
        pl.semaphore_signal(
            barrier, inc=1, device_id={"dp": lax.rem(dp + k, DP)}, device_id_type=MESH
        )
        return carry

    lax.fori_loop(1, DP, greet, 0)
    for k in range(1, TENSOR):
        pl.semaphore_signal(
            barrier, inc=1, device_id={"tensor": lax.rem(tensor + k, TENSOR)}, device_id_type=MESH
        )
    for started in shard_loads:
        started.wait()
    mine = place.rows(place.at["z"], place.at["y"], x_at)
    full[mine, :] = shard[...]
    pl.semaphore_wait(barrier, DP - 1 + TENSOR - 1)

    def each(streams, name):
        for stream in streams:
            getattr(stream, name)()

    swaps, own, other = {}, [], []
    for start, width in gather_groups:
        for streams, x_side in ((own, x_at), (other, 1 - x_at)):
            build = lambda first, second, columns, x_side=x_side: GatherStream(
                place, full, first, second, x_side, columns
            )
            streams.append(both_orders(build, start, width))

    def swap(group):
        start, width = gather_groups[group]
        cut = full.at[mine, pl.ds(start, width)]
        swaps[group] = place.send(cut, cut, place.neighbour("x", 1))

    swap(0)
    each(own[0], "begin")

    all_gains = gains_ref[...].reshape(1, GAINS)
    gain_attn = all_gains[:, :MODEL_WIDTH]
    gain_ffn = all_gains[:, MODEL_WIDTH : 2 * MODEL_WIDTH]
    gain_query = all_gains[:, 2 * MODEL_WIDTH : 2 * MODEL_WIDTH + HEAD_SIZE]
    gain_key = all_gains[:, 2 * MODEL_WIDTH + HEAD_SIZE :]
    x_load.wait()
    x = x_ref[...].astype(f32)
    first_scale = rms_scale(x)
    normed[quad.own_rows, :] = (x * first_scale * gain_attn).astype(bf16)
    gather_normed = QuadGather(quad, normed)
    gather_normed.start()
    swap(1)

    angle = jnp.broadcast_to(
        positions_ref[...].reshape(1, SEQ).astype(f32), (HEAD_SIZE, SEQ)
    ).T
    lane = lax.broadcasted_iota(jnp.int32, (1, HEAD_SIZE), 1)
    low_half = lane < HEAD_SIZE // 2
    step = jnp.where(low_half, lane, lane - HEAD_SIZE // 2).astype(f32)
    angle = angle * jnp.exp(step * (-2.0 * math.log(rope_base) / HEAD_SIZE))
    cos_ref[...] = jnp.cos(angle)
    sin = jnp.sin(angle)
    sin_ref[...] = jnp.where(low_half, -sin, sin)

    swaps[0].wait_recv()
    each(other[0], "begin")
    each(own[0] + other[0], "forward_first")
    gather_normed.forward()
    each(own[0] + other[0], "finish_first")
    swap(2)
    each(own[1], "begin")
    each(own[0] + other[0], "forward_second")
    swaps[1].wait_recv()
    each(other[1], "begin")
    each(own[2], "begin")
    cotangent_load.wait()
    cotangents[quad.own_rows, :] = cotangent_ref[...]
    gather_cotangent = QuadGather(quad, cotangents)
    gather_normed.near()
    gather_normed.finish()
    turn_rows(normed, turned.at[1])
    each(own[0] + other[0], "finish_second")

    def project_query(k):
        pair = jnp.dot(normed[...], full[:, rows_at(k, 256)], preferred_element_type=f32)
        query_raw[:, rows_at(k, 256)] = pair
        for head in range(2):
            raw = pair[:, HEAD_SIZE * head : HEAD_SIZE * (head + 1)]
            rotated = rope(raw * rms_scale(raw) * gain_query, cos_ref[...], sin_ref[...])
            query_rot[:, rows_at(2 * k + head, HEAD_SIZE)] = rotated.astype(bf16)

    project_query(0)
    each(own[1] + other[1], "forward_first")
    project_query(1)
    swaps[2].wait_recv()
    each(other[2], "begin")
    swap(3)
    pair = jnp.dot(normed[...], full[:, 512:768], preferred_element_type=f32)
    key_raw[...] = pair
    for head in range(2):
        raw = pair[:, HEAD_SIZE * head : HEAD_SIZE * (head + 1)]
        rotated = rope(raw * rms_scale(raw) * gain_key, cos_ref[...], sin_ref[...]).astype(bf16)
        key_rot[:, HEAD_SIZE * head : HEAD_SIZE * (head + 1)] = rotated
        key_turned[HEAD_SIZE * head : HEAD_SIZE * (head + 1), :] = rotated.T
    each(own[1] + other[1], "finish_first")
    pair = jnp.dot(normed[...], full[:, 768:1024], preferred_element_type=f32).astype(bf16)
    value_low[...] = pair
    for head in range(2):
        value_turned[HEAD_SIZE * head : HEAD_SIZE * (head + 1), :] = pair[
            :, HEAD_SIZE * head : HEAD_SIZE * (head + 1)
        ].T
    each(own[2] + other[2], "forward_first")

    def attend(head):
        lanes, shared = rows_at(head, HEAD_SIZE), rows_at(head // 2, HEAD_SIZE)
        for block in range(2):
            keys, begin = 256 * (block + 1), 256 * block
            scores = lax.dot_general(
                key_rot[pl.ds(0, keys), shared],
                query_rot[pl.ds(begin, 256), lanes],
                contract_cols,
                preferred_element_type=f32,
            )
            row = lax.broadcasted_iota(jnp.int32, (keys, 256), 0)
            column = lax.broadcasted_iota(jnp.int32, (keys, 256), 1) + begin
            scores = jnp.where(row <= column, scores * SCALE, -1e30)
            shifted = jnp.exp(scores - jnp.max(scores, axis=0, keepdims=True))
            total = jnp.sum(shifted, axis=0, keepdims=True)
            low = (shifted * (1.0 / total)).astype(bf16)
            probs[head, pl.ds(0, keys), pl.ds(begin, 256)] = low
            mixed = jnp.dot(
                value_turned[shared, pl.ds(0, keys)], low, preferred_element_type=f32
            )
            attention[pl.ds(begin, 256), lanes] = mixed.T.astype(bf16)

    attend(0)
    each(own[1] + other[1], "forward_second")
    attend(1)
    each(own[2] + other[2], "finish_first")
    gather_cotangent.start()
    attend(2)
    swaps[3].wait_recv()
    each(own[3] + other[3], "begin")
    attend(3)
    each(own[1] + other[1], "finish_second")

    def project_back(source, start, width, target):
        def run(rows):
            for k in range(4):
                part = lax.dot_general(
                    source[rows, :],
                    full[256 * k : 256 * (k + 1), start : start + width],
                    contract_cols,
                    preferred_element_type=f32,
                )
                target[rows, 256 * k : 256 * (k + 1)] = part.astype(bf16)

        return run

    def reducer(k):
        return QuadReduce(quad, parts.at[k], chip_in.at[k], link_in.at[k])

    reduce_attn = reducer(0)
    out_rows = project_back(attention, 1024, 512, parts.at[0])
    out_rows(quad.far_rows)
    reduce_attn.far_ready()
    each(own[3] + other[3], "forward_first")
    out_rows(quad.near_rows)
    reduce_attn.near_ready()
    reduce_attn.link()
    gather_cotangent.forward()
    each(own[2] + other[2], "forward_second")
    each(own[3] + other[3], "finish_first")
    x = x_ref[...].astype(f32)
    first_hidden = x + reduce_attn.total()
    hidden_one[...] = first_hidden
    normed_two[quad.own_rows, :] = (
        first_hidden * rms_scale(first_hidden) * gain_ffn
    ).astype(bf16)
    gather_two = QuadGather(quad, normed_two)
    gather_two.start()
    each(own[3] + other[3], "forward_second")
    gather_cotangent.near()
    gather_cotangent.finish()
    turn_rows(cotangents, turned.at[0])
    each(own[2] + other[2], "finish_second")
    gather_two.forward()
    each(own[3] + other[3], "finish_second")

    def feed(rows):
        for k in range(3):
            low = normed_two[rows, :]
            at = 256 * k
            gate = jnp.dot(low, full[:, 1536 + at : 1792 + at], preferred_element_type=f32)
            up = jnp.dot(low, full[:, 2304 + at : 2560 + at], preferred_element_type=f32)
            grad = jnp.dot(
                cotangents[rows, :], full[:, 3072 + at : 3328 + at], preferred_element_type=f32
            )
            sigmoid = 1.0 / (1.0 + jnp.exp(-gate))
            activated = gate * sigmoid
            hidden[rows, at : at + 256] = (activated * up).astype(bf16)
            ffn_grads[rows, at : at + 256] = (
                grad * up * (sigmoid * (1.0 + gate * (1.0 - sigmoid)))
            ).astype(bf16)
            ffn_grads[rows, 768 + at : 1024 + at] = (grad * activated).astype(bf16)

    reduce_two = reducer(1)
    two_rows = project_back(ffn_grads, 1536, 1536, parts.at[1])
    gather_two.near()
    feed(quad.near_rows)
    two_rows(quad.near_rows)
    reduce_two.near_ready()
    gather_two.finish()
    feed(quad.far_rows)
    two_rows(quad.far_rows)
    reduce_two.far_ready()

    def weight_grads(left, right, start, first, last):
        for k in range(first, last):
            part = jnp.dot(
                left[...], right[:, 256 * k : 256 * (k + 1)], preferred_element_type=f32
            )
            sums[:, start + 256 * k : start + 256 * (k + 1)] = part.astype(bf16)

    weight_grads(turned.at[0], hidden, 3072, 0, 2)
    reduce_two.link()
    weight_grads(turned.at[0], hidden, 3072, 2, 3)
    turn_rows(normed_two, turned.at[0])
    weight_grads(turned.at[0], ffn_grads, 1536, 0, 4)

    own_sums, other_sums = [], []
    for start, width in reduce_groups:
        for streams, side in ((own_sums, 0), (other_sums, 1)):
            build = lambda first, second, columns, side=side: ReduceStream(
                place, sums, far, near, last_far, last_near, first, second, side, columns
            )
            streams.append(both_orders(build, start, width))
    sum_swaps = {}

    def swap_sums(group):
        start, width = reduce_groups[group]
        partial = sums.at[
            place.rows(place.at["z"], place.at["y"], 1 - x_at), pl.ds(start, width)
        ]
        sum_swaps[group] = place.send(
            partial, swapped.at[:, pl.ds(start, width)], place.neighbour("x", 1)
        )

    normed_two_grad = reduce_two.total()
    first_hidden = hidden_one[...]
    second_scale = rms_scale(first_hidden)
    second_hat = first_hidden * second_scale
    gain_parts[:, MODEL_WIDTH : 2 * MODEL_WIDTH] = jnp.sum(
        normed_two_grad * second_hat, axis=0, keepdims=True
    )
    hidden_one_grad = cotangent_ref[...].astype(f32) + norm_backward(
        normed_two_grad * gain_ffn, second_hat, second_scale
    )
    input_grad[...] = hidden_one_grad
    branch_grads[quad.own_rows, :] = hidden_one_grad.astype(bf16)
    gather_branch = QuadGather(quad, branch_grads)
    gather_branch.start()
    weight_grads(turned.at[0], ffn_grads, 1536, 4, 6)
    each(other_sums[2] + own_sums[2], "begin")

    reduce_ffn = reducer(2)
    down_rows = project_back(hidden, 3072, 768, parts.at[2])
    gather_branch.forward()
    down_rows(quad.far_rows)
    reduce_ffn.far_ready()

    def attend_grad(rows):
        part = jnp.dot(branch_grads[rows, :], full[:, 1024:1536], preferred_element_type=f32)
        attention_grad[rows, :] = part.astype(bf16)

    gather_branch.near()
    attend_grad(quad.near_rows)
    gather_branch.finish()
    attend_grad(quad.far_rows)
    reduce_ffn.link()
    turn_rows(branch_grads, turned.at[0])
    weight_grads(turned.at[0], attention, 1024, 0, 2)
    each(other_sums[1] + own_sums[1], "begin")
    each(other_sums[2], "pass_first")

    def head_norm_back(rotated_grad, raw, gain, rows):
        scale = rms_scale(raw)
        hat = raw * scale
        norm_grad = rope_back(rotated_grad, cos_ref[rows, :], sin_ref[rows, :])
        gain_grad = jnp.sum(norm_grad * hat, axis=0, keepdims=True)
        return norm_backward(norm_grad * gain, hat, scale).astype(bf16), gain_grad

    def attend_back(head, gain_sum):
        lanes, shared = rows_at(head, HEAD_SIZE), rows_at(head // 2, HEAD_SIZE)
        for block in (1, 0):
            keys, begin = 256 * (block + 1), 256 * block
            key_cut, query_cut = pl.ds(0, keys), pl.ds(begin, 256)
            mixed_grad = attention_grad[query_cut, lanes]
            low = probs[head, key_cut, query_cut]
            wide = low.astype(f32)
            probs_grad = lax.dot_general(
                value_low[key_cut, shared],
                mixed_grad,
                contract_cols,
                preferred_element_type=f32,
            )
            inner_sum = jnp.sum(wide * probs_grad, axis=0, keepdims=True)
            score_grad = (wide * (probs_grad - inner_sum)).astype(bf16)
            value_part = jnp.dot(low, mixed_grad, preferred_element_type=f32)
            key_part = jnp.dot(
                score_grad, query_rot[query_cut, lanes], preferred_element_type=f32
            )
            if head % 2 == 0 and block == 1:
                value_sum[:, shared] = value_part
                key_sum[:, shared] = key_part
            else:
                value_sum[key_cut, shared] += value_part
                key_sum[key_cut, shared] += key_part
            query_part = jnp.dot(
                key_turned[shared, key_cut], score_grad, preferred_element_type=f32
            )
            grad, gain_part = head_norm_back(
                query_part.T * SCALE, query_raw[query_cut, lanes], gain_query, query_cut
            )
            head_grads[query_cut, lanes] = grad
            gain_sum = gain_sum + gain_part
        return gain_sum

    def shared_back(head, gain_sum):
        shared = rows_at(head, HEAD_SIZE)
        grad, gain_part = head_norm_back(
            key_sum[:, shared] * SCALE, key_raw[:, shared], gain_key, pl.ds(0, SEQ)
        )
        head_grads[:, rows_at(4 + head, HEAD_SIZE)] = grad
        head_grads[:, rows_at(6 + head, HEAD_SIZE)] = value_sum[:, shared].astype(bf16)
        return gain_sum + gain_part

    none = jnp.zeros((1, HEAD_SIZE), f32)
    query_gain_sum = attend_back(0, none)
    each(own_sums[2], "pass_first")
    query_gain_sum = attend_back(1, query_gain_sum)
    key_gain_sum = shared_back(0, none)
    each(other_sums[2], "begin_second")
    query_gain_sum = attend_back(2, query_gain_sum)
    each(own_sums[2], "begin_second")
    each(other_sums[1] + own_sums[1], "pass_first")
    query_gain_sum = attend_back(3, query_gain_sum)
    key_gain_sum = shared_back(1, key_gain_sum)
    gain_parts[:, 2 * MODEL_WIDTH : 2 * MODEL_WIDTH + HEAD_SIZE] = query_gain_sum
    gain_parts[:, 2 * MODEL_WIDTH + HEAD_SIZE :] = key_gain_sum
    each(other_sums[2] + own_sums[2], "pass_second")
    weight_grads(turned.at[1], head_grads, 0, 0, 2)
    each(other_sums[1] + own_sums[1], "begin_second")
    weight_grads(turned.at[1], head_grads, 0, 2, 4)
    each(other_sums[0] + own_sums[0], "begin")
    each(other_sums[2], "finish")
    swap_sums(2)

    reduce_one = reducer(3)
    one_rows = project_back(head_grads, 0, 1024, parts.at[3])
    one_rows(quad.far_rows)
    reduce_one.far_ready()
    each(own_sums[2], "finish")
    each(other_sums[1] + own_sums[1], "pass_second")
    one_rows(quad.near_rows)
    reduce_one.near_ready()
    reduce_one.link()
    down_rows(quad.near_rows)
    reduce_ffn.near_ready()
    each(other_sums[0], "pass_first")
    each(other_sums[1], "finish")
    swap_sums(1)
    each(own_sums[1], "finish")
    each(own_sums[0], "pass_first")

    for started in moment_loads:
        started.wait()
    core = tensor % 2
    owner = [even + core * (odd - even) for even, odd in owners]
    stores = []

    def store(source, target):
        started = pltpu.make_async_copy(source, target, store_sems.at[len(stores)])
        started.start()
        stores.append(started)

    def post_copy(slot):
        return pltpu.make_async_remote_copy(
            src_ref=posted.at[:, cuts[slot]],
            dst_ref=inbox.at[dp, :, pl.ds(0, widths[slot])],
            send_sem=post_send.at[slot],
            recv_sem=post_recv.at[dp],
            device_id={"dp": owner[slot]},
            device_id_type=MESH,
        )

    def update(group):
        start, width = reduce_groups[group]
        cut = pl.ds(start, width)
        sum_swaps[group].wait_recv()
        total = sums[mine, cut].astype(f32) + swapped[:, cut].astype(f32)
        fresh = moment_decay * moments[:, cut] + total
        moments[:, cut] = fresh
        posted[:, cut] = fresh.astype(bf16)
        store(moments.at[:, cut], moments_ref.at[:, cut])
        for slot in group_slots[group]:

            @pl.when(dp != owner[slot])
            def _():
                post_copy(slot).start()

            @pl.when(dp == owner[slot])
            def _():
                inbox[dp, :, : widths[slot]] = posted[:, cuts[slot]]
                if widths[slot] < 512:
                    inbox[:, :, widths[slot] : 512] = jnp.zeros(
                        (DP, SHARD_ROWS, 512 - widths[slot]), bf16
                    )

    update(2)
    each(other_sums[0], "begin_second")

    reduce_ffn_total = reduce_ffn.total()
    hidden_one[...] = hidden_one[...] + reduce_ffn_total
    store(hidden_one, out_ref)
    each(own_sums[0], "begin_second")
    normed_grad = reduce_one.total()
    x = x_ref[...].astype(f32)
    first_scale = rms_scale(x)
    first_hat = x * first_scale
    gain_parts[:, :MODEL_WIDTH] = jnp.sum(normed_grad * first_hat, axis=0, keepdims=True)
    input_grad[...] = input_grad[...] + norm_backward(
        normed_grad * gain_attn, first_hat, first_scale
    )
    store(input_grad, grad_ref)
    each(other_sums[0] + own_sums[0], "pass_second")
    update(1)
    each(other_sums[0], "finish")
    swap_sums(0)
    each(own_sums[0], "finish")

    gain_tensor[tensor] = gain_parts[...]
    gain_copies = []
    for k in range(1, TENSOR):
        started = pltpu.make_async_remote_copy(
            src_ref=gain_parts,
            dst_ref=gain_tensor.at[tensor],
            send_sem=gain_send.at[k],
            recv_sem=gain_recv.at[k],
            device_id={"tensor": lax.rem(tensor + k, TENSOR)},
            device_id_type=MESH,
        )
        started.start()
        gain_copies.append(started)
    update(0)

    for copies in (swaps, sum_swaps):
        for started in copies.values():
            started.wait_send()
    for groups in (own, other, own_sums, other_sums):
        for streams in groups:
            each(streams, "drain")
    for exchange in (gather_normed, gather_cotangent, gather_two, gather_branch):
        exchange.drain()
    for exchange in (reduce_attn, reduce_two, reduce_ffn, reduce_one):
        exchange.drain()

    for started in gain_copies:
        started.wait_recv()
    gain_dp[dp] = gain_tensor[0] + gain_tensor[1] + gain_tensor[2] + gain_tensor[3]

    def gain_copy(k):
        return pltpu.make_async_remote_copy(
            src_ref=gain_dp.at[dp],
            dst_ref=gain_dp.at[dp],
            send_sem=gain_send.at[TENSOR + k],
            recv_sem=gain_recv.at[TENSOR + k],
            device_id={"dp": lax.rem(dp + k, DP)},
            device_id_type=MESH,
        )

    def gain_start(k, carry):
        gain_copy(k).start()
        return carry

    lax.fori_loop(1, DP, gain_start, 0)

    for slot in (4, 5, 6, 3, 0, 1, 2):

        @pl.when(dp == owner[slot])
        def _():
            def arrive(k, carry):
                source = lax.rem(dp + k, DP)
                piece = inbox.at[source, :, pl.ds(0, widths[slot])]
                pltpu.make_async_remote_copy(
                    src_ref=piece,
                    dst_ref=piece,
                    send_sem=post_send.at[slot],
                    recv_sem=post_recv.at[source],
                    device_id={"dp": source},
                    device_id_type=MESH,
                ).wait_recv()
                return carry

            lax.fori_loop(1, DP, arrive, 0)

    work = full.at[:, pl.ds(0, 2 * MODEL_WIDTH)]
    low_square = full.at[:WIDEST, pl.ds(2048, WIDEST)]
    mixer = full.at[:WIDEST, pl.ds(2816, WIDEST)]
    wide = (dp == owner[4]) | (dp == owner[5]) | (dp == owner[6])
    slim = (dp == owner[0]) | (dp == owner[1]) | (dp == owner[2]) | (dp == owner[3])

    @pl.when(wide)
    def _():
        orthogonalize(inbox, current, work, low_square, mixer, WIDEST)

    @pl.when(slim)
    def _():
        orthogonalize(inbox, current, work, low_square, mixer, 512)

    def back(slot, k):
        target = lax.rem(dp + k, DP)
        return pltpu.make_async_remote_copy(
            src_ref=inbox.at[target, :, pl.ds(0, widths[slot])],
            dst_ref=settled.at[:, cuts[slot]],
            send_sem=back_send.at[k],
            recv_sem=back_recv.at[slot],
            device_id={"dp": target},
            device_id_type=MESH,
        )

    for slot in range(7):

        @pl.when(dp == owner[slot])
        def _():
            def back_start(k, carry):
                back(slot, k).start()
                return carry

            lax.fori_loop(1, DP, back_start, 0)
            settled[:, cuts[slot]] = inbox[dp, :, : widths[slot]]

    def gain_arrive(k, carry):
        gain_copy(k).wait_recv()
        return carry

    lax.fori_loop(1, DP, gain_arrive, 0)

    def gain_add(k, carry):
        return carry + gain_dp[k]

    gain_total = lax.fori_loop(1, DP, gain_add, gain_dp[0]).reshape(GAINS)
    fresh_gain = gain_decay * gain_moment_ref[...] + gain_total
    gain_moment_out[...] = fresh_gain
    gains_out[...] = gains_ref[...] - gain_rate / math.sqrt(SEQ * DP) * fresh_gain

    for slot in (1, 2, 0, 3, 4, 5, 6):

        @pl.when(dp != owner[slot])
        def _():
            pltpu.make_async_remote_copy(
                src_ref=inbox.at[0, :, pl.ds(0, widths[slot])],
                dst_ref=settled.at[:, cuts[slot]],
                send_sem=post_send.at[slot],
                recv_sem=back_recv.at[slot],
                device_id={"dp": owner[slot]},
                device_id_type=MESH,
            ).wait_recv()

        cut = cuts[slot]
        weights[:, cut] = shard[:, cut].astype(f32) - rates[slot] * settled[:, cut].astype(f32)
        store(weights.at[:, cut], weights_ref.at[:, cut])

    for started in gain_copies:
        started.wait_send()

    def gain_sent(k, carry):
        gain_copy(k).wait_send()
        return carry

    lax.fori_loop(1, DP, gain_sent, 0)
    for slot in range(7):

        @pl.when(dp != owner[slot])
        def _():
            post_copy(slot).wait_send()

        @pl.when(dp == owner[slot])
        def _():
            def back_sent(k, carry):
                back(slot, k).wait_send()
                return carry

            lax.fori_loop(1, DP, back_sent, 0)

    for started in stores:
        started.wait()


def run_layer(args):
    bf16, f32 = jnp.bfloat16, jnp.float32
    shard_shape = (SHARD_ROWS, COLUMNS)
    dma = pltpu.SemaphoreType.DMA
    copies = 660
    in_specs = [ANY] * 19
    in_specs[1] = in_specs[17] = in_specs[18] = VMEM
    return pl.pallas_call(
        layer_kernel,
        out_shape=(
            jax.ShapeDtypeStruct((ROWS, MODEL_WIDTH), f32),
            jax.ShapeDtypeStruct((ROWS, MODEL_WIDTH), f32),
            jax.ShapeDtypeStruct(shard_shape, f32),
            jax.ShapeDtypeStruct(shard_shape, f32),
            jax.ShapeDtypeStruct((GAINS,), f32),
            jax.ShapeDtypeStruct((GAINS,), f32),
        ),
        in_specs=in_specs,
        out_specs=(ANY, ANY, ANY, ANY, VMEM, VMEM),
        scratch_shapes=[
            pltpu.VMEM((ROWS, MODEL_WIDTH), bf16),
            pltpu.VMEM((ROWS, MODEL_WIDTH), bf16),
            pltpu.VMEM(shard_shape, bf16),
            pltpu.VMEM(shard_shape, f32),
            pltpu.VMEM(shard_shape, f32),
            pltpu.VMEM((SEQ, HEAD_SIZE), f32),
            pltpu.VMEM((SEQ, HEAD_SIZE), f32),
            pltpu.VMEM((MODEL_WIDTH, COLUMNS), bf16),
            pltpu.VMEM((MODEL_WIDTH, COLUMNS), bf16),
            pltpu.VMEM((2, 4, SHARD_ROWS, COLUMNS), bf16),
            pltpu.VMEM((2, 2, 4, SHARD_ROWS, COLUMNS), bf16),
            pltpu.VMEM((2, SHARD_ROWS, COLUMNS), bf16),
            pltpu.VMEM((2, 2, SHARD_ROWS, COLUMNS), bf16),
            pltpu.VMEM(shard_shape, bf16),
            pltpu.VMEM((SEQ, MODEL_WIDTH), bf16),
            pltpu.VMEM((SEQ, MODEL_WIDTH), bf16),
            pltpu.VMEM((SEQ, MODEL_WIDTH), bf16),
            pltpu.VMEM((SEQ, MODEL_WIDTH), bf16),
            pltpu.VMEM((2, MODEL_WIDTH, SEQ), bf16),
            pltpu.VMEM((SEQ, 512), f32),
            pltpu.VMEM((SEQ, 256), f32),
            pltpu.VMEM((SEQ, 512), bf16),
            pltpu.VMEM((SEQ, 256), bf16),
            pltpu.VMEM((SEQ, 256), bf16),
            pltpu.VMEM((256, SEQ), bf16),
            pltpu.VMEM((256, SEQ), bf16),
            pltpu.VMEM((4, SEQ, SEQ), bf16),
            pltpu.VMEM((SEQ, 512), bf16),
            pltpu.VMEM((SEQ, 512), bf16),
            pltpu.VMEM((SEQ, 768), bf16),
            pltpu.VMEM((SEQ, 1536), bf16),
            pltpu.VMEM((SEQ, 1024), bf16),
            pltpu.VMEM((SEQ, 256), f32),
            pltpu.VMEM((SEQ, 256), f32),
            pltpu.VMEM((ROWS, MODEL_WIDTH), f32),
            pltpu.VMEM((ROWS, MODEL_WIDTH), f32),
            pltpu.VMEM((4, SEQ, MODEL_WIDTH), bf16),
            pltpu.VMEM((4, 2, ROWS, MODEL_WIDTH), bf16),
            pltpu.VMEM((4, ROWS, MODEL_WIDTH), bf16),
            pltpu.VMEM(shard_shape, bf16),
            pltpu.VMEM((DP, SHARD_ROWS, WIDEST), bf16),
            pltpu.VMEM((WIDEST, MODEL_WIDTH), f32),
            pltpu.VMEM(shard_shape, bf16),
            pltpu.VMEM((1, GAINS), f32),
            pltpu.VMEM((TENSOR, 1, GAINS), f32),
            pltpu.VMEM((DP, 1, GAINS), f32),
            dma((copies,)),
            dma((copies,)),
            dma((7,)),
            dma((DP,)),
            dma((DP,)),
            dma((7,)),
            dma((TENSOR + DP,)),
            dma((TENSOR + DP,)),
            dma((16,)),
            dma((12,)),
        ],
        compiler_params=pltpu.CompilerParams(
            collective_id=0, has_side_effects=True, vmem_limit_bytes=62 << 20
        ),
        name="layer",
    )(*args)


def unpack_kernel(*refs):
    sources, targets = refs[:6], refs[6:]
    out, grad, moments, weights, gain_moment, gains = sources
    targets[0][...] = out[...]
    targets[1][...] = grad[...]
    for slot in range(7):
        cut = pl.ds(starts[slot], widths[slot])
        targets[2 + slot][...] = moments[:, cut]
        targets[9 + slot][...] = weights[:, cut]
    targets[16][...] = gain_moment[...]
    targets[17][...] = gains[...]


def unpack(results):
    f32 = jnp.float32
    pieces = [jax.ShapeDtypeStruct((SHARD_ROWS, width), f32) for width in widths]
    shapes = [jax.ShapeDtypeStruct((ROWS, MODEL_WIDTH), f32)] * 2
    shapes += pieces + pieces + [jax.ShapeDtypeStruct((GAINS,), f32)] * 2
    return pl.pallas_call(
        unpack_kernel,
        out_shape=tuple(shapes),
        in_specs=[VMEM] * 6,
        out_specs=(VMEM,) * 18,
        name="unpack",
    )(*results)


def body(*args):
    args = list(args)
    for index in (6, 9, 13, 16):
        args[index] = args[index].T
    results = list(unpack(run_layer(args)))
    for index in (5, 8, 12, 15):
        results[index] = results[index].T
    return tuple(results)


def solution(mesh):
    placed = (
        P(("dp", "tensor"), None),
        P("dp"),
        P(("dp", "tensor"), None),
        P("dp", "tensor"),
        P("dp", "tensor"),
        P("dp", "tensor"),
        P("tensor", "dp"),
        P("dp", "tensor"),
        P("dp", "tensor"),
        P("tensor", "dp"),
        P("dp", "tensor"),
        P("dp", "tensor"),
        P("dp", "tensor"),
        P("tensor", "dp"),
        P("dp", "tensor"),
        P("dp", "tensor"),
        P("tensor", "dp"),
        P(),
        P(),
    )
    return jax.shard_map(
        body,
        mesh=mesh,
        in_specs=placed,
        out_specs=(
            P(("dp", "tensor"), None),
            P(("dp", "tensor"), None),
            P("dp", "tensor"),
            P("dp", "tensor"),
            P("dp", "tensor"),
            P("tensor", "dp"),
            P("dp", "tensor"),
            P("dp", "tensor"),
            P("tensor", "dp"),
            P("dp", "tensor"),
            P("dp", "tensor"),
            P("dp", "tensor"),
            P("tensor", "dp"),
            P("dp", "tensor"),
            P("dp", "tensor"),
            P("tensor", "dp"),
            P(),
            P(),
        ),
        check_vma=False,
    )
```

```python
import functools
import math

import jax
import jax.numpy as jnp
from jax import lax
from jax.experimental import pallas as pl
from jax.experimental.pallas import tpu as pltpu
from jax.sharding import PartitionSpec as P

MODEL_WIDTH = 1024
HEAD_SIZE = 128
NS_ITERS = 5


epsilon = 1e-06
moment_decay = 0.95
gain_decay = 0.9
gain_rate = 0.3
rope_base = 1000000.0
newton_one = 3.4445
newton_two = -4.775
newton_three = 2.0315
contract_rows = (((0,), (0,)), ((), ()))
contract_cols = (((1,), (1,)), ((), ()))


def rms_scale(values):
    return lax.rsqrt(jnp.mean(values * values, axis=-1, keepdims=True) + epsilon)


def norm_backward(gradient_value, normalized_input, scale_value):
    return scale_value * (
        gradient_value
        - normalized_input * jnp.mean(gradient_value * normalized_input, axis=-1, keepdims=True)
    )


COLUMNS = 3840
widths = (512, 256, 256, 512, 768, 768, 768)
starts = (0, 512, 768, 1024, 1536, 2304, 3072)
owners = ((8, 26), (6, 17), (28, 3), (25, 14), (0, 31), (13, 5), (18, 23))
rates = (1.0, 1.0, 1.0, math.sqrt(8.0), 1.0, 1.0, math.sqrt(4.0 / 3.0))
column_groups = ((0, 1024), (1024, 512), (1536, 1536), (3072, 768))
group_slots = ((0, 1, 2), (3,), (4, 5), (6,))
DP = 32
TENSOR = 4
SHARD_ROWS = 32
HALF = SHARD_ROWS // 2
WIDEST = 768
MESH = pl.DeviceIdType.MESH
ANY = pl.BlockSpec(memory_space=pl.ANY)
VMEM = pl.BlockSpec(memory_space=pltpu.VMEM)


class Place:
    def __init__(self, send_sems, recv_sems):
        self.send_sems, self.recv_sems = send_sems, recv_sems
        self.sends, self.recvs = 0, 0
        self.dp = lax.axis_index("dp")
        self.tensor = lax.axis_index("tensor")
        self.at = {"z": self.dp // 8, "y": (self.dp // 2) % 4, "x": self.dp % 2}

    def send_sem(self):
        self.sends += 1
        return self.send_sems.at[self.sends - 1]

    def recv_sem(self):
        self.recvs += 1
        return self.recv_sems.at[self.recvs - 1]

    def step(self, axis, delta):
        size = 2 if axis == "x" else 4
        return lax.rem(self.at[axis] + size + delta, size)

    def neighbour(self, axis, delta):
        at = dict(self.at)
        at[axis] = self.step(axis, delta)
        return {"dp": at["z"] * 8 + at["y"] * 2 + at["x"]}

    def block(self, axis, delta, other, other_delta):
        first, second = self.step(axis, delta), self.step(other, other_delta)
        return (first, second) if axis == "z" else (second, first)

    def rows(self, z_at, y_at, x_at, low=0, rows=SHARD_ROWS):
        begin = (z_at * 8 + y_at * 2 + x_at) * SHARD_ROWS + low
        return pl.ds(pl.multiple_of(begin, 16), rows)

    def copy(self, source, target, device, sent, received):
        return pltpu.make_async_remote_copy(
            src_ref=source,
            dst_ref=target,
            send_sem=sent,
            recv_sem=received,
            device_id=device,
            device_id_type=MESH,
        )

    def send(self, source, target, device, sent, received):
        self.copy(source, target, device, sent, received).start()

    def arrived(self, like, received):
        self.copy(like, like, self.neighbour("x", 1), received, received).wait_recv()

    def left(self, like, sent):
        self.copy(like, like, self.neighbour("x", 1), sent, sent).wait_send()


def two_orders(group):
    start, width = group
    half = width // 2
    return (("z", "y", (start, half)), ("y", "z", (start + half, half)))


class GatherSide:
    def __init__(self, place, full, x_at, group, sent):
        self.place, self.full, self.x_at, self.group, self.sent = place, full, x_at, group, sent
        self.direct, self.passed = place.recv_sem(), place.recv_sem()
        self.along = {k: place.recv_sem() for k in (0, -1, 1, 2)}
        self.last = place.recv_sem()

    def send(self, stream, first_delta, second_delta, low, rows, axis, delta, received):
        first, second, columns = stream
        z_at, y_at = self.place.block(first, first_delta, second, second_delta)
        ref = self.full.at[self.place.rows(z_at, y_at, self.x_at, low, rows), pl.ds(*columns)]
        self.place.send(ref, ref, self.place.neighbour(axis, delta), self.sent, received)

    def wait(self, received, rows):
        self.place.arrived(self.full.at[pl.ds(0, rows), pl.ds(*self.group)], received)

    def spread(self, first_delta):
        for stream in two_orders(self.group):
            for delta in (1, -1):
                self.send(
                    stream, first_delta, 0, 0, SHARD_ROWS, stream[1], delta, self.along[first_delta]
                )

    def begin(self):
        for stream in two_orders(self.group):
            for delta in (1, -1):
                self.send(stream, 0, 0, 0, SHARD_ROWS, stream[0], delta, self.direct)
        self.spread(0)

    def forward_first(self):
        self.wait(self.direct, 2 * SHARD_ROWS)
        for stream in two_orders(self.group):
            self.send(stream, -1, 0, 0, HALF, stream[0], 1, self.passed)
            self.send(stream, 1, 0, HALF, HALF, stream[0], -1, self.passed)
        self.spread(-1)
        self.spread(1)

    def finish_first(self):
        self.wait(self.passed, SHARD_ROWS)
        self.spread(2)

    def forward_second(self):
        for first_delta in (0, -1, 1, 2):
            self.wait(self.along[first_delta], 2 * SHARD_ROWS)
            for stream in two_orders(self.group):
                self.send(stream, first_delta, -1, 0, HALF, stream[1], 1, self.last)
                self.send(stream, first_delta, 1, HALF, HALF, stream[1], -1, self.last)

    def finish_second(self):
        self.wait(self.last, 4 * SHARD_ROWS)


class Gather:
    def __init__(self, place, full, group):
        self.place, self.full, self.group = place, full, group
        self.sent, self.swapped = place.send_sem(), place.recv_sem()
        x_at = place.at["x"]
        self.own = GatherSide(place, full, x_at, group, self.sent)
        self.other = GatherSide(place, full, 1 - x_at, group, self.sent)
        self.mine = full.at[place.rows(place.at["z"], place.at["y"], x_at), pl.ds(*group)]

    def swap(self):
        self.place.send(
            self.mine, self.mine, self.place.neighbour("x", 1), self.sent, self.swapped
        )

    def begin_other(self):
        self.place.arrived(self.mine, self.swapped)
        self.other.begin()

    def both(self, name):
        for side in (self.own, self.other):
            getattr(side, name)()

    def drain(self):
        rows = (DP - 1) * SHARD_ROWS
        self.place.left(self.full.at[pl.ds(0, rows), pl.ds(*self.group)], self.sent)


def add_into(target, *terms):
    total = target[...].astype(jnp.float32)
    for term in terms:
        total = total + term[...].astype(jnp.float32)
    target[...] = total.astype(target.dtype)


class ReduceSide:
    def __init__(self, place, buffers, side, group, sent):
        self.place, self.side, self.group, self.sent = place, side, group, sent
        self.sums, self.far, self.near, self.last_far, self.last_near = buffers
        self.x_at = place.at["x"] if side == 0 else 1 - place.at["x"]
        self.far_sem = {k: place.recv_sem() for k in (0, -1, 1, 2)}
        self.near_sem = {k: place.recv_sem() for k in (0, -1, 1, 2)}
        self.last_far_sem, self.last_near_sem = place.recv_sem(), place.recv_sem()

    def block(self, stream, first_delta, second_delta, low=0, rows=SHARD_ROWS):
        first, second, columns = stream
        z_at, y_at = self.place.block(first, first_delta, second, second_delta)
        return self.sums.at[self.place.rows(z_at, y_at, self.x_at, low, rows), pl.ds(*columns)]

    def send(self, source, target, axis, delta, received):
        self.place.send(source, target, self.place.neighbour(axis, delta), self.sent, received)

    def wait(self, received, rows):
        self.place.arrived(self.sums.at[pl.ds(0, rows), pl.ds(*self.group)], received)

    def begin(self):
        for k in (2, 1, -1, 0):
            for stream in two_orders(self.group):
                far = self.far.at[self.side, k % 4, :, pl.ds(*stream[2])]
                for low, delta in ((0, 1), (HALF, -1)):
                    self.send(
                        self.block(stream, 2, k, low, HALF),
                        far.at[pl.ds(low, HALF)],
                        stream[0],
                        delta,
                        self.far_sem[k],
                    )

    def pass_first(self):
        for k in (2, 1, -1, 0):
            self.wait(self.far_sem[k], SHARD_ROWS)
            for stream in two_orders(self.group):
                far = self.far.at[self.side, k % 4, :, pl.ds(*stream[2])]
                for way, (low, delta) in enumerate(((0, 1), (HALF, -1))):
                    add_into(self.block(stream, delta, k, low, HALF), far.at[pl.ds(low, HALF)])
                    self.send(
                        self.block(stream, delta, k),
                        self.near.at[way, self.side, k % 4, :, pl.ds(*stream[2])],
                        stream[0],
                        delta,
                        self.near_sem[k],
                    )

    def begin_second(self):
        for k in (2, 1, -1, 0):
            self.wait(self.near_sem[k], 2 * SHARD_ROWS)
            for stream in two_orders(self.group):
                columns = pl.ds(*stream[2])
                add_into(
                    self.block(stream, 0, k),
                    self.near.at[0, self.side, k % 4, :, columns],
                    self.near.at[1, self.side, k % 4, :, columns],
                )
                if k == 2:
                    for low, delta in ((0, 1), (HALF, -1)):
                        self.send(
                            self.block(stream, 0, 2, low, HALF),
                            self.last_far.at[self.side, pl.ds(low, HALF), columns],
                            stream[1],
                            delta,
                            self.last_far_sem,
                        )

    def pass_second(self):
        self.wait(self.last_far_sem, SHARD_ROWS)
        for stream in two_orders(self.group):
            columns = pl.ds(*stream[2])
            for way, (low, delta) in enumerate(((0, 1), (HALF, -1))):
                add_into(
                    self.block(stream, 0, delta, low, HALF),
                    self.last_far.at[self.side, pl.ds(low, HALF), columns],
                )
                self.send(
                    self.block(stream, 0, delta),
                    self.last_near.at[way, self.side, :, columns],
                    stream[1],
                    delta,
                    self.last_near_sem,
                )

    def finish(self):
        self.wait(self.last_near_sem, 2 * SHARD_ROWS)
        for stream in two_orders(self.group):
            columns = pl.ds(*stream[2])
            add_into(
                self.block(stream, 0, 0),
                self.last_near.at[0, self.side, :, columns],
                self.last_near.at[1, self.side, :, columns],
            )


class Reduce:
    def __init__(self, place, buffers, swapped, group):
        self.place, self.sums, self.group = place, buffers[0], group
        self.sent, self.swap_sem = place.send_sem(), place.recv_sem()
        self.own = ReduceSide(place, buffers, 0, group, self.sent)
        self.other = ReduceSide(place, buffers, 1, group, self.sent)
        self.swapped = swapped.at[:, pl.ds(*group)]

    def both(self, name):
        for side in (self.other, self.own):
            getattr(side, name)()

    def finish(self):
        place, cut = self.place, pl.ds(*self.group)
        z_at, y_at, x_at = place.at["z"], place.at["y"], place.at["x"]
        self.other.finish()
        partial = self.sums.at[place.rows(z_at, y_at, 1 - x_at), cut]
        place.send(partial, self.swapped, place.neighbour("x", 1), self.sent, self.swap_sem)
        self.own.finish()

    def total(self):
        place, cut = self.place, pl.ds(*self.group)
        place.arrived(self.swapped, self.swap_sem)
        mine = place.rows(place.at["z"], place.at["y"], place.at["x"])
        return self.sums[mine, cut].astype(jnp.float32) + self.swapped[...].astype(jnp.float32)

    def drain(self):
        rows = (DP - 1) * SHARD_ROWS
        self.place.left(self.sums.at[pl.ds(0, rows), pl.ds(*self.group)], self.sent)


SEQ = 512
ROWS = 128
CHIP_ROWS = 256
SCALE = HEAD_SIZE ** (-0.5)
GAINS = 2 * MODEL_WIDTH + 2 * HEAD_SIZE


def rows_at(index, size):
    if isinstance(index, int):
        return pl.ds(index * size, size)
    return pl.ds(pl.multiple_of(index * size, size), size)


class Quad:
    def __init__(self, place):
        self.place = place
        self.tensor = place.tensor
        self.core, self.chip = place.tensor % 2, place.tensor // 2
        self.partner = {"tensor": self.chip * 2 + 1 - self.core}
        self.across = {"tensor": (1 - self.chip) * 2 + self.core}
        self.own_rows = rows_at(self.tensor, ROWS)
        self.near_rows = rows_at(self.chip, CHIP_ROWS)
        self.far_rows = rows_at(1 - self.chip, CHIP_ROWS)


class QuadGather:
    def __init__(self, quad, full):
        self.quad, self.full, self.place = quad, full, quad.place
        self.sent, self.side = self.place.send_sem(), self.place.recv_sem()
        self.over = [self.place.recv_sem() for part in range(2)]
        self.on = self.place.recv_sem()

    def half(self, block, part):
        return self.full.at[pl.ds(pl.multiple_of(block * ROWS + part * 64, 64), 64)]

    def start(self):
        quad, place = self.quad, self.place
        for part in range(2):
            piece = self.half(quad.tensor, part)
            place.send(piece, piece, quad.across, self.sent, self.over[part])
        own = self.full.at[quad.own_rows]
        place.send(own, own, quad.partner, self.sent, self.side)

    def near(self):
        self.place.arrived(self.full.at[self.quad.own_rows], self.side)

    def forward(self):
        quad, place = self.quad, self.place
        far = (1 - quad.chip) * 2 + quad.core
        for part in range(2):
            piece = self.half(far, part)
            place.arrived(piece, self.over[part])
            place.send(piece, piece, quad.partner, self.sent, self.on)

    def finish(self):
        self.place.arrived(self.full.at[self.quad.own_rows], self.on)

    def drain(self):
        self.place.left(self.full.at[pl.ds(0, 3 * ROWS)], self.sent)


class QuadReduce:
    def __init__(self, quad, parts, chip_in, link_in):
        self.quad, self.parts, self.chip_in, self.link_in = quad, parts, chip_in, link_in
        self.place = quad.place
        far, near = 2 * (1 - quad.chip), 2 * quad.chip
        self.far_own, self.far_other = far + quad.core, far + 1 - quad.core
        self.near_other = near + 1 - quad.core
        self.sent, self.near_sem = self.place.send_sem(), self.place.recv_sem()
        self.far_sem = [self.place.recv_sem() for part in range(2)]
        self.link_sem = self.place.recv_sem()

    def piece(self, block, part):
        return self.parts.at[rows_at(block, ROWS), pl.ds(512 * part, 512)]

    def far_in(self, part):
        return self.chip_in.at[0, :, pl.ds(512 * part, 512)]

    def far_ready(self):
        for part in range(2):
            self.place.send(
                self.piece(self.far_other, part),
                self.far_in(part),
                self.quad.partner,
                self.sent,
                self.far_sem[part],
            )

    def near_ready(self):
        self.place.send(
            self.parts.at[rows_at(self.near_other, ROWS)],
            self.chip_in.at[1],
            self.quad.partner,
            self.sent,
            self.near_sem,
        )

    def link(self):
        for part in range(2):
            self.place.arrived(self.far_in(part), self.far_sem[part])
            piece = self.piece(self.far_own, part)
            add_into(piece, self.far_in(part))
            self.place.send(
                piece,
                self.link_in.at[:, pl.ds(512 * part, 512)],
                self.quad.across,
                self.sent,
                self.link_sem,
            )

    def total(self):
        self.place.arrived(self.chip_in.at[1], self.near_sem)
        self.place.arrived(self.link_in, self.link_sem)
        total = self.parts[self.quad.own_rows, :].astype(jnp.float32)
        total = total + self.chip_in[1].astype(jnp.float32)
        return total + self.link_in[...].astype(jnp.float32)

    def drain(self):
        self.place.left(self.parts.at[pl.ds(0, 3 * ROWS)], self.sent)


def turn_rows(source, target):
    for k in range(source.shape[1] // 128):
        target[128 * k : 128 * (k + 1), :] = source[:, 128 * k : 128 * (k + 1)].T


def rope(values, cos, sin):
    return values * cos + pltpu.roll(values, HEAD_SIZE // 2, 1) * sin


def rope_back(values, cos, sin):
    return values * cos + pltpu.roll(values * sin, HEAD_SIZE // 2, 1)


def orthogonalize(inbox, current, work, low_square, mixer, side):
    f32, bf16 = jnp.float32, jnp.bfloat16
    tiles = side // 256

    total = jnp.float32(0.0)
    for k in range(8):
        piece = inbox[4 * k : 4 * (k + 1), :, :side].reshape(4 * SHARD_ROWS, side).astype(f32)
        current[:side, 128 * k : 128 * (k + 1)] = piece.T
        total = total + jnp.sum(piece * piece)
    scale = 1.0 / (jnp.sqrt(total) + 1e-07)

    def narrow(slot):
        return work.at[pl.ds(0, side), pl.ds(pl.multiple_of(slot * MODEL_WIDTH, MODEL_WIDTH), MODEL_WIDTH)]

    energy = jnp.float32(0.0)
    for k in range(tiles):
        cut = slice(256 * k, 256 * (k + 1))
        piece = current[cut, :] * scale
        current[cut, :] = piece
        narrow(0)[cut, :] = piece.astype(bf16)
        energy = energy + jnp.sum(piece * piece)

    def newton(step, energy):
        now, later = narrow(step % 2), narrow((step + 1) % 2)
        shift = energy * (1.0 / side)
        linear = newton_two + 2.0 * newton_three * shift
        constant = newton_one + newton_two * shift + newton_three * shift * shift
        row = lax.broadcasted_iota(jnp.int32, (256, 256), 0)
        column = lax.broadcasted_iota(jnp.int32, (256, 256), 1)

        def put(target, k, part):
            cut = slice(256 * k, 256 * (k + 1))
            target[cut, 256 * k : side] = part
            for other in range(k + 1, tiles):
                block = part[:, 256 * (other - k) : 256 * (other - k + 1)]
                target[256 * other : 256 * (other + 1), cut] = block.T

        for k in range(tiles):
            part = lax.dot_general(
                now[256 * k : 256 * (k + 1), :],
                now[256 * k : side, :],
                contract_cols,
                preferred_element_type=f32,
            )
            first = jnp.where(row == column, part[:, :256] - shift, part[:, :256])
            if k < tiles - 1:
                part = jnp.concatenate([first, part[:, 256:]], axis=1)
            else:
                part = first
            put(low_square, k, part.astype(bf16))
        for k in range(tiles):
            cut = slice(256 * k, 256 * (k + 1))
            part = jnp.dot(
                low_square[cut, :side],
                low_square[:side, 256 * k : side],
                preferred_element_type=f32,
            )
            part = linear * low_square[cut, 256 * k : side].astype(f32) + newton_three * part
            put(mixer, k, part.astype(bf16))
        energy = jnp.float32(0.0)
        for k in range(tiles):
            cut = slice(256 * k, 256 * (k + 1))
            part = jnp.dot(mixer[cut, :side], now[...], preferred_element_type=f32)
            part = part + constant * current[cut, :]
            current[cut, :] = part
            later[cut, :] = part.astype(bf16)
            energy = energy + jnp.sum(part * part)
        return energy

    lax.fori_loop(0, NS_ITERS, newton, energy)
    for k in range(8):
        piece = current[:side, 128 * k : 128 * (k + 1)].T
        inbox[4 * k : 4 * (k + 1), :, :side] = piece.astype(bf16).reshape(4, SHARD_ROWS, side)


def layer_kernel(*refs):
    (
        x_in,
        positions_ref,
        cotangent_in,
        query_in,
        key_in,
        value_in,
        out_in,
        gate_in,
        up_in,
        down_in,
        query_moment_in,
        key_moment_in,
        value_moment_in,
        out_moment_in,
        gate_moment_in,
        up_moment_in,
        down_moment_in,
        gains_ref,
        gain_moment_ref,
        out_ref,
        grad_ref,
        moments_ref,
        weights_ref,
        gain_moment_out,
        gains_out,
        x_ref,
        cotangent_ref,
        shard,
        moments,
        weights,
        cos_ref,
        sin_ref,
        full,
        sums,
        far,
        near,
        last_far,
        last_near,
        swapped,
        normed,
        normed_two,
        cotangents,
        branch_grads,
        turned,
        query_raw,
        key_raw,
        query_rot,
        key_rot,
        value_low,
        key_turned,
        value_turned,
        probs,
        attention,
        attention_grad,
        hidden,
        ffn_grads,
        head_grads,
        key_sum,
        value_sum,
        hidden_one,
        input_grad,
        parts,
        chip_in,
        link_in,
        posted,
        inbox,
        current,
        settled,
        gain_parts,
        gain_tensor,
        gain_dp,
        send_sems,
        recv_sems,
        post_send,
        post_recv,
        back_send,
        back_recv,
        gain_sems,
        local_sems,
    ) = refs
    bf16, f32 = jnp.bfloat16, jnp.float32
    place = Place(send_sems, recv_sems)
    quad = Quad(place)
    dp, tensor = place.dp, place.tensor
    x_at = place.at["x"]

    shard_ins = (query_in, key_in, value_in, out_in, gate_in, up_in, down_in)
    moment_ins = (
        query_moment_in,
        key_moment_in,
        value_moment_in,
        out_moment_in,
        gate_moment_in,
        up_moment_in,
        down_moment_in,
    )
    cuts = [pl.ds(start, width) for start, width in zip(starts, widths)]
    shard_load, x_load, cotangent_load, moment_load = (local_sems.at[k] for k in range(4))
    out_store, grad_store, moment_store, weight_store = (local_sems.at[k] for k in range(4, 8))
    for source, cut in zip(shard_ins, cuts):
        pltpu.make_async_copy(source, shard.at[:, cut], shard_load).start()
    pltpu.make_async_copy(x_in, x_ref, x_load).start()
    pltpu.make_async_copy(cotangent_in, cotangent_ref, cotangent_load).start()
    for source, cut in zip(moment_ins, cuts):
        pltpu.make_async_copy(source, moments.at[:, cut], moment_load).start()

    def loaded(target, sem):
        pltpu.make_async_copy(target, target, sem).wait()

    barrier = pltpu.get_barrier_semaphore()

    def greet(k, carry):
        pl.semaphore_signal(
            barrier, inc=1, device_id={"dp": lax.rem(dp + k, DP)}, device_id_type=MESH
        )
        return carry

    lax.fori_loop(1, DP, greet, 0)
    for k in range(1, TENSOR):
        pl.semaphore_signal(
            barrier, inc=1, device_id={"tensor": lax.rem(tensor + k, TENSOR)}, device_id_type=MESH
        )
    loaded(shard, shard_load)
    mine = place.rows(place.at["z"], place.at["y"], x_at)
    full[mine, :] = shard[...]
    pl.semaphore_wait(barrier, DP - 1 + TENSOR - 1)

    gather_query, gather_out, gather_gate, gather_down = gathers = [
        Gather(place, full, group) for group in column_groups
    ]
    gather_query.swap()
    gather_query.own.begin()
    gather_out.swap()

    all_gains = gains_ref[...].reshape(1, GAINS)
    gain_attn = all_gains[:, :MODEL_WIDTH]
    gain_ffn = all_gains[:, MODEL_WIDTH : 2 * MODEL_WIDTH]
    gain_query = all_gains[:, 2 * MODEL_WIDTH : 2 * MODEL_WIDTH + HEAD_SIZE]
    gain_key = all_gains[:, 2 * MODEL_WIDTH + HEAD_SIZE :]
    loaded(x_ref, x_load)
    x = x_ref[...].astype(f32)
    first_scale = rms_scale(x)
    normed[quad.own_rows, :] = (x * first_scale * gain_attn).astype(bf16)
    gather_query.begin_other()
    gather_normed = QuadGather(quad, normed)
    gather_normed.start()
    gather_query.both("forward_first")
    gather_query.both("finish_first")
    gather_out.own.begin()
    gather_out.begin_other()
    gather_normed.forward()
    gather_query.both("forward_second")
    gather_gate.swap()
    gather_out.both("forward_first")
    gather_gate.own.begin()

    angle = jnp.broadcast_to(
        positions_ref[...].reshape(1, SEQ).astype(f32), (HEAD_SIZE, SEQ)
    ).T
    lane = lax.broadcasted_iota(jnp.int32, (1, HEAD_SIZE), 1)
    low_half = lane < HEAD_SIZE // 2
    step = jnp.where(low_half, lane, lane - HEAD_SIZE // 2).astype(f32)
    angle = angle * jnp.exp(step * (-2.0 * math.log(rope_base) / HEAD_SIZE))
    cos_ref[...] = jnp.cos(angle)
    sin = jnp.sin(angle)
    sin_ref[...] = jnp.where(low_half, -sin, sin)

    loaded(cotangent_ref, cotangent_load)
    cotangents[quad.own_rows, :] = cotangent_ref[...]
    gather_cotangent = QuadGather(quad, cotangents)
    gather_normed.near()
    gather_normed.finish()
    gather_out.both("finish_first")
    gather_query.both("finish_second")

    def project_query(k):
        pair = jnp.dot(normed[...], full[:, rows_at(k, 256)], preferred_element_type=f32)
        query_raw[:, rows_at(k, 256)] = pair
        for head in range(2):
            raw = pair[:, HEAD_SIZE * head : HEAD_SIZE * (head + 1)]
            rotated = rope(raw * rms_scale(raw) * gain_query, cos_ref[...], sin_ref[...])
            query_rot[:, rows_at(2 * k + head, HEAD_SIZE)] = rotated.astype(bf16)

    project_query(0)
    gather_gate.begin_other()
    gather_down.swap()
    project_query(1)
    gather_out.both("forward_second")
    pair = jnp.dot(normed[...], full[:, 512:768], preferred_element_type=f32)
    key_raw[...] = pair
    for head in range(2):
        raw = pair[:, HEAD_SIZE * head : HEAD_SIZE * (head + 1)]
        rotated = rope(raw * rms_scale(raw) * gain_key, cos_ref[...], sin_ref[...]).astype(bf16)
        key_rot[:, HEAD_SIZE * head : HEAD_SIZE * (head + 1)] = rotated
        key_turned[HEAD_SIZE * head : HEAD_SIZE * (head + 1), :] = rotated.T
    pair = jnp.dot(normed[...], full[:, 768:1024], preferred_element_type=f32).astype(bf16)
    value_low[...] = pair
    for head in range(2):
        value_turned[HEAD_SIZE * head : HEAD_SIZE * (head + 1), :] = pair[
            :, HEAD_SIZE * head : HEAD_SIZE * (head + 1)
        ].T
    turn_rows(normed, turned.at[1])
    gather_gate.both("forward_first")

    def attend(head):
        lanes, shared = rows_at(head, HEAD_SIZE), rows_at(head // 2, HEAD_SIZE)
        for block in range(2):
            keys, begin = 256 * (block + 1), 256 * block
            scores = lax.dot_general(
                key_rot[pl.ds(0, keys), shared],
                query_rot[pl.ds(begin, 256), lanes],
                contract_cols,
                preferred_element_type=f32,
            )
            row = lax.broadcasted_iota(jnp.int32, (keys, 256), 0)
            column = lax.broadcasted_iota(jnp.int32, (keys, 256), 1) + begin
            scores = jnp.where(row <= column, scores * SCALE, -1e30)
            shifted = jnp.exp(scores - jnp.max(scores, axis=0, keepdims=True))
            total = jnp.sum(shifted, axis=0, keepdims=True)
            low = (shifted * (1.0 / total)).astype(bf16)
            probs[head, pl.ds(0, keys), pl.ds(begin, 256)] = low
            mixed = jnp.dot(
                value_turned[shared, pl.ds(0, keys)], low, preferred_element_type=f32
            )
            attention[pl.ds(begin, 256), lanes] = mixed.T.astype(bf16)

    attend(0)
    gather_out.both("finish_second")
    attend(1)
    gather_gate.both("finish_first")
    gather_cotangent.start()
    attend(2)
    gather_down.own.begin()
    gather_down.begin_other()
    attend(3)
    gather_gate.both("forward_second")

    def project_back(source, start, width, target):
        def run(rows):
            for k in range(4):
                part = lax.dot_general(
                    source[rows, :],
                    full[256 * k : 256 * (k + 1), start : start + width],
                    contract_cols,
                    preferred_element_type=f32,
                )
                target[rows, 256 * k : 256 * (k + 1)] = part.astype(bf16)

        return run

    def reducer(k):
        return QuadReduce(quad, parts.at[k], chip_in.at[k], link_in.at[k])

    reduce_attn = reducer(0)
    out_rows = project_back(attention, 1024, 512, parts.at[0])
    out_rows(quad.far_rows)
    reduce_attn.far_ready()
    out_rows(quad.near_rows)
    reduce_attn.near_ready()
    reduce_attn.link()
    gather_down.both("forward_first")
    gather_cotangent.forward()
    gather_down.both("finish_first")
    x = x_ref[...].astype(f32)
    first_hidden = x + reduce_attn.total()
    hidden_one[...] = first_hidden
    normed_two[quad.own_rows, :] = (
        first_hidden * rms_scale(first_hidden) * gain_ffn
    ).astype(bf16)
    gather_two = QuadGather(quad, normed_two)
    gather_two.start()
    gather_down.both("forward_second")
    gather_cotangent.near()
    gather_cotangent.finish()
    turn_rows(cotangents, turned.at[0])
    gather_two.forward()
    gather_gate.both("finish_second")
    gather_down.both("finish_second")

    def feed(rows):
        for k in range(3):
            low = normed_two[rows, :]
            at = 256 * k
            gate = jnp.dot(low, full[:, 1536 + at : 1792 + at], preferred_element_type=f32)
            up = jnp.dot(low, full[:, 2304 + at : 2560 + at], preferred_element_type=f32)
            grad = jnp.dot(
                cotangents[rows, :], full[:, 3072 + at : 3328 + at], preferred_element_type=f32
            )
            sigmoid = 1.0 / (1.0 + jnp.exp(-gate))
            activated = gate * sigmoid
            hidden[rows, at : at + 256] = (activated * up).astype(bf16)
            ffn_grads[rows, at : at + 256] = (
                grad * up * (sigmoid * (1.0 + gate * (1.0 - sigmoid)))
            ).astype(bf16)
            ffn_grads[rows, 768 + at : 1024 + at] = (grad * activated).astype(bf16)

    reduce_two = reducer(1)
    two_rows = project_back(ffn_grads, 1536, 1536, parts.at[1])
    gather_two.near()
    feed(quad.near_rows)
    two_rows(quad.near_rows)
    reduce_two.near_ready()
    gather_two.finish()
    feed(quad.far_rows)
    two_rows(quad.far_rows)
    reduce_two.far_ready()

    def weight_grads(left, right, start, first, last):
        for k in range(first, last):
            part = jnp.dot(
                left[...], right[:, 256 * k : 256 * (k + 1)], preferred_element_type=f32
            )
            sums[:, start + 256 * k : start + 256 * (k + 1)] = part.astype(bf16)

    weight_grads(turned.at[0], hidden, 3072, 0, 2)
    reduce_two.link()
    weight_grads(turned.at[0], hidden, 3072, 2, 3)
    buffers = (sums, far, near, last_far, last_near)
    sum_query, sum_out, sum_gate, sum_down = all_sums = [
        Reduce(place, buffers, swapped, group) for group in column_groups
    ]
    sum_down.both("begin")
    turn_rows(normed_two, turned.at[0])
    weight_grads(turned.at[0], ffn_grads, 1536, 0, 4)

    normed_two_grad = reduce_two.total()
    first_hidden = hidden_one[...]
    second_scale = rms_scale(first_hidden)
    second_hat = first_hidden * second_scale
    gain_parts[:, MODEL_WIDTH : 2 * MODEL_WIDTH] = jnp.sum(
        normed_two_grad * second_hat, axis=0, keepdims=True
    )
    hidden_one_grad = cotangent_ref[...].astype(f32) + norm_backward(
        normed_two_grad * gain_ffn, second_hat, second_scale
    )
    input_grad[...] = hidden_one_grad
    branch_grads[quad.own_rows, :] = hidden_one_grad.astype(bf16)
    gather_branch = QuadGather(quad, branch_grads)
    gather_branch.start()
    weight_grads(turned.at[0], ffn_grads, 1536, 4, 6)
    sum_gate.both("begin")

    reduce_ffn = reducer(2)
    down_rows = project_back(hidden, 3072, 768, parts.at[2])
    gather_branch.forward()
    sum_down.both("pass_first")
    down_rows(quad.far_rows)
    reduce_ffn.far_ready()

    def attend_grad(rows):
        part = jnp.dot(branch_grads[rows, :], full[:, 1024:1536], preferred_element_type=f32)
        attention_grad[rows, :] = part.astype(bf16)

    gather_branch.near()
    attend_grad(quad.near_rows)
    gather_branch.finish()
    attend_grad(quad.far_rows)
    reduce_ffn.link()
    turn_rows(branch_grads, turned.at[0])
    weight_grads(turned.at[0], attention, 1024, 0, 2)
    sum_out.both("begin")

    def head_norm_back(rotated_grad, raw, gain, rows):
        scale = rms_scale(raw)
        hat = raw * scale
        norm_grad = rope_back(rotated_grad, cos_ref[rows, :], sin_ref[rows, :])
        gain_grad = jnp.sum(norm_grad * hat, axis=0, keepdims=True)
        return norm_backward(norm_grad * gain, hat, scale).astype(bf16), gain_grad

    def attend_back(head, gain_sum):
        lanes, shared = rows_at(head, HEAD_SIZE), rows_at(head // 2, HEAD_SIZE)
        for block in (1, 0):
            keys, begin = 256 * (block + 1), 256 * block
            key_cut, query_cut = pl.ds(0, keys), pl.ds(begin, 256)
            mixed_grad = attention_grad[query_cut, lanes]
            low = probs[head, key_cut, query_cut]
            wide = low.astype(f32)
            probs_grad = lax.dot_general(
                value_low[key_cut, shared],
                mixed_grad,
                contract_cols,
                preferred_element_type=f32,
            )
            inner_sum = jnp.sum(wide * probs_grad, axis=0, keepdims=True)
            score_grad = (wide * (probs_grad - inner_sum)).astype(bf16)
            value_part = jnp.dot(low, mixed_grad, preferred_element_type=f32)
            key_part = jnp.dot(
                score_grad, query_rot[query_cut, lanes], preferred_element_type=f32
            )
            if head % 2 == 0 and block == 1:
                value_sum[:, shared] = value_part
                key_sum[:, shared] = key_part
            else:
                value_sum[key_cut, shared] += value_part
                key_sum[key_cut, shared] += key_part
            query_part = jnp.dot(
                key_turned[shared, key_cut], score_grad, preferred_element_type=f32
            )
            grad, gain_part = head_norm_back(
                query_part.T * SCALE, query_raw[query_cut, lanes], gain_query, query_cut
            )
            head_grads[query_cut, lanes] = grad
            gain_sum = gain_sum + gain_part
        return gain_sum

    def shared_back(head, gain_sum):
        shared = rows_at(head, HEAD_SIZE)
        grad, gain_part = head_norm_back(
            key_sum[:, shared] * SCALE, key_raw[:, shared], gain_key, pl.ds(0, SEQ)
        )
        head_grads[:, rows_at(4 + head, HEAD_SIZE)] = grad
        head_grads[:, rows_at(6 + head, HEAD_SIZE)] = value_sum[:, shared].astype(bf16)
        return gain_sum + gain_part

    none = jnp.zeros((1, HEAD_SIZE), f32)
    query_gain_sum = attend_back(0, none)
    sum_gate.other.pass_first()
    query_gain_sum = attend_back(1, query_gain_sum)
    key_gain_sum = shared_back(0, none)
    sum_gate.own.pass_first()
    sum_down.both("begin_second")
    query_gain_sum = attend_back(2, query_gain_sum)
    sum_out.both("pass_first")
    sum_gate.other.begin_second()
    query_gain_sum = attend_back(3, query_gain_sum)
    key_gain_sum = shared_back(1, key_gain_sum)
    gain_parts[:, 2 * MODEL_WIDTH : 2 * MODEL_WIDTH + HEAD_SIZE] = query_gain_sum
    gain_parts[:, 2 * MODEL_WIDTH + HEAD_SIZE :] = key_gain_sum
    sum_down.both("pass_second")
    weight_grads(turned.at[1], head_grads, 0, 0, 2)
    sum_gate.own.begin_second()
    sum_gate.other.pass_second()
    weight_grads(turned.at[1], head_grads, 0, 2, 4)
    sum_query.both("begin")
    sum_out.both("begin_second")
    sum_down.finish()

    reduce_one = reducer(3)
    one_rows = project_back(head_grads, 0, 1024, parts.at[3])
    one_rows(quad.far_rows)
    reduce_one.far_ready()
    sum_gate.own.pass_second()
    sum_out.both("pass_second")
    one_rows(quad.near_rows)
    reduce_one.near_ready()
    reduce_one.link()
    sum_query.other.pass_first()
    down_rows(quad.near_rows)
    reduce_ffn.near_ready()
    sum_query.own.pass_first()
    sum_gate.finish()
    sum_out.finish()

    loaded(moments, moment_load)
    core = tensor % 2
    owner = [even + core * (odd - even) for even, odd in owners]

    def post_copy(slot):
        return pltpu.make_async_remote_copy(
            src_ref=posted.at[:, cuts[slot]],
            dst_ref=inbox.at[dp, :, pl.ds(0, widths[slot])],
            send_sem=post_send.at[slot],
            recv_sem=post_recv.at[0],
            device_id={"dp": owner[slot]},
            device_id_type=MESH,
        )

    def update(group):
        start, width = column_groups[group]
        cut = pl.ds(start, width)
        fresh = moment_decay * moments[:, cut] + all_sums[group].total()
        moments[:, cut] = fresh
        posted[:, cut] = fresh.astype(bf16)
        pltpu.make_async_copy(moments.at[:, cut], moments_ref.at[:, cut], moment_store).start()
        for slot in group_slots[group]:

            @pl.when(dp != owner[slot])
            def _():
                post_copy(slot).start()

            @pl.when(dp == owner[slot])
            def _():
                inbox[dp, :, : widths[slot]] = posted[:, cuts[slot]]
                if widths[slot] < 512:
                    inbox[:, :, widths[slot] : 512] = jnp.zeros(
                        (DP, SHARD_ROWS, 512 - widths[slot]), bf16
                    )

    update(3)
    sum_query.other.begin_second()
    update(2)

    hidden_one[...] = hidden_one[...] + reduce_ffn.total()
    pltpu.make_async_copy(hidden_one, out_ref, out_store).start()
    sum_query.own.begin_second()
    sum_query.other.pass_second()
    update(1)
    normed_grad = reduce_one.total()
    x = x_ref[...].astype(f32)
    first_scale = rms_scale(x)
    first_hat = x * first_scale
    gain_parts[:, :MODEL_WIDTH] = jnp.sum(normed_grad * first_hat, axis=0, keepdims=True)
    input_grad[...] = input_grad[...] + norm_backward(
        normed_grad * gain_attn, first_hat, first_scale
    )
    pltpu.make_async_copy(input_grad, grad_ref, grad_store).start()
    sum_query.own.pass_second()
    sum_query.finish()

    gain_tensor[tensor] = gain_parts[...]
    for k in range(1, TENSOR):
        place.send(
            gain_parts,
            gain_tensor.at[tensor],
            {"tensor": lax.rem(tensor + k, TENSOR)},
            gain_sems.at[0],
            gain_sems.at[1],
        )
    update(0)

    for group in gathers + all_sums:
        group.drain()
    for exchange in (gather_normed, gather_cotangent, gather_two, gather_branch):
        exchange.drain()
    for exchange in (reduce_attn, reduce_two, reduce_ffn, reduce_one):
        exchange.drain()

    place.arrived(gain_tensor.at[pl.ds(0, TENSOR - 1)], gain_sems.at[1])
    gain_dp[dp] = gain_tensor[0] + gain_tensor[1] + gain_tensor[2] + gain_tensor[3]

    def gain_start(k, carry):
        place.send(
            gain_dp.at[dp],
            gain_dp.at[dp],
            {"dp": lax.rem(dp + k, DP)},
            gain_sems.at[2],
            gain_sems.at[3],
        )
        return carry

    lax.fori_loop(1, DP, gain_start, 0)

    for slot in (4, 5, 6, 3, 0, 1, 2):

        @pl.when(dp == owner[slot])
        def _():
            place.arrived(inbox.at[pl.ds(0, DP - 1), :, pl.ds(0, widths[slot])], post_recv.at[0])

    work = full.at[:, pl.ds(0, 2 * MODEL_WIDTH)]
    low_square = full.at[:WIDEST, pl.ds(2048, WIDEST)]
    mixer = full.at[:WIDEST, pl.ds(2816, WIDEST)]
    wide = (dp == owner[4]) | (dp == owner[5]) | (dp == owner[6])
    slim = (dp == owner[0]) | (dp == owner[1]) | (dp == owner[2]) | (dp == owner[3])

    @pl.when(wide)
    def _():
        orthogonalize(inbox, current, work, low_square, mixer, WIDEST)

    @pl.when(slim)
    def _():
        orthogonalize(inbox, current, work, low_square, mixer, 512)

    def back(slot, k):
        target = lax.rem(dp + k, DP)
        return pltpu.make_async_remote_copy(
            src_ref=inbox.at[target, :, pl.ds(0, widths[slot])],
            dst_ref=settled.at[:, cuts[slot]],
            send_sem=back_send.at[0],
            recv_sem=back_recv.at[slot],
            device_id={"dp": target},
            device_id_type=MESH,
        )

    for slot in range(7):

        @pl.when(dp == owner[slot])
        def _():
            def back_start(k, carry):
                back(slot, k).start()
                return carry

            lax.fori_loop(1, DP, back_start, 0)
            settled[:, cuts[slot]] = inbox[dp, :, : widths[slot]]

    place.arrived(gain_dp.at[pl.ds(0, DP - 1)], gain_sems.at[3])

    def gain_add(k, carry):
        return carry + gain_dp[k]

    gain_total = lax.fori_loop(1, DP, gain_add, gain_dp[0]).reshape(GAINS)
    fresh_gain = gain_decay * gain_moment_ref[...] + gain_total
    gain_moment_out[...] = fresh_gain
    gains_out[...] = gains_ref[...] - gain_rate / math.sqrt(SEQ * DP) * fresh_gain

    for slot in (1, 2, 0, 3, 4, 5, 6):

        @pl.when(dp != owner[slot])
        def _():
            place.arrived(settled.at[:, cuts[slot]], back_recv.at[slot])

        cut = cuts[slot]
        weights[:, cut] = shard[:, cut].astype(f32) - rates[slot] * settled[:, cut].astype(f32)
        pltpu.make_async_copy(weights.at[:, cut], weights_ref.at[:, cut], weight_store).start()

    place.left(gain_tensor.at[pl.ds(0, TENSOR - 1)], gain_sems.at[0])
    place.left(gain_dp.at[pl.ds(0, DP - 1)], gain_sems.at[2])
    for slot in range(7):

        @pl.when(dp != owner[slot])
        def _():
            post_copy(slot).wait_send()

        @pl.when(dp == owner[slot])
        def _():
            place.left(inbox.at[pl.ds(0, DP - 1), :, pl.ds(0, widths[slot])], back_send.at[0])

    loaded(hidden_one, out_store)
    loaded(input_grad, grad_store)
    loaded(moments, moment_store)
    loaded(weights, weight_store)


def run_layer(args):
    bf16, f32 = jnp.bfloat16, jnp.float32
    shard_shape = (SHARD_ROWS, COLUMNS)
    dma = pltpu.SemaphoreType.DMA
    in_specs = [ANY] * 19
    in_specs[1] = in_specs[17] = in_specs[18] = VMEM
    return pl.pallas_call(
        layer_kernel,
        out_shape=(
            jax.ShapeDtypeStruct((ROWS, MODEL_WIDTH), f32),
            jax.ShapeDtypeStruct((ROWS, MODEL_WIDTH), f32),
            jax.ShapeDtypeStruct(shard_shape, f32),
            jax.ShapeDtypeStruct(shard_shape, f32),
            jax.ShapeDtypeStruct((GAINS,), f32),
            jax.ShapeDtypeStruct((GAINS,), f32),
        ),
        in_specs=in_specs,
        out_specs=(ANY, ANY, ANY, ANY, VMEM, VMEM),
        scratch_shapes=[
            pltpu.VMEM((ROWS, MODEL_WIDTH), bf16),
            pltpu.VMEM((ROWS, MODEL_WIDTH), bf16),
            pltpu.VMEM(shard_shape, bf16),
            pltpu.VMEM(shard_shape, f32),
            pltpu.VMEM(shard_shape, f32),
            pltpu.VMEM((SEQ, HEAD_SIZE), f32),
            pltpu.VMEM((SEQ, HEAD_SIZE), f32),
            pltpu.VMEM((MODEL_WIDTH, COLUMNS), bf16),
            pltpu.VMEM((MODEL_WIDTH, COLUMNS), bf16),
            pltpu.VMEM((2, 4, SHARD_ROWS, COLUMNS), bf16),
            pltpu.VMEM((2, 2, 4, SHARD_ROWS, COLUMNS), bf16),
            pltpu.VMEM((2, SHARD_ROWS, COLUMNS), bf16),
            pltpu.VMEM((2, 2, SHARD_ROWS, COLUMNS), bf16),
            pltpu.VMEM(shard_shape, bf16),
            pltpu.VMEM((SEQ, MODEL_WIDTH), bf16),
            pltpu.VMEM((SEQ, MODEL_WIDTH), bf16),
            pltpu.VMEM((SEQ, MODEL_WIDTH), bf16),
            pltpu.VMEM((SEQ, MODEL_WIDTH), bf16),
            pltpu.VMEM((2, MODEL_WIDTH, SEQ), bf16),
            pltpu.VMEM((SEQ, 512), f32),
            pltpu.VMEM((SEQ, 256), f32),
            pltpu.VMEM((SEQ, 512), bf16),
            pltpu.VMEM((SEQ, 256), bf16),
            pltpu.VMEM((SEQ, 256), bf16),
            pltpu.VMEM((256, SEQ), bf16),
            pltpu.VMEM((256, SEQ), bf16),
            pltpu.VMEM((4, SEQ, SEQ), bf16),
            pltpu.VMEM((SEQ, 512), bf16),
            pltpu.VMEM((SEQ, 512), bf16),
            pltpu.VMEM((SEQ, 768), bf16),
            pltpu.VMEM((SEQ, 1536), bf16),
            pltpu.VMEM((SEQ, 1024), bf16),
            pltpu.VMEM((SEQ, 256), f32),
            pltpu.VMEM((SEQ, 256), f32),
            pltpu.VMEM((ROWS, MODEL_WIDTH), f32),
            pltpu.VMEM((ROWS, MODEL_WIDTH), f32),
            pltpu.VMEM((4, SEQ, MODEL_WIDTH), bf16),
            pltpu.VMEM((4, 2, ROWS, MODEL_WIDTH), bf16),
            pltpu.VMEM((4, ROWS, MODEL_WIDTH), bf16),
            pltpu.VMEM(shard_shape, bf16),
            pltpu.VMEM((DP, SHARD_ROWS, WIDEST), bf16),
            pltpu.VMEM((WIDEST, MODEL_WIDTH), f32),
            pltpu.VMEM(shard_shape, bf16),
            pltpu.VMEM((1, GAINS), f32),
            pltpu.VMEM((TENSOR, 1, GAINS), f32),
            pltpu.VMEM((DP, 1, GAINS), f32),
            dma((16,)),
            dma((176,)),
            dma((7,)),
            dma((1,)),
            dma((1,)),
            dma((7,)),
            dma((4,)),
            dma((8,)),
        ],
        compiler_params=pltpu.CompilerParams(
            collective_id=0, has_side_effects=True, vmem_limit_bytes=62 << 20
        ),
        name="layer",
    )(*args)


def unpack_kernel(*refs):
    sources, targets = refs[:6], refs[6:]
    out, grad, moments, weights, gain_moment, gains = sources
    targets[0][...] = out[...]
    targets[1][...] = grad[...]
    for slot in range(7):
        cut = pl.ds(starts[slot], widths[slot])
        targets[2 + slot][...] = moments[:, cut]
        targets[9 + slot][...] = weights[:, cut]
    targets[16][...] = gain_moment[...]
    targets[17][...] = gains[...]


def unpack(results):
    f32 = jnp.float32
    pieces = [jax.ShapeDtypeStruct((SHARD_ROWS, width), f32) for width in widths]
    shapes = [jax.ShapeDtypeStruct((ROWS, MODEL_WIDTH), f32)] * 2
    shapes += pieces + pieces + [jax.ShapeDtypeStruct((GAINS,), f32)] * 2
    return pl.pallas_call(
        unpack_kernel,
        out_shape=tuple(shapes),
        in_specs=[VMEM] * 6,
        out_specs=(VMEM,) * 18,
        name="unpack",
    )(*results)


def body(*args):
    args = list(args)
    for index in (6, 9, 13, 16):
        args[index] = args[index].T
    results = list(unpack(run_layer(args)))
    for index in (5, 8, 12, 15):
        results[index] = results[index].T
    return tuple(results)


def solution(mesh):
    placed = (
        P(("dp", "tensor"), None),
        P("dp"),
        P(("dp", "tensor"), None),
        P("dp", "tensor"),
        P("dp", "tensor"),
        P("dp", "tensor"),
        P("tensor", "dp"),
        P("dp", "tensor"),
        P("dp", "tensor"),
        P("tensor", "dp"),
        P("dp", "tensor"),
        P("dp", "tensor"),
        P("dp", "tensor"),
        P("tensor", "dp"),
        P("dp", "tensor"),
        P("dp", "tensor"),
        P("tensor", "dp"),
        P(),
        P(),
    )
    return jax.shard_map(
        body,
        mesh=mesh,
        in_specs=placed,
        out_specs=(
            P(("dp", "tensor"), None),
            P(("dp", "tensor"), None),
            P("dp", "tensor"),
            P("dp", "tensor"),
            P("dp", "tensor"),
            P("tensor", "dp"),
            P("dp", "tensor"),
            P("dp", "tensor"),
            P("tensor", "dp"),
            P("dp", "tensor"),
            P("dp", "tensor"),
            P("dp", "tensor"),
            P("tensor", "dp"),
            P("dp", "tensor"),
            P("dp", "tensor"),
            P("tensor", "dp"),
            P(),
            P(),
        ),
        check_vma=False,
    )
```

```python
import functools
import math

import jax
import jax.numpy as jnp
from jax import lax
from jax.experimental import pallas as pl
from jax.experimental.pallas import tpu as pltpu
from jax.sharding import PartitionSpec as P

MODEL_WIDTH = 1024
HEAD_SIZE = 128
NS_ITERS = 5


epsilon = 1e-06
moment_decay = 0.95
gain_decay = 0.9
gain_rate = 0.3
rope_base = 1000000.0
newton_one = 3.4445
newton_two = -4.775
newton_three = 2.0315
contract_rows = (((0,), (0,)), ((), ()))
contract_cols = (((1,), (1,)), ((), ()))


def rms_scale(values):
    return lax.rsqrt(jnp.mean(values * values, axis=-1, keepdims=True) + epsilon)


def norm_backward(gradient_value, normalized_input, scale_value):
    return scale_value * (
        gradient_value
        - normalized_input * jnp.mean(gradient_value * normalized_input, axis=-1, keepdims=True)
    )


COLUMNS = 3840
widths = (512, 256, 256, 512, 768, 768, 768)
pieces = (
    ((0, 256, 0), (512, 256, 256)),
    ((256, 128, 0), (768, 128, 128)),
    ((384, 128, 0), (896, 128, 128)),
    ((1024, 512, 0),),
    ((1536, 768, 0),),
    ((2304, 768, 0),),
    ((3072, 768, 0),),
)
owners = ((8, 26), (6, 17), (28, 3), (25, 14), (0, 31), (13, 5), (18, 23))
rates = (1.0, 1.0, 1.0, math.sqrt(8.0), 1.0, 1.0, math.sqrt(4.0 / 3.0))
column_groups = ((0, 512), (512, 512), (1024, 512), (1536, 1536), (3072, 768))
classes = ((4, 5, 6), (0, 3), (1, 2))
DP = 32
TENSOR = 4
SHARD_ROWS = 32
HALF = SHARD_ROWS // 2
WIDEST = 768
MESH = pl.DeviceIdType.MESH
ANY = pl.BlockSpec(memory_space=pl.ANY)
VMEM = pl.BlockSpec(memory_space=pltpu.VMEM)


class Place:
    def __init__(self, send_sems, recv_sems):
        self.send_sems, self.recv_sems = send_sems, recv_sems
        self.sends, self.recvs = 0, 0
        self.dp = lax.axis_index("dp")
        self.tensor = lax.axis_index("tensor")
        self.at = {"z": self.dp // 8, "y": (self.dp // 2) % 4, "x": self.dp % 2}

    def send_sem(self):
        self.sends += 1
        return self.send_sems.at[self.sends - 1]

    def recv_sem(self):
        self.recvs += 1
        return self.recv_sems.at[self.recvs - 1]

    def step(self, axis, delta):
        size = 2 if axis == "x" else 4
        return lax.rem(self.at[axis] + size + delta, size)

    def neighbour(self, axis, delta):
        at = dict(self.at)
        at[axis] = self.step(axis, delta)
        return {"dp": at["z"] * 8 + at["y"] * 2 + at["x"]}

    def block(self, axis, delta, other, other_delta):
        first, second = self.step(axis, delta), self.step(other, other_delta)
        return (first, second) if axis == "z" else (second, first)

    def rows(self, z_at, y_at, x_at, low=0, rows=SHARD_ROWS):
        begin = (z_at * 8 + y_at * 2 + x_at) * SHARD_ROWS + low
        return pl.ds(pl.multiple_of(begin, 16), rows)

    def copy(self, source, target, device, sent, received):
        return pltpu.make_async_remote_copy(
            src_ref=source,
            dst_ref=target,
            send_sem=sent,
            recv_sem=received,
            device_id=device,
            device_id_type=MESH,
        )

    def send(self, source, target, device, sent, received):
        self.copy(source, target, device, sent, received).start()

    def arrived(self, like, received):
        self.copy(like, like, self.neighbour("x", 1), received, received).wait_recv()

    def left(self, like, sent):
        self.copy(like, like, self.neighbour("x", 1), sent, sent).wait_send()


def two_orders(group):
    start, width = group
    half = width // 2
    return (("z", "y", (start, half)), ("y", "z", (start + half, half)))


class GatherSide:
    def __init__(self, place, full, x_at, group, sent):
        self.place, self.full, self.x_at, self.group, self.sent = place, full, x_at, group, sent
        self.direct, self.passed = place.recv_sem(), place.recv_sem()
        self.along = {k: place.recv_sem() for k in (0, -1, 1, 2)}
        self.last = place.recv_sem()

    def send(self, stream, first_delta, second_delta, low, rows, axis, delta, received):
        first, second, columns = stream
        z_at, y_at = self.place.block(first, first_delta, second, second_delta)
        ref = self.full.at[self.place.rows(z_at, y_at, self.x_at, low, rows), pl.ds(*columns)]
        self.place.send(ref, ref, self.place.neighbour(axis, delta), self.sent, received)

    def wait(self, received, rows):
        self.place.arrived(self.full.at[pl.ds(0, rows), pl.ds(*self.group)], received)

    def spread(self, first_delta):
        for stream in two_orders(self.group):
            for delta in (1, -1):
                self.send(
                    stream, first_delta, 0, 0, SHARD_ROWS, stream[1], delta, self.along[first_delta]
                )

    def begin(self):
        for stream in two_orders(self.group):
            for delta in (1, -1):
                self.send(stream, 0, 0, 0, SHARD_ROWS, stream[0], delta, self.direct)
        self.spread(0)

    def forward_first(self):
        self.wait(self.direct, 2 * SHARD_ROWS)
        for stream in two_orders(self.group):
            self.send(stream, -1, 0, 0, HALF, stream[0], 1, self.passed)
            self.send(stream, 1, 0, HALF, HALF, stream[0], -1, self.passed)
        self.spread(-1)
        self.spread(1)

    def finish_first(self):
        self.wait(self.passed, SHARD_ROWS)
        self.spread(2)

    def forward_second(self):
        for first_delta in (0, -1, 1, 2):
            self.wait(self.along[first_delta], 2 * SHARD_ROWS)
            for stream in two_orders(self.group):
                self.send(stream, first_delta, -1, 0, HALF, stream[1], 1, self.last)
                self.send(stream, first_delta, 1, HALF, HALF, stream[1], -1, self.last)

    def finish_second(self):
        self.wait(self.last, 4 * SHARD_ROWS)


class Gather:
    def __init__(self, place, full, group):
        self.place, self.full, self.group = place, full, group
        self.sent, self.swapped = place.send_sem(), place.recv_sem()
        x_at = place.at["x"]
        self.own = GatherSide(place, full, x_at, group, self.sent)
        self.other = GatherSide(place, full, 1 - x_at, group, self.sent)
        self.mine = full.at[place.rows(place.at["z"], place.at["y"], x_at), pl.ds(*group)]

    def swap(self):
        self.place.send(
            self.mine, self.mine, self.place.neighbour("x", 1), self.sent, self.swapped
        )

    def begin_other(self):
        self.place.arrived(self.mine, self.swapped)
        self.other.begin()

    def both(self, name):
        for side in (self.own, self.other):
            getattr(side, name)()

    def drain(self):
        rows = (DP - 1) * SHARD_ROWS
        self.place.left(self.full.at[pl.ds(0, rows), pl.ds(*self.group)], self.sent)


def add_into(target, *terms):
    total = target[...].astype(jnp.float32)
    for term in terms:
        total = total + term[...].astype(jnp.float32)
    target[...] = total.astype(target.dtype)


class ReduceSide:
    def __init__(self, place, buffers, side, group, sent):
        self.place, self.side, self.group, self.sent = place, side, group, sent
        self.sums, self.far, self.near, self.last_far, self.last_near = buffers
        self.x_at = place.at["x"] if side == 0 else 1 - place.at["x"]
        self.far_sem = {k: place.recv_sem() for k in (0, -1, 1, 2)}
        self.near_sem = {k: place.recv_sem() for k in (0, -1, 1, 2)}
        self.last_far_sem, self.last_near_sem = place.recv_sem(), place.recv_sem()

    def block(self, stream, first_delta, second_delta, low=0, rows=SHARD_ROWS):
        first, second, columns = stream
        z_at, y_at = self.place.block(first, first_delta, second, second_delta)
        return self.sums.at[self.place.rows(z_at, y_at, self.x_at, low, rows), pl.ds(*columns)]

    def send(self, source, target, axis, delta, received):
        self.place.send(source, target, self.place.neighbour(axis, delta), self.sent, received)

    def wait(self, received, rows):
        self.place.arrived(self.sums.at[pl.ds(0, rows), pl.ds(*self.group)], received)

    def begin(self):
        for k in (2, 1, -1, 0):
            for stream in two_orders(self.group):
                far = self.far.at[self.side, k % 4, :, pl.ds(*stream[2])]
                for low, delta in ((0, 1), (HALF, -1)):
                    self.send(
                        self.block(stream, 2, k, low, HALF),
                        far.at[pl.ds(low, HALF)],
                        stream[0],
                        delta,
                        self.far_sem[k],
                    )

    def pass_first(self):
        for k in (2, 1, -1, 0):
            self.wait(self.far_sem[k], SHARD_ROWS)
            for stream in two_orders(self.group):
                far = self.far.at[self.side, k % 4, :, pl.ds(*stream[2])]
                for way, (low, delta) in enumerate(((0, 1), (HALF, -1))):
                    add_into(self.block(stream, delta, k, low, HALF), far.at[pl.ds(low, HALF)])
                    self.send(
                        self.block(stream, delta, k),
                        self.near.at[way, self.side, k % 4, :, pl.ds(*stream[2])],
                        stream[0],
                        delta,
                        self.near_sem[k],
                    )

    def begin_second(self):
        for k in (2, 1, -1, 0):
            self.wait(self.near_sem[k], 2 * SHARD_ROWS)
            for stream in two_orders(self.group):
                columns = pl.ds(*stream[2])
                add_into(
                    self.block(stream, 0, k),
                    self.near.at[0, self.side, k % 4, :, columns],
                    self.near.at[1, self.side, k % 4, :, columns],
                )
                if k == 2:
                    for low, delta in ((0, 1), (HALF, -1)):
                        self.send(
                            self.block(stream, 0, 2, low, HALF),
                            self.last_far.at[self.side, pl.ds(low, HALF), columns],
                            stream[1],
                            delta,
                            self.last_far_sem,
                        )

    def pass_second(self):
        self.wait(self.last_far_sem, SHARD_ROWS)
        for stream in two_orders(self.group):
            columns = pl.ds(*stream[2])
            for way, (low, delta) in enumerate(((0, 1), (HALF, -1))):
                add_into(
                    self.block(stream, 0, delta, low, HALF),
                    self.last_far.at[self.side, pl.ds(low, HALF), columns],
                )
                self.send(
                    self.block(stream, 0, delta),
                    self.last_near.at[way, self.side, :, columns],
                    stream[1],
                    delta,
                    self.last_near_sem,
                )

    def finish(self):
        self.wait(self.last_near_sem, 2 * SHARD_ROWS)
        for stream in two_orders(self.group):
            columns = pl.ds(*stream[2])
            add_into(
                self.block(stream, 0, 0),
                self.last_near.at[0, self.side, :, columns],
                self.last_near.at[1, self.side, :, columns],
            )


class Reduce:
    def __init__(self, place, buffers, swapped, group):
        self.place, self.sums, self.group = place, buffers[0], group
        self.sent, self.swap_sem = place.send_sem(), place.recv_sem()
        self.own = ReduceSide(place, buffers, 0, group, self.sent)
        self.other = ReduceSide(place, buffers, 1, group, self.sent)
        self.swapped = swapped.at[:, pl.ds(*group)]

    def both(self, name):
        for side in (self.other, self.own):
            getattr(side, name)()

    def finish(self):
        place, cut = self.place, pl.ds(*self.group)
        z_at, y_at, x_at = place.at["z"], place.at["y"], place.at["x"]
        self.other.finish()
        partial = self.sums.at[place.rows(z_at, y_at, 1 - x_at), cut]
        place.send(partial, self.swapped, place.neighbour("x", 1), self.sent, self.swap_sem)
        self.own.finish()

    def total(self):
        place, cut = self.place, pl.ds(*self.group)
        place.arrived(self.swapped, self.swap_sem)
        mine = place.rows(place.at["z"], place.at["y"], place.at["x"])
        return self.sums[mine, cut].astype(jnp.float32) + self.swapped[...].astype(jnp.float32)

    def drain(self):
        rows = (DP - 1) * SHARD_ROWS
        self.place.left(self.sums.at[pl.ds(0, rows), pl.ds(*self.group)], self.sent)


SEQ = 512
ROWS = 128
CHIP_ROWS = 256
SCALE = HEAD_SIZE ** (-0.5)
GAINS = 2 * MODEL_WIDTH + 2 * HEAD_SIZE


def rows_at(index, size):
    if isinstance(index, int):
        return pl.ds(index * size, size)
    return pl.ds(pl.multiple_of(index * size, size), size)


class Quad:
    def __init__(self, place):
        self.place = place
        self.tensor = place.tensor
        self.core, self.chip = place.tensor % 2, place.tensor // 2
        self.partner = {"tensor": self.chip * 2 + 1 - self.core}
        self.across = {"tensor": (1 - self.chip) * 2 + self.core}
        self.own_rows = rows_at(self.tensor, ROWS)
        self.near_rows = rows_at(self.chip, CHIP_ROWS)
        self.far_rows = rows_at(1 - self.chip, CHIP_ROWS)


class QuadGather:
    def __init__(self, quad, full):
        self.quad, self.full, self.place = quad, full, quad.place
        self.sent, self.side = self.place.send_sem(), self.place.recv_sem()
        self.over = [self.place.recv_sem() for part in range(2)]
        self.on = self.place.recv_sem()

    def half(self, block, part):
        return self.full.at[pl.ds(pl.multiple_of(block * ROWS + part * 64, 64), 64)]

    def start(self, *which):
        quad, place = self.quad, self.place
        for part in which or range(2):
            piece = self.half(quad.tensor, part)
            place.send(piece, piece, quad.across, self.sent, self.over[part])
            place.send(piece, piece, quad.partner, self.sent, self.side)

    def near(self):
        self.place.arrived(self.full.at[self.quad.own_rows], self.side)

    def forward(self, *which):
        quad, place = self.quad, self.place
        far = (1 - quad.chip) * 2 + quad.core
        for part in which or range(2):
            piece = self.half(far, part)
            place.arrived(piece, self.over[part])
            place.send(piece, piece, quad.partner, self.sent, self.on)

    def finish(self):
        self.place.arrived(self.full.at[self.quad.own_rows], self.on)

    def drain(self):
        self.place.left(self.full.at[pl.ds(0, 3 * ROWS)], self.sent)


class QuadReduce:
    def __init__(self, quad, parts, chip_in, link_in):
        self.quad, self.parts, self.chip_in, self.link_in = quad, parts, chip_in, link_in
        self.place = quad.place
        far, near = 2 * (1 - quad.chip), 2 * quad.chip
        self.far_own, self.far_other = far + quad.core, far + 1 - quad.core
        self.near_other = near + 1 - quad.core
        self.sent, self.near_sem = self.place.send_sem(), self.place.recv_sem()
        self.far_sem = [self.place.recv_sem() for part in range(2)]
        self.link_sem = [self.place.recv_sem() for part in range(2)]
        self.near_here = False

    def piece(self, block, part):
        return self.parts.at[pl.ds(pl.multiple_of(block * ROWS + part * 64, 64), 64)]

    def far_ready(self):
        for part in range(2):
            self.place.send(
                self.piece(self.far_other, part),
                self.chip_in.at[0, pl.ds(64 * part, 64)],
                self.quad.partner,
                self.sent,
                self.far_sem[part],
            )

    def near_ready(self):
        self.place.send(
            self.parts.at[rows_at(self.near_other, ROWS)],
            self.chip_in.at[1],
            self.quad.partner,
            self.sent,
            self.near_sem,
        )

    def link(self):
        for part in range(2):
            far_in = self.chip_in.at[0, pl.ds(64 * part, 64)]
            self.place.arrived(far_in, self.far_sem[part])
            piece = self.piece(self.far_own, part)
            add_into(piece, far_in)
            self.place.send(
                piece,
                self.link_in.at[pl.ds(64 * part, 64)],
                self.quad.across,
                self.sent,
                self.link_sem[part],
            )

    def total(self, part):
        if not self.near_here:
            self.place.arrived(self.chip_in.at[1], self.near_sem)
            self.near_here = True
        rows = pl.ds(64 * part, 64)
        self.place.arrived(self.link_in.at[rows], self.link_sem[part])
        total = self.piece(self.quad.tensor, part)[...].astype(jnp.float32)
        total = total + self.chip_in[1, rows].astype(jnp.float32)
        return total + self.link_in[rows].astype(jnp.float32)

    def drain(self):
        self.place.left(self.parts.at[pl.ds(0, 3 * ROWS)], self.sent)


def turn_rows(source, target):
    for k in range(source.shape[1] // 128):
        target[128 * k : 128 * (k + 1), :] = source[:, 128 * k : 128 * (k + 1)].T


def rope(values, cos, sin):
    return values * cos + pltpu.roll(values, HEAD_SIZE // 2, 1) * sin


def rope_back(values, cos, sin):
    return values * cos + pltpu.roll(values * sin, HEAD_SIZE // 2, 1)


def orthogonalize(inbox, current, work, low_square, mixer, side, leave):
    f32, bf16 = jnp.float32, jnp.bfloat16
    tiles = side // 256

    total = jnp.float32(0.0)
    for k in range(8):
        piece = inbox[4 * k : 4 * (k + 1), :, :side].reshape(4 * SHARD_ROWS, side).astype(f32)
        current[:side, 128 * k : 128 * (k + 1)] = piece.T
        total = total + jnp.sum(piece * piece)
    scale = 1.0 / (jnp.sqrt(total) + 1e-07)

    def narrow(slot):
        return work.at[pl.ds(0, side), pl.ds(slot * MODEL_WIDTH, MODEL_WIDTH)]

    energy = jnp.zeros((1, MODEL_WIDTH), f32)
    for k in range(tiles):
        cut = slice(256 * k, 256 * (k + 1))
        piece = current[cut, :] * scale
        current[cut, :] = piece
        narrow(0)[cut, :] = piece.astype(bf16)
        energy = energy + jnp.sum(piece * piece, axis=0, keepdims=True)

    def newton(step, energy):
        now, later = narrow(step), narrow(1 - step)
        shift = jnp.sum(energy, axis=1, keepdims=True) * (1.0 / side)
        linear = newton_two + 2.0 * newton_three * shift
        constant = newton_one + newton_two * shift + newton_three * shift * shift
        row = lax.broadcasted_iota(jnp.int32, (256, 256), 0)
        column = lax.broadcasted_iota(jnp.int32, (256, 256), 1)

        def put(target, k, part):
            cut = slice(256 * k, 256 * (k + 1))
            target[cut, 256 * k : side] = part
            for other in range(k + 1, tiles):
                block = part[:, 256 * (other - k) : 256 * (other - k + 1)]
                target[256 * other : 256 * (other + 1), cut] = block.T

        for k in range(tiles):
            part = lax.dot_general(
                now[256 * k : 256 * (k + 1), :],
                now[256 * k : side, :],
                contract_cols,
                preferred_element_type=f32,
            )
            first = jnp.where(row == column, part[:, :256] - shift, part[:, :256])
            if k < tiles - 1:
                part = jnp.concatenate([first, part[:, 256:]], axis=1)
            else:
                part = first
            put(low_square, k, part.astype(bf16))
        for k in range(tiles):
            cut = slice(256 * k, 256 * (k + 1))
            part = jnp.dot(
                low_square[cut, :side],
                low_square[:side, 256 * k : side],
                preferred_element_type=f32,
            )
            part = linear * low_square[cut, 256 * k : side].astype(f32) + newton_three * part
            put(mixer, k, part.astype(bf16))
        energy = jnp.zeros((1, MODEL_WIDTH), f32)
        for k in range(tiles):
            cut = slice(256 * k, 256 * (k + 1))
            part = jnp.dot(mixer[cut, :side], now[...], preferred_element_type=f32)
            part = part + constant * current[cut, :]
            current[cut, :] = part
            later[cut, :] = part.astype(bf16)
            energy = energy + jnp.sum(part * part, axis=0, keepdims=True)
        return energy

    def pair(step, energy):
        return newton(1, newton(0, energy))

    newton(0, lax.fori_loop(0, NS_ITERS // 2, pair, energy))
    for k in range(8):
        piece = current[:side, 128 * k : 128 * (k + 1)].T
        inbox[4 * k : 4 * (k + 1), :, :side] = piece.astype(bf16).reshape(4, SHARD_ROWS, side)
        leave(k)


def layer_kernel(*refs):
    (
        x_in,
        positions_ref,
        cotangent_in,
        query_in,
        key_in,
        value_in,
        out_in,
        gate_in,
        up_in,
        down_in,
        query_moment_in,
        key_moment_in,
        value_moment_in,
        out_moment_in,
        gate_moment_in,
        up_moment_in,
        down_moment_in,
        gains_ref,
        gain_moment_ref,
        out_ref,
        grad_ref,
        moments_ref,
        weights_ref,
        gain_moment_out,
        gains_out,
        x_ref,
        cotangent_ref,
        shard,
        moments,
        weights,
        cos_ref,
        sin_ref,
        full,
        sums,
        far,
        near,
        last_far,
        last_near,
        swapped,
        normed,
        normed_two,
        cotangents,
        branch_grads,
        turned,
        query_raw,
        key_raw,
        query_rot,
        key_rot,
        value_low,
        key_turned,
        value_turned,
        probs,
        attention,
        attention_grad,
        hidden,
        ffn_grads,
        head_grads,
        key_sum,
        value_sum,
        hidden_one,
        input_grad,
        parts,
        chip_in,
        link_in,
        posted,
        inbox,
        current,
        settled,
        gain_parts,
        gain_tensor,
        gain_dp,
        send_sems,
        recv_sems,
        post_send,
        post_recv,
        back_send,
        back_recv,
        gain_sems,
        local_sems,
    ) = refs
    bf16, f32 = jnp.bfloat16, jnp.float32
    place = Place(send_sems, recv_sems)
    quad = Quad(place)
    dp, tensor = place.dp, place.tensor
    x_at = place.at["x"]

    shard_ins = (query_in, key_in, value_in, out_in, gate_in, up_in, down_in)
    moment_ins = (
        query_moment_in,
        key_moment_in,
        value_moment_in,
        out_moment_in,
        gate_moment_in,
        up_moment_in,
        down_moment_in,
    )
    shard_load, x_load, cotangent_load, moment_load = (local_sems.at[k] for k in range(4))
    out_store, grad_store, moment_store, weight_store = (local_sems.at[k] for k in range(4, 8))
    def load_pieces(sources, target, sem):
        for slot, source in enumerate(sources):
            for start, width, at in pieces[slot]:
                pltpu.make_async_copy(
                    source.at[:, pl.ds(at, width)], target.at[:, pl.ds(start, width)], sem
                ).start()

    load_pieces(shard_ins, shard, shard_load)
    pltpu.make_async_copy(x_in, x_ref, x_load).start()
    pltpu.make_async_copy(cotangent_in, cotangent_ref, cotangent_load).start()
    load_pieces(moment_ins, moments, moment_load)

    def loaded(target, sem):
        pltpu.make_async_copy(target, target, sem).wait()

    barrier = pltpu.get_barrier_semaphore()

    def greet(k, carry):
        pl.semaphore_signal(
            barrier, inc=1, device_id={"dp": lax.rem(dp + k, DP)}, device_id_type=MESH
        )
        return carry

    lax.fori_loop(1, DP, greet, 0)
    for k in range(1, TENSOR):
        pl.semaphore_signal(
            barrier, inc=1, device_id={"tensor": lax.rem(tensor + k, TENSOR)}, device_id_type=MESH
        )
    loaded(shard, shard_load)
    mine = place.rows(place.at["z"], place.at["y"], x_at)
    full[mine, :] = shard[...]
    pl.semaphore_wait(barrier, DP - 1 + TENSOR - 1)

    gather_low, gather_high, gather_out, gather_gate, gather_down = gathers = [
        Gather(place, full, group) for group in column_groups
    ]
    gather_low.swap()
    gather_low.own.begin()
    gather_high.swap()
    gather_high.own.begin()
    gather_out.swap()
    gather_out.own.begin()

    all_gains = gains_ref[...].reshape(1, GAINS)
    gain_attn = all_gains[:, :MODEL_WIDTH]
    gain_ffn = all_gains[:, MODEL_WIDTH : 2 * MODEL_WIDTH]
    gain_query = all_gains[:, 2 * MODEL_WIDTH : 2 * MODEL_WIDTH + HEAD_SIZE]
    gain_key = all_gains[:, 2 * MODEL_WIDTH + HEAD_SIZE :]
    loaded(x_ref, x_load)
    x = x_ref[...].astype(f32)
    first_scale = rms_scale(x)
    normed[quad.own_rows, :] = (x * first_scale * gain_attn).astype(bf16)
    gather_low.begin_other()
    gather_normed = QuadGather(quad, normed)
    gather_normed.start()
    gather_gate.swap()
    gather_low.own.forward_first()
    gather_high.begin_other()
    gather_low.other.forward_first()
    gather_low.both("finish_first")
    gather_high.both("forward_first")
    gather_low.both("forward_second")
    gather_normed.forward()
    gather_high.both("finish_first")
    gather_out.begin_other()
    gather_high.both("forward_second")
    gather_out.both("forward_first")
    gather_gate.own.begin()
    gather_gate.begin_other()
    gather_down.swap()

    angle = jnp.broadcast_to(
        positions_ref[...].reshape(1, SEQ).astype(f32), (HEAD_SIZE, SEQ)
    ).T
    lane = lax.broadcasted_iota(jnp.int32, (1, HEAD_SIZE), 1)
    low_half = lane < HEAD_SIZE // 2
    step = jnp.where(low_half, lane, lane - HEAD_SIZE // 2).astype(f32)
    angle = angle * jnp.exp(step * (-2.0 * math.log(rope_base) / HEAD_SIZE))
    cos_ref[...] = jnp.cos(angle)
    sin = jnp.sin(angle)
    sin_ref[...] = jnp.where(low_half, -sin, sin)

    loaded(cotangent_ref, cotangent_load)
    cotangents[quad.own_rows, :] = cotangent_ref[...]
    gather_cotangent = QuadGather(quad, cotangents)
    gather_cotangent.start()
    gather_normed.near()
    gather_normed.finish()
    gather_low.both("finish_second")
    gather_out.both("finish_first")

    def project(half):
        heads = jnp.dot(
            normed[...], full[:, 512 * half : 512 * (half + 1)], preferred_element_type=f32
        )
        query_raw[:, 256 * half : 256 * (half + 1)] = heads[:, :256]
        for head in range(2):
            raw = heads[:, HEAD_SIZE * head : HEAD_SIZE * (head + 1)]
            rotated = rope(raw * rms_scale(raw) * gain_query, cos_ref[...], sin_ref[...])
            query_rot[:, rows_at(2 * half + head, HEAD_SIZE)] = rotated.astype(bf16)
        lanes = rows_at(half, HEAD_SIZE)
        raw = heads[:, 256:384]
        key_raw[:, lanes] = raw
        rotated = rope(raw * rms_scale(raw) * gain_key, cos_ref[...], sin_ref[...]).astype(bf16)
        key_rot[:, lanes] = rotated
        key_turned[lanes, :] = rotated.T
        value = heads[:, 384:].astype(bf16)
        value_low[:, lanes] = value
        value_turned[lanes, :] = value.T

    project(0)
    gather_gate.both("forward_first")
    gather_high.both("finish_second")
    project(1)
    gather_out.both("forward_second")
    gather_down.own.begin()
    gather_down.begin_other()
    gather_gate.both("finish_first")

    def attend(head):
        lanes, shared = rows_at(head, HEAD_SIZE), rows_at(head // 2, HEAD_SIZE)
        for block in range(2):
            keys, begin = 256 * (block + 1), 256 * block
            scores = lax.dot_general(
                key_rot[pl.ds(0, keys), shared],
                query_rot[pl.ds(begin, 256), lanes],
                contract_cols,
                preferred_element_type=f32,
            )
            row = lax.broadcasted_iota(jnp.int32, (keys, 256), 0)
            column = lax.broadcasted_iota(jnp.int32, (keys, 256), 1) + begin
            scores = jnp.where(row <= column, scores * SCALE, -1e30)
            shifted = jnp.exp(scores - jnp.max(scores, axis=0, keepdims=True))
            total = jnp.sum(shifted, axis=0, keepdims=True)
            low = (shifted * (1.0 / total)).astype(bf16)
            probs[head, pl.ds(0, keys), pl.ds(begin, 256)] = low
            mixed = jnp.dot(
                value_turned[shared, pl.ds(0, keys)], low, preferred_element_type=f32
            )
            attention[pl.ds(begin, 256), lanes] = mixed.T.astype(bf16)

    attend(0)
    gather_gate.own.forward_second()
    gather_down.both("forward_first")
    attend(1)
    gather_out.both("finish_second")
    gather_gate.other.forward_second()
    attend(2)
    gather_down.both("finish_first")
    gather_cotangent.forward()
    attend(3)
    gather_down.own.forward_second()

    def project_back(source, start, width, target):
        def run(rows):
            for k in range(4):
                part = lax.dot_general(
                    source[rows, :],
                    full[256 * k : 256 * (k + 1), start : start + width],
                    contract_cols,
                    preferred_element_type=f32,
                )
                target[rows, 256 * k : 256 * (k + 1)] = part.astype(bf16)

        return run

    def reducer(k):
        return QuadReduce(quad, parts.at[k], chip_in.at[k], link_in.at[k])

    reduce_attn = reducer(0)
    out_rows = project_back(attention, 1024, 512, parts.at[0])
    out_rows(quad.far_rows)
    reduce_attn.far_ready()
    out_rows(quad.near_rows)
    reduce_attn.near_ready()
    reduce_attn.link()
    gather_down.other.forward_second()
    turn_rows(normed, turned.at[1])
    gather_cotangent.near()
    gather_cotangent.finish()
    turn_rows(cotangents, turned.at[0])
    gather_two = QuadGather(quad, normed_two)
    for part in range(2):
        rows = pl.ds(64 * part, 64)
        first_hidden = x_ref[rows, :].astype(f32) + reduce_attn.total(part)
        hidden_one[rows, :] = first_hidden
        normed_two[pl.ds(pl.multiple_of(tensor * ROWS + 64 * part, 64), 64), :] = (
            first_hidden * rms_scale(first_hidden) * gain_ffn
        ).astype(bf16)
        gather_two.start(part)
    gather_gate.both("finish_second")
    gather_two.forward()
    gather_down.both("finish_second")

    def feed(rows):
        for k in range(3):
            low = normed_two[rows, :]
            at = 256 * k
            gate = jnp.dot(low, full[:, 1536 + at : 1792 + at], preferred_element_type=f32)
            up = jnp.dot(low, full[:, 2304 + at : 2560 + at], preferred_element_type=f32)
            grad = jnp.dot(
                cotangents[rows, :], full[:, 3072 + at : 3328 + at], preferred_element_type=f32
            )
            sigmoid = 1.0 / (1.0 + jnp.exp(-gate))
            activated = gate * sigmoid
            hidden[rows, at : at + 256] = (activated * up).astype(bf16)
            ffn_grads[rows, at : at + 256] = (
                grad * up * (sigmoid * (1.0 + gate * (1.0 - sigmoid)))
            ).astype(bf16)
            ffn_grads[rows, 768 + at : 1024 + at] = (grad * activated).astype(bf16)

    reduce_two = reducer(1)
    two_rows = project_back(ffn_grads, 1536, 1536, parts.at[1])
    gather_two.near()
    feed(quad.near_rows)
    two_rows(quad.near_rows)
    reduce_two.near_ready()
    gather_two.finish()
    feed(quad.far_rows)
    two_rows(quad.far_rows)
    reduce_two.far_ready()

    def weight_grads(left, right, start, first, last):
        for k in range(first, last):
            part = jnp.dot(
                left[...], right[:, 256 * k : 256 * (k + 1)], preferred_element_type=f32
            )
            sums[:, start + 256 * k : start + 256 * (k + 1)] = part.astype(bf16)

    weight_grads(turned.at[0], hidden, 3072, 0, 2)
    reduce_two.link()
    weight_grads(turned.at[0], hidden, 3072, 2, 3)
    buffers = (sums, far, near, last_far, last_near)
    sum_low, sum_high, sum_out, sum_gate, sum_down = all_sums = [
        Reduce(place, buffers, swapped, group) for group in column_groups
    ]
    sum_down.both("begin")
    turn_rows(normed_two, turned.at[0])
    weight_grads(turned.at[0], ffn_grads, 1536, 0, 4)
    sum_down.both("pass_first")

    gather_branch = QuadGather(quad, branch_grads)
    ffn_gain_grad = jnp.zeros((1, MODEL_WIDTH), f32)
    for part in range(2):
        rows = pl.ds(64 * part, 64)
        normed_two_grad = reduce_two.total(part)
        first_hidden = hidden_one[rows, :]
        second_scale = rms_scale(first_hidden)
        second_hat = first_hidden * second_scale
        ffn_gain_grad = ffn_gain_grad + jnp.sum(
            normed_two_grad * second_hat, axis=0, keepdims=True
        )
        hidden_one_grad = cotangent_ref[rows, :].astype(f32) + norm_backward(
            normed_two_grad * gain_ffn, second_hat, second_scale
        )
        input_grad[rows, :] = hidden_one_grad
        branch_grads[pl.ds(pl.multiple_of(tensor * ROWS + 64 * part, 64), 64), :] = (
            hidden_one_grad.astype(bf16)
        )
        gather_branch.start(part)
    gain_parts[:, MODEL_WIDTH : 2 * MODEL_WIDTH] = ffn_gain_grad
    weight_grads(turned.at[0], ffn_grads, 1536, 4, 6)
    sum_gate.both("begin")

    reduce_ffn = reducer(2)
    down_rows = project_back(hidden, 3072, 768, parts.at[2])
    down_rows(quad.far_rows)
    reduce_ffn.far_ready()

    def attend_grad(rows):
        part = jnp.dot(branch_grads[rows, :], full[:, 1024:1536], preferred_element_type=f32)
        attention_grad[rows, :] = part.astype(bf16)

    gather_branch.near()
    gather_branch.forward(0)
    attend_grad(quad.near_rows)
    gather_branch.forward(1)
    sum_down.both("begin_second")
    down_rows(quad.near_rows)
    reduce_ffn.near_ready()
    reduce_ffn.link()
    gather_branch.finish()
    attend_grad(quad.far_rows)
    sum_gate.both("pass_first")
    turn_rows(branch_grads, turned.at[0])
    weight_grads(turned.at[0], attention, 1024, 0, 2)
    sum_out.both("begin")

    def head_norm_back(rotated_grad, raw, gain, rows):
        scale = rms_scale(raw)
        hat = raw * scale
        norm_grad = rope_back(rotated_grad, cos_ref[rows, :], sin_ref[rows, :])
        gain_grad = jnp.sum(norm_grad * hat, axis=0, keepdims=True)
        return norm_backward(norm_grad * gain, hat, scale).astype(bf16), gain_grad

    def attend_back(head, gain_sum):
        lanes, shared = rows_at(head, HEAD_SIZE), rows_at(head // 2, HEAD_SIZE)
        for block in (1, 0):
            keys, begin = 256 * (block + 1), 256 * block
            key_cut, query_cut = pl.ds(0, keys), pl.ds(begin, 256)
            mixed_grad = attention_grad[query_cut, lanes]
            low = probs[head, key_cut, query_cut]
            wide = low.astype(f32)
            probs_grad = lax.dot_general(
                value_low[key_cut, shared],
                mixed_grad,
                contract_cols,
                preferred_element_type=f32,
            )
            inner_sum = jnp.sum(wide * probs_grad, axis=0, keepdims=True)
            score_grad = (wide * (probs_grad - inner_sum)).astype(bf16)
            value_part = jnp.dot(low, mixed_grad, preferred_element_type=f32)
            key_part = jnp.dot(
                score_grad, query_rot[query_cut, lanes], preferred_element_type=f32
            )
            if head % 2 == 0 and block == 1:
                value_sum[:, shared] = value_part
                key_sum[:, shared] = key_part
            else:
                value_sum[key_cut, shared] += value_part
                key_sum[key_cut, shared] += key_part
            query_part = jnp.dot(
                key_turned[shared, key_cut], score_grad, preferred_element_type=f32
            )
            grad, gain_part = head_norm_back(
                query_part.T * SCALE, query_raw[query_cut, lanes], gain_query, query_cut
            )
            head_grads[query_cut, rows_at(head + 2 * (head // 2), HEAD_SIZE)] = grad
            gain_sum = gain_sum + gain_part
        return gain_sum

    def shared_back(head, gain_sum):
        shared = rows_at(head, HEAD_SIZE)
        grad, gain_part = head_norm_back(
            key_sum[:, shared] * SCALE, key_raw[:, shared], gain_key, pl.ds(0, SEQ)
        )
        head_grads[:, rows_at(4 * head + 2, HEAD_SIZE)] = grad
        head_grads[:, rows_at(4 * head + 3, HEAD_SIZE)] = value_sum[:, shared].astype(bf16)
        return gain_sum + gain_part

    none = jnp.zeros((1, HEAD_SIZE), f32)
    query_gain_sum = attend_back(0, none)
    sum_down.both("pass_second")
    query_gain_sum = attend_back(1, query_gain_sum)
    key_gain_sum = shared_back(0, none)
    weight_grads(turned.at[1], head_grads, 0, 0, 2)
    sum_low.both("begin")
    sum_gate.other.begin_second()
    query_gain_sum = attend_back(2, query_gain_sum)
    sum_out.both("pass_first")
    sum_gate.own.begin_second()
    sum_down.finish()
    query_gain_sum = attend_back(3, query_gain_sum)
    key_gain_sum = shared_back(1, key_gain_sum)
    gain_parts[:, 2 * MODEL_WIDTH : 2 * MODEL_WIDTH + HEAD_SIZE] = query_gain_sum
    gain_parts[:, 2 * MODEL_WIDTH + HEAD_SIZE :] = key_gain_sum
    sum_gate.both("pass_second")
    weight_grads(turned.at[1], head_grads, 0, 2, 4)
    sum_high.both("begin")
    sum_low.both("pass_first")
    sum_out.both("begin_second")

    reduce_one = reducer(3)
    one_rows = project_back(head_grads, 0, 1024, parts.at[3])
    one_rows(quad.far_rows)
    reduce_one.far_ready()
    sum_gate.finish()
    sum_low.both("begin_second")
    one_rows(quad.near_rows)
    reduce_one.near_ready()
    sum_high.both("pass_first")
    sum_out.both("pass_second")
    reduce_one.link()
    sum_low.both("pass_second")
    sum_out.finish()

    loaded(moments, moment_load)
    core = tensor % 2
    owner = [even + core * (odd - even) for even, odd in owners]

    def update(group):
        start, width = column_groups[group]
        cut = pl.ds(start, width)
        fresh = moment_decay * moments[:, cut] + all_sums[group].total()
        moments[:, cut] = fresh
        posted[:, cut] = fresh.astype(bf16)
        pltpu.make_async_copy(moments.at[:, cut], moments_ref.at[:, cut], moment_store).start()
        for slot in range(7):
            for piece_start, piece_width, at in pieces[slot]:
                if start <= piece_start < start + width:
                    post(slot, pl.ds(piece_start, piece_width), pl.ds(at, piece_width))

    def post(slot, cut, at):
        @pl.when(dp != owner[slot])
        def _():
            place.send(
                posted.at[:, cut],
                inbox.at[dp, :, at],
                {"dp": owner[slot]},
                post_send.at[slot],
                post_recv.at[0],
            )

        @pl.when(dp == owner[slot])
        def _():
            inbox[dp, :, at] = posted[:, cut]

    update(4)
    update(3)
    sum_high.both("begin_second")

    for part in range(2):
        rows = pl.ds(64 * part, 64)
        hidden_one[rows, :] = hidden_one[rows, :] + reduce_ffn.total(part)
    pltpu.make_async_copy(hidden_one, out_ref, out_store).start()
    sum_low.finish()
    sum_high.both("pass_second")
    update(2)
    attn_gain_grad = jnp.zeros((1, MODEL_WIDTH), f32)
    for part in range(2):
        rows = pl.ds(64 * part, 64)
        normed_grad = reduce_one.total(part)
        x = x_ref[rows, :].astype(f32)
        first_scale = rms_scale(x)
        first_hat = x * first_scale
        attn_gain_grad = attn_gain_grad + jnp.sum(normed_grad * first_hat, axis=0, keepdims=True)
        input_grad[rows, :] = input_grad[rows, :] + norm_backward(
            normed_grad * gain_attn, first_hat, first_scale
        )
    gain_parts[:, :MODEL_WIDTH] = attn_gain_grad
    pltpu.make_async_copy(input_grad, grad_ref, grad_store).start()
    sum_high.finish()
    update(0)

    gain_tensor[tensor] = gain_parts[...]
    for k in range(1, TENSOR):
        place.send(
            gain_parts,
            gain_tensor.at[tensor],
            {"tensor": lax.rem(tensor + k, TENSOR)},
            gain_sems.at[0],
            gain_sems.at[1],
        )
    update(1)

    for group in gathers + all_sums:
        group.drain()
    for exchange in (gather_normed, gather_cotangent, gather_two, gather_branch):
        exchange.drain()
    for exchange in (reduce_attn, reduce_two, reduce_ffn, reduce_one):
        exchange.drain()

    place.arrived(gain_tensor.at[pl.ds(0, TENSOR - 1)], gain_sems.at[1])
    gain_dp[dp] = gain_tensor[0] + gain_tensor[1] + gain_tensor[2] + gain_tensor[3]

    def gain_start(k, carry):
        place.send(
            gain_dp.at[dp],
            gain_dp.at[dp],
            {"dp": lax.rem(dp + k, DP)},
            gain_sems.at[2],
            gain_sems.at[3],
        )
        return carry

    lax.fori_loop(1, DP, gain_start, 0)

    for slot in (4, 5, 6, 3, 0, 1, 2):

        @pl.when(dp == owner[slot])
        def _():
            place.arrived(inbox.at[pl.ds(0, DP - 1), :, pl.ds(0, widths[slot])], post_recv.at[0])

    work = full.at[:, pl.ds(0, 2 * MODEL_WIDTH)]
    low_square = full.at[:WIDEST, pl.ds(2048, WIDEST)]
    mixer = full.at[:WIDEST, pl.ds(2816, WIDEST)]
    def run_class(slots):
        side = widths[slots[0]]
        here = dp == owner[slots[0]]
        for slot in slots[1:]:
            here = here | (dp == owner[slot])

        def leave(k):
            for slot in slots:

                @pl.when(dp == owner[slot])
                def _():
                    def send_back(j, carry):
                        target = 4 * k + j
                        for start, width, at in pieces[slot]:
                            cut, at = pl.ds(start, width), pl.ds(at, width)

                            @pl.when(target != dp)
                            def _():
                                place.send(
                                    inbox.at[target, :, at],
                                    settled.at[:, cut],
                                    {"dp": target},
                                    back_send.at[0],
                                    back_recv.at[slot],
                                )

                            @pl.when(target == dp)
                            def _():
                                settled[:, cut] = inbox[target, :, at]

                        return carry

                    lax.fori_loop(0, 4, send_back, 0)

        @pl.when(here)
        def _():
            orthogonalize(inbox, current, work, low_square, mixer, side, leave)

    for slots in classes:
        run_class(slots)

    place.arrived(gain_dp.at[pl.ds(0, DP - 1)], gain_sems.at[3])

    def gain_add(k, carry):
        return carry + gain_dp[k]

    gain_total = lax.fori_loop(1, DP, gain_add, gain_dp[0]).reshape(GAINS)
    fresh_gain = gain_decay * gain_moment_ref[...] + gain_total
    gain_moment_out[...] = fresh_gain
    gains_out[...] = gains_ref[...] - gain_rate / math.sqrt(SEQ * DP) * fresh_gain

    for slot in (1, 2, 0, 3, 4, 5, 6):

        @pl.when(dp != owner[slot])
        def _():
            place.arrived(settled.at[:, pl.ds(0, widths[slot])], back_recv.at[slot])

        for start, width, at in pieces[slot]:
            cut = pl.ds(start, width)
            weights[:, cut] = shard[:, cut].astype(f32) - rates[slot] * settled[:, cut].astype(f32)
            pltpu.make_async_copy(weights.at[:, cut], weights_ref.at[:, cut], weight_store).start()

    place.left(gain_tensor.at[pl.ds(0, TENSOR - 1)], gain_sems.at[0])
    place.left(gain_dp.at[pl.ds(0, DP - 1)], gain_sems.at[2])
    for slot in range(7):

        @pl.when(dp != owner[slot])
        def _():
            place.left(posted.at[:, pl.ds(0, widths[slot])], post_send.at[slot])

        @pl.when(dp == owner[slot])
        def _():
            place.left(inbox.at[pl.ds(0, DP - 1), :, pl.ds(0, widths[slot])], back_send.at[0])

    loaded(hidden_one, out_store)
    loaded(input_grad, grad_store)
    loaded(moments, moment_store)
    loaded(weights, weight_store)


def run_layer(args):
    bf16, f32 = jnp.bfloat16, jnp.float32
    shard_shape = (SHARD_ROWS, COLUMNS)
    dma = pltpu.SemaphoreType.DMA
    in_specs = [ANY] * 19
    in_specs[1] = in_specs[17] = in_specs[18] = VMEM
    return pl.pallas_call(
        layer_kernel,
        out_shape=(
            jax.ShapeDtypeStruct((ROWS, MODEL_WIDTH), f32),
            jax.ShapeDtypeStruct((ROWS, MODEL_WIDTH), f32),
            jax.ShapeDtypeStruct(shard_shape, f32),
            jax.ShapeDtypeStruct(shard_shape, f32),
            jax.ShapeDtypeStruct((GAINS,), f32),
            jax.ShapeDtypeStruct((GAINS,), f32),
        ),
        in_specs=in_specs,
        out_specs=(ANY, ANY, ANY, ANY, VMEM, VMEM),
        scratch_shapes=[
            pltpu.VMEM((ROWS, MODEL_WIDTH), bf16),
            pltpu.VMEM((ROWS, MODEL_WIDTH), bf16),
            pltpu.VMEM(shard_shape, bf16),
            pltpu.VMEM(shard_shape, f32),
            pltpu.VMEM(shard_shape, f32),
            pltpu.VMEM((SEQ, HEAD_SIZE), f32),
            pltpu.VMEM((SEQ, HEAD_SIZE), f32),
            pltpu.VMEM((MODEL_WIDTH, COLUMNS), bf16),
            pltpu.VMEM((MODEL_WIDTH, COLUMNS), bf16),
            pltpu.VMEM((2, 4, SHARD_ROWS, COLUMNS), bf16),
            pltpu.VMEM((2, 2, 4, SHARD_ROWS, COLUMNS), bf16),
            pltpu.VMEM((2, SHARD_ROWS, COLUMNS), bf16),
            pltpu.VMEM((2, 2, SHARD_ROWS, COLUMNS), bf16),
            pltpu.VMEM(shard_shape, bf16),
            pltpu.VMEM((SEQ, MODEL_WIDTH), bf16),
            pltpu.VMEM((SEQ, MODEL_WIDTH), bf16),
            pltpu.VMEM((SEQ, MODEL_WIDTH), bf16),
            pltpu.VMEM((SEQ, MODEL_WIDTH), bf16),
            pltpu.VMEM((2, MODEL_WIDTH, SEQ), bf16),
            pltpu.VMEM((SEQ, 512), f32),
            pltpu.VMEM((SEQ, 256), f32),
            pltpu.VMEM((SEQ, 512), bf16),
            pltpu.VMEM((SEQ, 256), bf16),
            pltpu.VMEM((SEQ, 256), bf16),
            pltpu.VMEM((256, SEQ), bf16),
            pltpu.VMEM((256, SEQ), bf16),
            pltpu.VMEM((4, SEQ, SEQ), bf16),
            pltpu.VMEM((SEQ, 512), bf16),
            pltpu.VMEM((SEQ, 512), bf16),
            pltpu.VMEM((SEQ, 768), bf16),
            pltpu.VMEM((SEQ, 1536), bf16),
            pltpu.VMEM((SEQ, 1024), bf16),
            pltpu.VMEM((SEQ, 256), f32),
            pltpu.VMEM((SEQ, 256), f32),
            pltpu.VMEM((ROWS, MODEL_WIDTH), f32),
            pltpu.VMEM((ROWS, MODEL_WIDTH), f32),
            pltpu.VMEM((4, SEQ, MODEL_WIDTH), bf16),
            pltpu.VMEM((4, 2, ROWS, MODEL_WIDTH), bf16),
            pltpu.VMEM((4, ROWS, MODEL_WIDTH), bf16),
            pltpu.VMEM(shard_shape, bf16),
            pltpu.VMEM((DP, SHARD_ROWS, WIDEST), bf16),
            pltpu.VMEM((WIDEST, MODEL_WIDTH), f32),
            pltpu.VMEM(shard_shape, bf16),
            pltpu.VMEM((1, GAINS), f32),
            pltpu.VMEM((TENSOR, 1, GAINS), f32),
            pltpu.VMEM((DP, 1, GAINS), f32),
            dma((18,)),
            dma((216,)),
            dma((7,)),
            dma((1,)),
            dma((1,)),
            dma((7,)),
            dma((4,)),
            dma((8,)),
        ],
        compiler_params=pltpu.CompilerParams(
            collective_id=0, has_side_effects=True, vmem_limit_bytes=62 << 20
        ),
        name="layer",
    )(*args)


def unpack_kernel(*refs):
    sources, targets = refs[:6], refs[6:]
    out, grad, moments, weights, gain_moment, gains = sources
    targets[0][...] = out[...]
    targets[1][...] = grad[...]
    for slot in range(7):
        for start, width, at in pieces[slot]:
            cut, at = pl.ds(start, width), pl.ds(at, width)
            targets[2 + slot][:, at] = moments[:, cut]
            targets[9 + slot][:, at] = weights[:, cut]
    targets[16][...] = gain_moment[...]
    targets[17][...] = gains[...]


def unpack(results):
    f32 = jnp.float32
    pieces = [jax.ShapeDtypeStruct((SHARD_ROWS, width), f32) for width in widths]
    shapes = [jax.ShapeDtypeStruct((ROWS, MODEL_WIDTH), f32)] * 2
    shapes += pieces + pieces + [jax.ShapeDtypeStruct((GAINS,), f32)] * 2
    return pl.pallas_call(
        unpack_kernel,
        out_shape=tuple(shapes),
        in_specs=[VMEM] * 6,
        out_specs=(VMEM,) * 18,
        name="unpack",
    )(*results)


def body(*args):
    args = list(args)
    for index in (6, 9, 13, 16):
        args[index] = args[index].T
    results = list(unpack(run_layer(args)))
    for index in (5, 8, 12, 15):
        results[index] = results[index].T
    return tuple(results)


def solution(mesh):
    placed = (
        P(("dp", "tensor"), None),
        P("dp"),
        P(("dp", "tensor"), None),
        P("dp", "tensor"),
        P("dp", "tensor"),
        P("dp", "tensor"),
        P("tensor", "dp"),
        P("dp", "tensor"),
        P("dp", "tensor"),
        P("tensor", "dp"),
        P("dp", "tensor"),
        P("dp", "tensor"),
        P("dp", "tensor"),
        P("tensor", "dp"),
        P("dp", "tensor"),
        P("dp", "tensor"),
        P("tensor", "dp"),
        P(),
        P(),
    )
    return jax.shard_map(
        body,
        mesh=mesh,
        in_specs=placed,
        out_specs=(
            P(("dp", "tensor"), None),
            P(("dp", "tensor"), None),
            P("dp", "tensor"),
            P("dp", "tensor"),
            P("dp", "tensor"),
            P("tensor", "dp"),
            P("dp", "tensor"),
            P("dp", "tensor"),
            P("tensor", "dp"),
            P("dp", "tensor"),
            P("dp", "tensor"),
            P("dp", "tensor"),
            P("tensor", "dp"),
            P("dp", "tensor"),
            P("dp", "tensor"),
            P("tensor", "dp"),
            P(),
            P(),
        ),
        check_vma=False,
    )
```

```python
import functools
import math

import jax
import jax.numpy as jnp
from jax import lax
from jax.experimental import pallas as pl
from jax.experimental.pallas import tpu as pltpu
from jax.sharding import PartitionSpec as P

MODEL_WIDTH = 1024
HEAD_SIZE = 128
NS_ITERS = 5


epsilon = 1e-06
moment_decay = 0.95
gain_decay = 0.9
gain_rate = 0.3
rope_base = 1000000.0
newton_one = 3.4445
newton_two = -4.775
newton_three = 2.0315
contract_rows = (((0,), (0,)), ((), ()))
contract_cols = (((1,), (1,)), ((), ()))


def rms_scale(values):
    return lax.rsqrt(jnp.mean(values * values, axis=-1, keepdims=True) + epsilon)


def norm_backward(gradient_value, normalized_input, scale_value):
    return scale_value * (
        gradient_value
        - normalized_input * jnp.mean(gradient_value * normalized_input, axis=-1, keepdims=True)
    )


COLUMNS = 3840
widths = (512, 256, 256, 512, 768, 768, 768)
pieces = (
    ((0, 256, 0), (512, 256, 256)),
    ((256, 128, 0), (768, 128, 128)),
    ((384, 128, 0), (896, 128, 128)),
    ((1024, 512, 0),),
    ((1536, 768, 0),),
    ((2304, 768, 0),),
    ((3072, 768, 0),),
)
owners = ((8, 26), (6, 17), (28, 3), (25, 14), (0, 31), (13, 5), (18, 23))
rates = (1.0, 1.0, 1.0, math.sqrt(8.0), 1.0, 1.0, math.sqrt(4.0 / 3.0))
column_groups = ((0, 512), (512, 512), (1024, 512), (1536, 1536), (3072, 768))
classes = ((4, 5, 6), (0, 3), (1, 2))
DP = 32
TENSOR = 4
SHARD_ROWS = 32
HALF = SHARD_ROWS // 2
WIDEST = 768
MESH = pl.DeviceIdType.MESH
ANY = pl.BlockSpec(memory_space=pl.ANY)
VMEM = pl.BlockSpec(memory_space=pltpu.VMEM)


class Place:
    def __init__(self, send_sems, recv_sems):
        self.send_sems, self.recv_sems = send_sems, recv_sems
        self.sends, self.recvs = 0, 0
        self.dp = lax.axis_index("dp")
        self.tensor = lax.axis_index("tensor")
        self.at = {"z": self.dp // 8, "y": (self.dp // 2) % 4, "x": self.dp % 2}

    def send_sem(self):
        self.sends += 1
        return self.send_sems.at[self.sends - 1]

    def recv_sem(self):
        self.recvs += 1
        return self.recv_sems.at[self.recvs - 1]

    def step(self, axis, delta):
        size = 2 if axis == "x" else 4
        return lax.rem(self.at[axis] + size + delta, size)

    def neighbour(self, axis, delta):
        at = dict(self.at)
        at[axis] = self.step(axis, delta)
        return {"dp": at["z"] * 8 + at["y"] * 2 + at["x"]}

    def block(self, axis, delta, other, other_delta):
        first, second = self.step(axis, delta), self.step(other, other_delta)
        return (first, second) if axis == "z" else (second, first)

    def rows(self, z_at, y_at, x_at, low=0, rows=SHARD_ROWS):
        begin = (z_at * 8 + y_at * 2 + x_at) * SHARD_ROWS + low
        return pl.ds(pl.multiple_of(begin, 16), rows)

    def copy(self, source, target, device, sent, received):
        return pltpu.make_async_remote_copy(
            src_ref=source,
            dst_ref=target,
            send_sem=sent,
            recv_sem=received,
            device_id=device,
            device_id_type=MESH,
        )

    def send(self, source, target, device, sent, received):
        self.copy(source, target, device, sent, received).start()

    def arrived(self, like, received):
        self.copy(like, like, self.neighbour("x", 1), received, received).wait_recv()

    def left(self, like, sent):
        self.copy(like, like, self.neighbour("x", 1), sent, sent).wait_send()


def two_orders(group):
    start, width = group
    half = width // 2
    return (("z", "y", (start, half)), ("y", "z", (start + half, half)))


class GatherSide:
    def __init__(self, place, full, x_at, group, sent):
        self.place, self.full, self.x_at, self.group, self.sent = place, full, x_at, group, sent
        self.direct, self.passed = place.recv_sem(), place.recv_sem()
        self.along = {k: place.recv_sem() for k in (0, -1, 1, 2)}
        self.last = place.recv_sem()

    def send(self, stream, first_delta, second_delta, low, rows, axis, delta, received):
        first, second, columns = stream
        z_at, y_at = self.place.block(first, first_delta, second, second_delta)
        ref = self.full.at[self.place.rows(z_at, y_at, self.x_at, low, rows), pl.ds(*columns)]
        self.place.send(ref, ref, self.place.neighbour(axis, delta), self.sent, received)

    def wait(self, received, rows):
        self.place.arrived(self.full.at[pl.ds(0, rows), pl.ds(*self.group)], received)

    def spread(self, first_delta):
        for stream in two_orders(self.group):
            for delta in (1, -1):
                self.send(
                    stream, first_delta, 0, 0, SHARD_ROWS, stream[1], delta, self.along[first_delta]
                )

    def begin(self):
        for stream in two_orders(self.group):
            for delta in (1, -1):
                self.send(stream, 0, 0, 0, SHARD_ROWS, stream[0], delta, self.direct)
        self.spread(0)

    def forward_first(self):
        self.wait(self.direct, 2 * SHARD_ROWS)
        for stream in two_orders(self.group):
            self.send(stream, -1, 0, 0, HALF, stream[0], 1, self.passed)
            self.send(stream, 1, 0, HALF, HALF, stream[0], -1, self.passed)
        self.spread(-1)
        self.spread(1)

    def finish_first(self):
        self.wait(self.passed, SHARD_ROWS)
        self.spread(2)

    def forward_second(self):
        for first_delta in (0, -1, 1, 2):
            self.wait(self.along[first_delta], 2 * SHARD_ROWS)
            for stream in two_orders(self.group):
                self.send(stream, first_delta, -1, 0, HALF, stream[1], 1, self.last)
                self.send(stream, first_delta, 1, HALF, HALF, stream[1], -1, self.last)

    def finish_second(self):
        self.wait(self.last, 4 * SHARD_ROWS)


class Gather:
    def __init__(self, place, full, group):
        self.place, self.full, self.group = place, full, group
        self.sent, self.swapped = place.send_sem(), place.recv_sem()
        x_at = place.at["x"]
        self.own = GatherSide(place, full, x_at, group, self.sent)
        self.other = GatherSide(place, full, 1 - x_at, group, self.sent)
        self.mine = full.at[place.rows(place.at["z"], place.at["y"], x_at), pl.ds(*group)]

    def swap(self):
        self.place.send(
            self.mine, self.mine, self.place.neighbour("x", 1), self.sent, self.swapped
        )

    def begin_other(self):
        self.place.arrived(self.mine, self.swapped)
        self.other.begin()

    def both(self, name):
        for side in (self.own, self.other):
            getattr(side, name)()

    def drain(self):
        rows = (DP - 1) * SHARD_ROWS
        self.place.left(self.full.at[pl.ds(0, rows), pl.ds(*self.group)], self.sent)


def add_into(target, *terms):
    total = target[...].astype(jnp.float32)
    for term in terms:
        total = total + term[...].astype(jnp.float32)
    target[...] = total.astype(target.dtype)


class ReduceSide:
    def __init__(self, place, buffers, side, group, sent):
        self.place, self.side, self.group, self.sent = place, side, group, sent
        self.sums, self.far, self.near, self.last_far, self.last_near = buffers
        self.x_at = place.at["x"] if side == 0 else 1 - place.at["x"]
        self.far_sem = {k: place.recv_sem() for k in (0, -1, 1, 2)}
        self.near_sem = {k: place.recv_sem() for k in (0, -1, 1, 2)}
        self.last_far_sem, self.last_near_sem = place.recv_sem(), place.recv_sem()

    def block(self, stream, first_delta, second_delta, low=0, rows=SHARD_ROWS):
        first, second, columns = stream
        z_at, y_at = self.place.block(first, first_delta, second, second_delta)
        return self.sums.at[self.place.rows(z_at, y_at, self.x_at, low, rows), pl.ds(*columns)]

    def send(self, source, target, axis, delta, received):
        self.place.send(source, target, self.place.neighbour(axis, delta), self.sent, received)

    def wait(self, received, rows):
        self.place.arrived(self.sums.at[pl.ds(0, rows), pl.ds(*self.group)], received)

    def begin(self):
        for k in (2, 1, -1, 0):
            for stream in two_orders(self.group):
                far = self.far.at[self.side, k % 4, :, pl.ds(*stream[2])]
                for low, delta in ((0, 1), (HALF, -1)):
                    self.send(
                        self.block(stream, 2, k, low, HALF),
                        far.at[pl.ds(low, HALF)],
                        stream[0],
                        delta,
                        self.far_sem[k],
                    )

    def pass_first(self):
        for k in (2, 1, -1, 0):
            self.wait(self.far_sem[k], SHARD_ROWS)
            for stream in two_orders(self.group):
                far = self.far.at[self.side, k % 4, :, pl.ds(*stream[2])]
                for way, (low, delta) in enumerate(((0, 1), (HALF, -1))):
                    add_into(self.block(stream, delta, k, low, HALF), far.at[pl.ds(low, HALF)])
                    self.send(
                        self.block(stream, delta, k),
                        self.near.at[way, self.side, k % 4, :, pl.ds(*stream[2])],
                        stream[0],
                        delta,
                        self.near_sem[k],
                    )

    def begin_second(self):
        for k in (2, 1, -1, 0):
            self.wait(self.near_sem[k], 2 * SHARD_ROWS)
            for stream in two_orders(self.group):
                columns = pl.ds(*stream[2])
                add_into(
                    self.block(stream, 0, k),
                    self.near.at[0, self.side, k % 4, :, columns],
                    self.near.at[1, self.side, k % 4, :, columns],
                )
                if k == 2:
                    for low, delta in ((0, 1), (HALF, -1)):
                        self.send(
                            self.block(stream, 0, 2, low, HALF),
                            self.last_far.at[self.side, pl.ds(low, HALF), columns],
                            stream[1],
                            delta,
                            self.last_far_sem,
                        )

    def pass_second(self):
        self.wait(self.last_far_sem, SHARD_ROWS)
        for stream in two_orders(self.group):
            columns = pl.ds(*stream[2])
            for way, (low, delta) in enumerate(((0, 1), (HALF, -1))):
                add_into(
                    self.block(stream, 0, delta, low, HALF),
                    self.last_far.at[self.side, pl.ds(low, HALF), columns],
                )
                self.send(
                    self.block(stream, 0, delta),
                    self.last_near.at[way, self.side, :, columns],
                    stream[1],
                    delta,
                    self.last_near_sem,
                )

    def finish(self):
        self.wait(self.last_near_sem, 2 * SHARD_ROWS)
        for stream in two_orders(self.group):
            columns = pl.ds(*stream[2])
            add_into(
                self.block(stream, 0, 0),
                self.last_near.at[0, self.side, :, columns],
                self.last_near.at[1, self.side, :, columns],
            )


class Reduce:
    def __init__(self, place, buffers, swapped, group):
        self.place, self.sums, self.group = place, buffers[0], group
        self.sent, self.swap_sem = place.send_sem(), place.recv_sem()
        self.own = ReduceSide(place, buffers, 0, group, self.sent)
        self.other = ReduceSide(place, buffers, 1, group, self.sent)
        self.swapped = swapped.at[:, pl.ds(*group)]

    def both(self, name):
        for side in (self.other, self.own):
            getattr(side, name)()

    def finish(self):
        place, cut = self.place, pl.ds(*self.group)
        z_at, y_at, x_at = place.at["z"], place.at["y"], place.at["x"]
        self.other.finish()
        partial = self.sums.at[place.rows(z_at, y_at, 1 - x_at), cut]
        place.send(partial, self.swapped, place.neighbour("x", 1), self.sent, self.swap_sem)
        self.own.finish()

    def total(self):
        place, cut = self.place, pl.ds(*self.group)
        place.arrived(self.swapped, self.swap_sem)
        mine = place.rows(place.at["z"], place.at["y"], place.at["x"])
        return self.sums[mine, cut].astype(jnp.float32) + self.swapped[...].astype(jnp.float32)

    def drain(self):
        rows = (DP - 1) * SHARD_ROWS
        self.place.left(self.sums.at[pl.ds(0, rows), pl.ds(*self.group)], self.sent)


SEQ = 512
ROWS = 128
CHIP_ROWS = 256
SCALE = HEAD_SIZE ** (-0.5)
GAINS = 2 * MODEL_WIDTH + 2 * HEAD_SIZE


def rows_at(index, size):
    if isinstance(index, int):
        return pl.ds(index * size, size)
    return pl.ds(pl.multiple_of(index * size, size), size)


class Quad:
    def __init__(self, place):
        self.place = place
        self.tensor = place.tensor
        self.core, self.chip = place.tensor % 2, place.tensor // 2
        self.partner = {"tensor": self.chip * 2 + 1 - self.core}
        self.across = {"tensor": (1 - self.chip) * 2 + self.core}
        self.own_rows = rows_at(self.tensor, ROWS)
        self.near_rows = rows_at(self.chip, CHIP_ROWS)
        self.far_rows = rows_at(1 - self.chip, CHIP_ROWS)


class QuadGather:
    def __init__(self, quad, full):
        self.quad, self.full, self.place = quad, full, quad.place
        self.sent, self.side = self.place.send_sem(), self.place.recv_sem()
        self.over = [self.place.recv_sem() for part in range(2)]
        self.on = self.place.recv_sem()

    def half(self, block, part):
        return self.full.at[pl.ds(pl.multiple_of(block * ROWS + part * 64, 64), 64)]

    def start(self, *which):
        quad, place = self.quad, self.place
        for part in which or range(2):
            piece = self.half(quad.tensor, part)
            place.send(piece, piece, quad.across, self.sent, self.over[part])
            place.send(piece, piece, quad.partner, self.sent, self.side)

    def near(self):
        self.place.arrived(self.full.at[self.quad.own_rows], self.side)

    def forward(self, *which):
        quad, place = self.quad, self.place
        far = (1 - quad.chip) * 2 + quad.core
        for part in which or range(2):
            piece = self.half(far, part)
            place.arrived(piece, self.over[part])
            place.send(piece, piece, quad.partner, self.sent, self.on)

    def finish(self):
        self.place.arrived(self.full.at[self.quad.own_rows], self.on)

    def drain(self):
        self.place.left(self.full.at[pl.ds(0, 3 * ROWS)], self.sent)


class QuadReduce:
    def __init__(self, quad, parts, chip_in, link_in):
        self.quad, self.parts, self.chip_in, self.link_in = quad, parts, chip_in, link_in
        self.place = quad.place
        far, near = 2 * (1 - quad.chip), 2 * quad.chip
        self.far_own, self.far_other = far + quad.core, far + 1 - quad.core
        self.near_other = near + 1 - quad.core
        self.sent, self.near_sem = self.place.send_sem(), self.place.recv_sem()
        self.far_sem = [self.place.recv_sem() for part in range(2)]
        self.link_sem = [self.place.recv_sem() for part in range(2)]
        self.near_here = False

    def piece(self, block, part):
        return self.parts.at[pl.ds(pl.multiple_of(block * ROWS + part * 64, 64), 64)]

    def far_ready(self):
        for part in range(2):
            self.place.send(
                self.piece(self.far_other, part),
                self.chip_in.at[0, pl.ds(64 * part, 64)],
                self.quad.partner,
                self.sent,
                self.far_sem[part],
            )

    def near_ready(self):
        self.place.send(
            self.parts.at[rows_at(self.near_other, ROWS)],
            self.chip_in.at[1],
            self.quad.partner,
            self.sent,
            self.near_sem,
        )

    def link(self):
        for part in range(2):
            far_in = self.chip_in.at[0, pl.ds(64 * part, 64)]
            self.place.arrived(far_in, self.far_sem[part])
            piece = self.piece(self.far_own, part)
            add_into(piece, far_in)
            self.place.send(
                piece,
                self.link_in.at[pl.ds(64 * part, 64)],
                self.quad.across,
                self.sent,
                self.link_sem[part],
            )

    def total(self, part):
        if not self.near_here:
            self.place.arrived(self.chip_in.at[1], self.near_sem)
            self.near_here = True
        rows = pl.ds(64 * part, 64)
        self.place.arrived(self.link_in.at[rows], self.link_sem[part])
        total = self.piece(self.quad.tensor, part)[...].astype(jnp.float32)
        total = total + self.chip_in[1, rows].astype(jnp.float32)
        return total + self.link_in[rows].astype(jnp.float32)

    def drain(self):
        self.place.left(self.parts.at[pl.ds(0, 3 * ROWS)], self.sent)


def turn_rows(source, target):
    for k in range(source.shape[1] // 128):
        target[128 * k : 128 * (k + 1), :] = source[:, 128 * k : 128 * (k + 1)].T


def rope(values, cos, sin):
    return values * cos + pltpu.roll(values, HEAD_SIZE // 2, 1) * sin


def rope_back(values, cos, sin):
    return values * cos + pltpu.roll(values * sin, HEAD_SIZE // 2, 1)


def orthogonalize(inbox, current, work, low_square, mixer, side, leave):
    f32, bf16 = jnp.float32, jnp.bfloat16
    tiles = side // 256

    total = jnp.float32(0.0)
    for k in range(8):
        piece = inbox[4 * k : 4 * (k + 1), :, :side].reshape(4 * SHARD_ROWS, side).astype(f32)
        current[:side, 128 * k : 128 * (k + 1)] = piece.T
        total = total + jnp.sum(piece * piece)
    scale = 1.0 / (jnp.sqrt(total) + 1e-07)

    def narrow(slot):
        return work.at[pl.ds(0, side), pl.ds(slot * MODEL_WIDTH, MODEL_WIDTH)]

    energy = jnp.zeros((1, MODEL_WIDTH), f32)
    for k in range(tiles):
        cut = slice(256 * k, 256 * (k + 1))
        piece = current[cut, :] * scale
        current[cut, :] = piece
        narrow(0)[cut, :] = piece.astype(bf16)
        energy = energy + jnp.sum(piece * piece, axis=0, keepdims=True)

    def newton(step, energy):
        now, later = narrow(step), narrow(1 - step)
        shift = jnp.sum(energy, axis=1, keepdims=True) * (1.0 / side)
        linear = newton_two + 2.0 * newton_three * shift
        constant = newton_one + newton_two * shift + newton_three * shift * shift
        row = lax.broadcasted_iota(jnp.int32, (256, 256), 0)
        column = lax.broadcasted_iota(jnp.int32, (256, 256), 1)

        def put(target, k, part):
            cut = slice(256 * k, 256 * (k + 1))
            target[cut, 256 * k : side] = part
            for other in range(k + 1, tiles):
                block = part[:, 256 * (other - k) : 256 * (other - k + 1)]
                target[256 * other : 256 * (other + 1), cut] = block.T

        for k in range(tiles):
            part = lax.dot_general(
                now[256 * k : 256 * (k + 1), :],
                now[256 * k : side, :],
                contract_cols,
                preferred_element_type=f32,
            )
            first = jnp.where(row == column, part[:, :256] - shift, part[:, :256])
            if k < tiles - 1:
                part = jnp.concatenate([first, part[:, 256:]], axis=1)
            else:
                part = first
            put(low_square, k, part.astype(bf16))
        for k in range(tiles):
            cut = slice(256 * k, 256 * (k + 1))
            part = jnp.dot(
                low_square[cut, :side],
                low_square[:side, 256 * k : side],
                preferred_element_type=f32,
            )
            part = linear * low_square[cut, 256 * k : side].astype(f32) + newton_three * part
            put(mixer, k, part.astype(bf16))
        energy = jnp.zeros((1, MODEL_WIDTH), f32)
        for k in range(tiles):
            cut = slice(256 * k, 256 * (k + 1))
            part = jnp.dot(mixer[cut, :side], now[...], preferred_element_type=f32)
            part = part + constant * current[cut, :]
            current[cut, :] = part
            later[cut, :] = part.astype(bf16)
            energy = energy + jnp.sum(part * part, axis=0, keepdims=True)
        return energy

    def pair(step, energy):
        return newton(1, newton(0, energy))

    newton(0, lax.fori_loop(0, NS_ITERS // 2, pair, energy))
    for k in range(8):
        piece = current[:side, 128 * k : 128 * (k + 1)].T
        inbox[4 * k : 4 * (k + 1), :, :side] = piece.astype(bf16).reshape(4, SHARD_ROWS, side)
        leave(k)


def layer_kernel(*refs):
    (
        x_in,
        positions_ref,
        cotangent_in,
        query_in,
        key_in,
        value_in,
        out_in,
        gate_in,
        up_in,
        down_in,
        query_moment_in,
        key_moment_in,
        value_moment_in,
        out_moment_in,
        gate_moment_in,
        up_moment_in,
        down_moment_in,
        gains_ref,
        gain_moment_ref,
        out_ref,
        grad_ref,
        moments_ref,
        weights_ref,
        gain_moment_out,
        gains_out,
        x_ref,
        cotangent_ref,
        shard,
        moments,
        weights,
        cos_ref,
        sin_ref,
        full,
        sums,
        far,
        near,
        last_far,
        last_near,
        swapped,
        normed,
        normed_two,
        cotangents,
        branch_grads,
        turned,
        query_raw,
        key_raw,
        query_rot,
        key_rot,
        value_low,
        key_turned,
        value_turned,
        probs,
        attention,
        attention_grad,
        hidden,
        ffn_grads,
        head_grads,
        key_sum,
        value_sum,
        hidden_one,
        input_grad,
        parts,
        chip_in,
        link_in,
        posted,
        inbox,
        current,
        settled,
        gain_parts,
        gain_tensor,
        gain_dp,
        send_sems,
        recv_sems,
        post_send,
        post_recv,
        back_send,
        back_recv,
        gain_sems,
        local_sems,
    ) = refs
    bf16, f32 = jnp.bfloat16, jnp.float32
    place = Place(send_sems, recv_sems)
    quad = Quad(place)
    dp, tensor = place.dp, place.tensor
    x_at = place.at["x"]

    shard_ins = (query_in, key_in, value_in, out_in, gate_in, up_in, down_in)
    moment_ins = (
        query_moment_in,
        key_moment_in,
        value_moment_in,
        out_moment_in,
        gate_moment_in,
        up_moment_in,
        down_moment_in,
    )
    shard_load, x_load, cotangent_load, moment_load = (local_sems.at[k] for k in range(4))
    out_store, grad_store, moment_store, weight_store = (local_sems.at[k] for k in range(4, 8))
    def load_pieces(sources, target, sem):
        for slot, source in enumerate(sources):
            for start, width, at in pieces[slot]:
                pltpu.make_async_copy(
                    source.at[:, pl.ds(at, width)], target.at[:, pl.ds(start, width)], sem
                ).start()

    load_pieces(shard_ins, shard, shard_load)
    pltpu.make_async_copy(x_in, x_ref, x_load).start()
    pltpu.make_async_copy(cotangent_in, cotangent_ref, cotangent_load).start()
    load_pieces(moment_ins, moments, moment_load)

    def loaded(target, sem):
        pltpu.make_async_copy(target, target, sem).wait()

    barrier = pltpu.get_barrier_semaphore()

    def greet(k, carry):
        pl.semaphore_signal(
            barrier, inc=1, device_id={"dp": lax.rem(dp + k, DP)}, device_id_type=MESH
        )
        return carry

    lax.fori_loop(1, DP, greet, 0)
    for k in range(1, TENSOR):
        pl.semaphore_signal(
            barrier, inc=1, device_id={"tensor": lax.rem(tensor + k, TENSOR)}, device_id_type=MESH
        )
    loaded(shard, shard_load)
    mine = place.rows(place.at["z"], place.at["y"], x_at)
    full[mine, :] = shard[...]
    pl.semaphore_wait(barrier, DP - 1 + TENSOR - 1)

    gather_low, gather_high, gather_out, gather_gate, gather_down = gathers = [
        Gather(place, full, group) for group in column_groups
    ]
    gather_low.swap()
    gather_low.own.begin()
    gather_high.swap()
    gather_high.own.begin()
    gather_out.swap()
    gather_out.own.begin()

    all_gains = gains_ref[...].reshape(1, GAINS)
    gain_attn = all_gains[:, :MODEL_WIDTH]
    gain_ffn = all_gains[:, MODEL_WIDTH : 2 * MODEL_WIDTH]
    gain_query = all_gains[:, 2 * MODEL_WIDTH : 2 * MODEL_WIDTH + HEAD_SIZE]
    gain_key = all_gains[:, 2 * MODEL_WIDTH + HEAD_SIZE :]
    loaded(x_ref, x_load)
    x = x_ref[...].astype(f32)
    first_scale = rms_scale(x)
    normed[quad.own_rows, :] = (x * first_scale * gain_attn).astype(bf16)
    gather_low.begin_other()
    gather_normed = QuadGather(quad, normed)
    gather_normed.start()
    gather_gate.swap()
    gather_low.own.forward_first()
    gather_high.begin_other()
    gather_low.other.forward_first()
    gather_low.both("finish_first")
    gather_high.both("forward_first")
    gather_low.both("forward_second")
    gather_normed.forward()
    gather_high.both("finish_first")
    gather_out.begin_other()
    gather_high.both("forward_second")
    gather_out.both("forward_first")
    gather_gate.own.begin()
    gather_gate.begin_other()
    gather_down.swap()

    angle = jnp.broadcast_to(
        positions_ref[...].reshape(1, SEQ).astype(f32), (HEAD_SIZE, SEQ)
    ).T
    lane = lax.broadcasted_iota(jnp.int32, (1, HEAD_SIZE), 1)
    low_half = lane < HEAD_SIZE // 2
    step = jnp.where(low_half, lane, lane - HEAD_SIZE // 2).astype(f32)
    angle = angle * jnp.exp(step * (-2.0 * math.log(rope_base) / HEAD_SIZE))
    cos_ref[...] = jnp.cos(angle)
    sin = jnp.sin(angle)
    sin_ref[...] = jnp.where(low_half, -sin, sin)

    loaded(cotangent_ref, cotangent_load)
    cotangents[quad.own_rows, :] = cotangent_ref[...]
    gather_cotangent = QuadGather(quad, cotangents)
    gather_cotangent.start()
    gather_normed.near()
    gather_normed.finish()
    gather_low.both("finish_second")
    gather_out.both("finish_first")

    def project(half):
        heads = jnp.dot(
            normed[...], full[:, 512 * half : 512 * (half + 1)], preferred_element_type=f32
        )
        query_raw[:, 256 * half : 256 * (half + 1)] = heads[:, :256]
        for head in range(2):
            raw = heads[:, HEAD_SIZE * head : HEAD_SIZE * (head + 1)]
            rotated = rope(raw * rms_scale(raw) * gain_query, cos_ref[...], sin_ref[...])
            query_rot[:, rows_at(2 * half + head, HEAD_SIZE)] = rotated.astype(bf16)
        lanes = rows_at(half, HEAD_SIZE)
        raw = heads[:, 256:384]
        key_raw[:, lanes] = raw
        rotated = rope(raw * rms_scale(raw) * gain_key, cos_ref[...], sin_ref[...]).astype(bf16)
        key_rot[:, lanes] = rotated
        key_turned[lanes, :] = rotated.T
        value = heads[:, 384:].astype(bf16)
        value_low[:, lanes] = value
        value_turned[lanes, :] = value.T

    project(0)
    gather_gate.both("forward_first")
    gather_high.both("finish_second")
    project(1)
    gather_out.both("forward_second")
    gather_down.own.begin()
    gather_down.begin_other()
    gather_gate.both("finish_first")

    def attend(head):
        lanes, shared = rows_at(head, HEAD_SIZE), rows_at(head // 2, HEAD_SIZE)
        for block in range(2):
            keys, begin = 256 * (block + 1), 256 * block
            scores = lax.dot_general(
                key_rot[pl.ds(0, keys), shared],
                query_rot[pl.ds(begin, 256), lanes],
                contract_cols,
                preferred_element_type=f32,
            )
            row = lax.broadcasted_iota(jnp.int32, (keys, 256), 0)
            column = lax.broadcasted_iota(jnp.int32, (keys, 256), 1) + begin
            scores = jnp.where(row <= column, scores * SCALE, -1e30)
            shifted = jnp.exp(scores - jnp.max(scores, axis=0, keepdims=True))
            total = jnp.sum(shifted, axis=0, keepdims=True)
            low = (shifted * (1.0 / total)).astype(bf16)
            probs[head, pl.ds(0, keys), pl.ds(begin, 256)] = low
            mixed = jnp.dot(
                value_turned[shared, pl.ds(0, keys)], low, preferred_element_type=f32
            )
            attention[pl.ds(begin, 256), lanes] = mixed.T.astype(bf16)

    attend(0)
    gather_down.both("forward_first")
    attend(1)
    gather_gate.both("forward_second")
    attend(2)
    gather_out.both("finish_second")
    gather_down.both("finish_first")
    gather_cotangent.forward()
    attend(3)

    def project_back(source, start, width, target):
        def run(rows):
            for k in range(4):
                part = lax.dot_general(
                    source[rows, :],
                    full[256 * k : 256 * (k + 1), start : start + width],
                    contract_cols,
                    preferred_element_type=f32,
                )
                target[rows, 256 * k : 256 * (k + 1)] = part.astype(bf16)

        return run

    def reducer(k):
        return QuadReduce(quad, parts.at[k], chip_in.at[k], link_in.at[k])

    reduce_attn = reducer(0)
    out_rows = project_back(attention, 1024, 512, parts.at[0])
    out_rows(quad.far_rows)
    reduce_attn.far_ready()
    out_rows(quad.near_rows)
    reduce_attn.near_ready()
    reduce_attn.link()
    gather_down.both("forward_second")
    turn_rows(normed, turned.at[1])
    gather_cotangent.near()
    gather_cotangent.finish()
    turn_rows(cotangents, turned.at[0])
    gather_two = QuadGather(quad, normed_two)
    for part in range(2):
        rows = pl.ds(64 * part, 64)
        first_hidden = x_ref[rows, :].astype(f32) + reduce_attn.total(part)
        hidden_one[rows, :] = first_hidden
        normed_two[pl.ds(pl.multiple_of(tensor * ROWS + 64 * part, 64), 64), :] = (
            first_hidden * rms_scale(first_hidden) * gain_ffn
        ).astype(bf16)
        gather_two.start(part)
    gather_gate.both("finish_second")
    gather_two.forward()
    gather_down.both("finish_second")

    def feed(rows):
        for k in range(3):
            low = normed_two[rows, :]
            at = 256 * k
            gate = jnp.dot(low, full[:, 1536 + at : 1792 + at], preferred_element_type=f32)
            up = jnp.dot(low, full[:, 2304 + at : 2560 + at], preferred_element_type=f32)
            grad = jnp.dot(
                cotangents[rows, :], full[:, 3072 + at : 3328 + at], preferred_element_type=f32
            )
            sigmoid = 1.0 / (1.0 + jnp.exp(-gate))
            activated = gate * sigmoid
            hidden[rows, at : at + 256] = (activated * up).astype(bf16)
            ffn_grads[rows, at : at + 256] = (
                grad * up * (sigmoid * (1.0 + gate * (1.0 - sigmoid)))
            ).astype(bf16)
            ffn_grads[rows, 768 + at : 1024 + at] = (grad * activated).astype(bf16)

    reduce_two = reducer(1)
    two_rows = project_back(ffn_grads, 1536, 1536, parts.at[1])
    gather_two.near()
    feed(quad.near_rows)
    two_rows(quad.near_rows)
    reduce_two.near_ready()
    gather_two.finish()
    feed(quad.far_rows)
    two_rows(quad.far_rows)
    reduce_two.far_ready()

    def weight_grads(left, right, start, first, last):
        for k in range(first, last):
            part = jnp.dot(
                left[...], right[:, 256 * k : 256 * (k + 1)], preferred_element_type=f32
            )
            sums[:, start + 256 * k : start + 256 * (k + 1)] = part.astype(bf16)

    weight_grads(turned.at[0], hidden, 3072, 0, 2)
    reduce_two.link()
    weight_grads(turned.at[0], hidden, 3072, 2, 3)
    buffers = (sums, far, near, last_far, last_near)
    sum_low, sum_high, sum_out, sum_gate, sum_down = all_sums = [
        Reduce(place, buffers, swapped, group) for group in column_groups
    ]
    sum_down.both("begin")
    turn_rows(normed_two, turned.at[0])
    weight_grads(turned.at[0], ffn_grads, 1536, 0, 4)
    sum_down.both("pass_first")

    gather_branch = QuadGather(quad, branch_grads)
    ffn_gain_grad = jnp.zeros((1, MODEL_WIDTH), f32)
    for part in range(2):
        rows = pl.ds(64 * part, 64)
        normed_two_grad = reduce_two.total(part)
        first_hidden = hidden_one[rows, :]
        second_scale = rms_scale(first_hidden)
        second_hat = first_hidden * second_scale
        ffn_gain_grad = ffn_gain_grad + jnp.sum(
            normed_two_grad * second_hat, axis=0, keepdims=True
        )
        hidden_one_grad = cotangent_ref[rows, :].astype(f32) + norm_backward(
            normed_two_grad * gain_ffn, second_hat, second_scale
        )
        input_grad[rows, :] = hidden_one_grad
        branch_grads[pl.ds(pl.multiple_of(tensor * ROWS + 64 * part, 64), 64), :] = (
            hidden_one_grad.astype(bf16)
        )
        gather_branch.start(part)
    gain_parts[:, MODEL_WIDTH : 2 * MODEL_WIDTH] = ffn_gain_grad
    weight_grads(turned.at[0], ffn_grads, 1536, 4, 6)
    sum_gate.both("begin")

    reduce_ffn = reducer(2)
    down_rows = project_back(hidden, 3072, 768, parts.at[2])
    down_rows(quad.far_rows)
    reduce_ffn.far_ready()

    def attend_grad(rows):
        part = jnp.dot(branch_grads[rows, :], full[:, 1024:1536], preferred_element_type=f32)
        attention_grad[rows, :] = part.astype(bf16)

    gather_branch.near()
    gather_branch.forward(0)
    attend_grad(quad.near_rows)
    gather_branch.forward(1)
    sum_down.both("begin_second")
    down_rows(quad.near_rows)
    reduce_ffn.near_ready()
    reduce_ffn.link()
    gather_branch.finish()
    attend_grad(quad.far_rows)
    sum_gate.both("pass_first")
    turn_rows(branch_grads, turned.at[0])
    weight_grads(turned.at[0], attention, 1024, 0, 2)
    sum_out.both("begin")

    def head_norm_back(rotated_grad, raw, gain, rows):
        scale = rms_scale(raw)
        hat = raw * scale
        norm_grad = rope_back(rotated_grad, cos_ref[rows, :], sin_ref[rows, :])
        gain_grad = jnp.sum(norm_grad * hat, axis=0, keepdims=True)
        return norm_backward(norm_grad * gain, hat, scale).astype(bf16), gain_grad

    def attend_back(head, gain_sum):
        lanes, shared = rows_at(head, HEAD_SIZE), rows_at(head // 2, HEAD_SIZE)
        for block in (1, 0):
            keys, begin = 256 * (block + 1), 256 * block
            key_cut, query_cut = pl.ds(0, keys), pl.ds(begin, 256)
            mixed_grad = attention_grad[query_cut, lanes]
            low = probs[head, key_cut, query_cut]
            wide = low.astype(f32)
            probs_grad = lax.dot_general(
                value_low[key_cut, shared],
                mixed_grad,
                contract_cols,
                preferred_element_type=f32,
            )
            inner_sum = jnp.sum(wide * probs_grad, axis=0, keepdims=True)
            score_grad = (wide * (probs_grad - inner_sum)).astype(bf16)
            value_part = jnp.dot(low, mixed_grad, preferred_element_type=f32)
            key_part = jnp.dot(
                score_grad, query_rot[query_cut, lanes], preferred_element_type=f32
            )
            if head % 2 == 0 and block == 1:
                value_sum[:, shared] = value_part
                key_sum[:, shared] = key_part
            else:
                value_sum[key_cut, shared] += value_part
                key_sum[key_cut, shared] += key_part
            query_part = jnp.dot(
                key_turned[shared, key_cut], score_grad, preferred_element_type=f32
            )
            grad, gain_part = head_norm_back(
                query_part.T * SCALE, query_raw[query_cut, lanes], gain_query, query_cut
            )
            head_grads[query_cut, rows_at(head + 2 * (head // 2), HEAD_SIZE)] = grad
            gain_sum = gain_sum + gain_part
        return gain_sum

    def shared_back(head, gain_sum):
        shared = rows_at(head, HEAD_SIZE)
        grad, gain_part = head_norm_back(
            key_sum[:, shared] * SCALE, key_raw[:, shared], gain_key, pl.ds(0, SEQ)
        )
        head_grads[:, rows_at(4 * head + 2, HEAD_SIZE)] = grad
        head_grads[:, rows_at(4 * head + 3, HEAD_SIZE)] = value_sum[:, shared].astype(bf16)
        return gain_sum + gain_part

    none = jnp.zeros((1, HEAD_SIZE), f32)
    query_gain_sum = attend_back(0, none)
    sum_down.both("pass_second")
    query_gain_sum = attend_back(1, query_gain_sum)
    key_gain_sum = shared_back(0, none)
    weight_grads(turned.at[1], head_grads, 0, 0, 2)
    sum_low.both("begin")
    sum_gate.other.begin_second()
    query_gain_sum = attend_back(2, query_gain_sum)
    sum_out.both("pass_first")
    sum_gate.own.begin_second()
    sum_down.finish()
    query_gain_sum = attend_back(3, query_gain_sum)
    key_gain_sum = shared_back(1, key_gain_sum)
    gain_parts[:, 2 * MODEL_WIDTH : 2 * MODEL_WIDTH + HEAD_SIZE] = query_gain_sum
    gain_parts[:, 2 * MODEL_WIDTH + HEAD_SIZE :] = key_gain_sum
    sum_gate.both("pass_second")
    weight_grads(turned.at[1], head_grads, 0, 2, 4)
    sum_high.both("begin")
    sum_low.both("pass_first")
    sum_out.both("begin_second")

    reduce_one = reducer(3)
    one_rows = project_back(head_grads, 0, 1024, parts.at[3])
    one_rows(quad.far_rows)
    reduce_one.far_ready()
    sum_gate.finish()
    sum_low.both("begin_second")
    one_rows(quad.near_rows)
    reduce_one.near_ready()
    sum_high.both("pass_first")
    sum_out.both("pass_second")
    reduce_one.link()
    sum_low.both("pass_second")
    sum_out.finish()

    loaded(moments, moment_load)
    core = tensor % 2
    owner = [even + core * (odd - even) for even, odd in owners]

    def update(group):
        start, width = column_groups[group]
        cut = pl.ds(start, width)
        fresh = moment_decay * moments[:, cut] + all_sums[group].total()
        moments[:, cut] = fresh
        posted[:, cut] = fresh.astype(bf16)
        pltpu.make_async_copy(moments.at[:, cut], moments_ref.at[:, cut], moment_store).start()
        for slot in range(7):
            for piece_start, piece_width, at in pieces[slot]:
                if start <= piece_start < start + width:
                    post(slot, pl.ds(piece_start, piece_width), pl.ds(at, piece_width))

    def post(slot, cut, at):
        @pl.when(dp != owner[slot])
        def _():
            place.send(
                posted.at[:, cut],
                inbox.at[dp, :, at],
                {"dp": owner[slot]},
                post_send.at[slot],
                post_recv.at[0],
            )

        @pl.when(dp == owner[slot])
        def _():
            inbox[dp, :, at] = posted[:, cut]

    update(4)
    update(3)
    sum_high.both("begin_second")

    for part in range(2):
        rows = pl.ds(64 * part, 64)
        hidden_one[rows, :] = hidden_one[rows, :] + reduce_ffn.total(part)
    pltpu.make_async_copy(hidden_one, out_ref, out_store).start()
    sum_low.finish()
    sum_high.both("pass_second")
    update(2)
    attn_gain_grad = jnp.zeros((1, MODEL_WIDTH), f32)
    for part in range(2):
        rows = pl.ds(64 * part, 64)
        normed_grad = reduce_one.total(part)
        x = x_ref[rows, :].astype(f32)
        first_scale = rms_scale(x)
        first_hat = x * first_scale
        attn_gain_grad = attn_gain_grad + jnp.sum(normed_grad * first_hat, axis=0, keepdims=True)
        input_grad[rows, :] = input_grad[rows, :] + norm_backward(
            normed_grad * gain_attn, first_hat, first_scale
        )
    gain_parts[:, :MODEL_WIDTH] = attn_gain_grad
    pltpu.make_async_copy(input_grad, grad_ref, grad_store).start()
    sum_high.finish()
    update(0)

    gain_tensor[tensor] = gain_parts[...]
    for k in range(1, TENSOR):
        place.send(
            gain_parts,
            gain_tensor.at[tensor],
            {"tensor": lax.rem(tensor + k, TENSOR)},
            gain_sems.at[0],
            gain_sems.at[1],
        )
    update(1)

    for group in gathers + all_sums:
        group.drain()
    for exchange in (gather_normed, gather_cotangent, gather_two, gather_branch):
        exchange.drain()
    for exchange in (reduce_attn, reduce_two, reduce_ffn, reduce_one):
        exchange.drain()

    place.arrived(gain_tensor.at[pl.ds(0, TENSOR - 1)], gain_sems.at[1])
    gain_dp[dp] = gain_tensor[0] + gain_tensor[1] + gain_tensor[2] + gain_tensor[3]

    def gain_start(k, carry):
        place.send(
            gain_dp.at[dp],
            gain_dp.at[dp],
            {"dp": lax.rem(dp + k, DP)},
            gain_sems.at[2],
            gain_sems.at[3],
        )
        return carry

    lax.fori_loop(1, DP, gain_start, 0)

    for slot in (4, 5, 6, 3, 0, 1, 2):

        @pl.when(dp == owner[slot])
        def _():
            place.arrived(inbox.at[pl.ds(0, DP - 1), :, pl.ds(0, widths[slot])], post_recv.at[0])

    work = full.at[:, pl.ds(0, 2 * MODEL_WIDTH)]
    low_square = full.at[:WIDEST, pl.ds(2048, WIDEST)]
    mixer = full.at[:WIDEST, pl.ds(2816, WIDEST)]
    def run_class(slots):
        side = widths[slots[0]]
        here = dp == owner[slots[0]]
        for slot in slots[1:]:
            here = here | (dp == owner[slot])

        def leave(k):
            for slot in slots:

                @pl.when(dp == owner[slot])
                def _():
                    def send_back(j, carry):
                        target = 4 * k + j
                        for start, width, at in pieces[slot]:
                            cut, at = pl.ds(start, width), pl.ds(at, width)

                            @pl.when(target != dp)
                            def _():
                                place.send(
                                    inbox.at[target, :, at],
                                    settled.at[:, cut],
                                    {"dp": target},
                                    back_send.at[0],
                                    back_recv.at[slot],
                                )

                            @pl.when(target == dp)
                            def _():
                                settled[:, cut] = inbox[target, :, at]

                        return carry

                    lax.fori_loop(0, 4, send_back, 0)

        @pl.when(here)
        def _():
            orthogonalize(inbox, current, work, low_square, mixer, side, leave)

    for slots in classes:
        run_class(slots)

    place.arrived(gain_dp.at[pl.ds(0, DP - 1)], gain_sems.at[3])

    def gain_add(k, carry):
        return carry + gain_dp[k]

    gain_total = lax.fori_loop(1, DP, gain_add, gain_dp[0]).reshape(GAINS)
    fresh_gain = gain_decay * gain_moment_ref[...] + gain_total
    gain_moment_out[...] = fresh_gain
    gains_out[...] = gains_ref[...] - gain_rate / math.sqrt(SEQ * DP) * fresh_gain

    for slot in (1, 2, 0, 3, 4, 5, 6):

        @pl.when(dp != owner[slot])
        def _():
            place.arrived(settled.at[:, pl.ds(0, widths[slot])], back_recv.at[slot])

        for start, width, at in pieces[slot]:
            cut = pl.ds(start, width)
            weights[:, cut] = shard[:, cut].astype(f32) - rates[slot] * settled[:, cut].astype(f32)
            pltpu.make_async_copy(weights.at[:, cut], weights_ref.at[:, cut], weight_store).start()

    place.left(gain_tensor.at[pl.ds(0, TENSOR - 1)], gain_sems.at[0])
    place.left(gain_dp.at[pl.ds(0, DP - 1)], gain_sems.at[2])
    for slot in range(7):

        @pl.when(dp != owner[slot])
        def _():
            place.left(posted.at[:, pl.ds(0, widths[slot])], post_send.at[slot])

        @pl.when(dp == owner[slot])
        def _():
            place.left(inbox.at[pl.ds(0, DP - 1), :, pl.ds(0, widths[slot])], back_send.at[0])

    loaded(hidden_one, out_store)
    loaded(input_grad, grad_store)
    loaded(moments, moment_store)
    loaded(weights, weight_store)


def run_layer(args):
    bf16, f32 = jnp.bfloat16, jnp.float32
    shard_shape = (SHARD_ROWS, COLUMNS)
    dma = pltpu.SemaphoreType.DMA
    in_specs = [ANY] * 19
    in_specs[1] = in_specs[17] = in_specs[18] = VMEM
    return pl.pallas_call(
        layer_kernel,
        out_shape=(
            jax.ShapeDtypeStruct((ROWS, MODEL_WIDTH), f32),
            jax.ShapeDtypeStruct((ROWS, MODEL_WIDTH), f32),
            jax.ShapeDtypeStruct(shard_shape, f32),
            jax.ShapeDtypeStruct(shard_shape, f32),
            jax.ShapeDtypeStruct((GAINS,), f32),
            jax.ShapeDtypeStruct((GAINS,), f32),
        ),
        in_specs=in_specs,
        out_specs=(ANY, ANY, ANY, ANY, VMEM, VMEM),
        scratch_shapes=[
            pltpu.VMEM((ROWS, MODEL_WIDTH), bf16),
            pltpu.VMEM((ROWS, MODEL_WIDTH), bf16),
            pltpu.VMEM(shard_shape, bf16),
            pltpu.VMEM(shard_shape, f32),
            pltpu.VMEM(shard_shape, f32),
            pltpu.VMEM((SEQ, HEAD_SIZE), f32),
            pltpu.VMEM((SEQ, HEAD_SIZE), f32),
            pltpu.VMEM((MODEL_WIDTH, COLUMNS), bf16),
            pltpu.VMEM((MODEL_WIDTH, COLUMNS), bf16),
            pltpu.VMEM((2, 4, SHARD_ROWS, COLUMNS), bf16),
            pltpu.VMEM((2, 2, 4, SHARD_ROWS, COLUMNS), bf16),
            pltpu.VMEM((2, SHARD_ROWS, COLUMNS), bf16),
            pltpu.VMEM((2, 2, SHARD_ROWS, COLUMNS), bf16),
            pltpu.VMEM(shard_shape, bf16),
            pltpu.VMEM((SEQ, MODEL_WIDTH), bf16),
            pltpu.VMEM((SEQ, MODEL_WIDTH), bf16),
            pltpu.VMEM((SEQ, MODEL_WIDTH), bf16),
            pltpu.VMEM((SEQ, MODEL_WIDTH), bf16),
            pltpu.VMEM((2, MODEL_WIDTH, SEQ), bf16),
            pltpu.VMEM((SEQ, 512), f32),
            pltpu.VMEM((SEQ, 256), f32),
            pltpu.VMEM((SEQ, 512), bf16),
            pltpu.VMEM((SEQ, 256), bf16),
            pltpu.VMEM((SEQ, 256), bf16),
            pltpu.VMEM((256, SEQ), bf16),
            pltpu.VMEM((256, SEQ), bf16),
            pltpu.VMEM((4, SEQ, SEQ), bf16),
            pltpu.VMEM((SEQ, 512), bf16),
            pltpu.VMEM((SEQ, 512), bf16),
            pltpu.VMEM((SEQ, 768), bf16),
            pltpu.VMEM((SEQ, 1536), bf16),
            pltpu.VMEM((SEQ, 1024), bf16),
            pltpu.VMEM((SEQ, 256), f32),
            pltpu.VMEM((SEQ, 256), f32),
            pltpu.VMEM((ROWS, MODEL_WIDTH), f32),
            pltpu.VMEM((ROWS, MODEL_WIDTH), f32),
            pltpu.VMEM((4, SEQ, MODEL_WIDTH), bf16),
            pltpu.VMEM((4, 2, ROWS, MODEL_WIDTH), bf16),
            pltpu.VMEM((4, ROWS, MODEL_WIDTH), bf16),
            pltpu.VMEM(shard_shape, bf16),
            pltpu.VMEM((DP, SHARD_ROWS, WIDEST), bf16),
            pltpu.VMEM((WIDEST, MODEL_WIDTH), f32),
            pltpu.VMEM(shard_shape, bf16),
            pltpu.VMEM((1, GAINS), f32),
            pltpu.VMEM((TENSOR, 1, GAINS), f32),
            pltpu.VMEM((DP, 1, GAINS), f32),
            dma((18,)),
            dma((216,)),
            dma((7,)),
            dma((1,)),
            dma((1,)),
            dma((7,)),
            dma((4,)),
            dma((8,)),
        ],
        compiler_params=pltpu.CompilerParams(
            collective_id=0, has_side_effects=True, vmem_limit_bytes=62 << 20
        ),
        name="layer",
    )(*args)


def unpack_kernel(*refs):
    sources, targets = refs[:6], refs[6:]
    out, grad, moments, weights, gain_moment, gains = sources
    targets[0][...] = out[...]
    targets[1][...] = grad[...]
    for slot in range(7):
        for start, width, at in pieces[slot]:
            cut, at = pl.ds(start, width), pl.ds(at, width)
            targets[2 + slot][:, at] = moments[:, cut]
            targets[9 + slot][:, at] = weights[:, cut]
    targets[16][...] = gain_moment[...]
    targets[17][...] = gains[...]


def unpack(results):
    f32 = jnp.float32
    pieces = [jax.ShapeDtypeStruct((SHARD_ROWS, width), f32) for width in widths]
    shapes = [jax.ShapeDtypeStruct((ROWS, MODEL_WIDTH), f32)] * 2
    shapes += pieces + pieces + [jax.ShapeDtypeStruct((GAINS,), f32)] * 2
    return pl.pallas_call(
        unpack_kernel,
        out_shape=tuple(shapes),
        in_specs=[VMEM] * 6,
        out_specs=(VMEM,) * 18,
        name="unpack",
    )(*results)


def body(*args):
    args = list(args)
    for index in (6, 9, 13, 16):
        args[index] = args[index].T
    results = list(unpack(run_layer(args)))
    for index in (5, 8, 12, 15):
        results[index] = results[index].T
    return tuple(results)


def solution(mesh):
    placed = (
        P(("dp", "tensor"), None),
        P("dp"),
        P(("dp", "tensor"), None),
        P("dp", "tensor"),
        P("dp", "tensor"),
        P("dp", "tensor"),
        P("tensor", "dp"),
        P("dp", "tensor"),
        P("dp", "tensor"),
        P("tensor", "dp"),
        P("dp", "tensor"),
        P("dp", "tensor"),
        P("dp", "tensor"),
        P("tensor", "dp"),
        P("dp", "tensor"),
        P("dp", "tensor"),
        P("tensor", "dp"),
        P(),
        P(),
    )
    return jax.shard_map(
        body,
        mesh=mesh,
        in_specs=placed,
        out_specs=(
            P(("dp", "tensor"), None),
            P(("dp", "tensor"), None),
            P("dp", "tensor"),
            P("dp", "tensor"),
            P("dp", "tensor"),
            P("tensor", "dp"),
            P("dp", "tensor"),
            P("dp", "tensor"),
            P("tensor", "dp"),
            P("dp", "tensor"),
            P("dp", "tensor"),
            P("dp", "tensor"),
            P("tensor", "dp"),
            P("dp", "tensor"),
            P("dp", "tensor"),
            P("tensor", "dp"),
            P(),
            P(),
        ),
        check_vma=False,
    )
```
